32 devices in a mesh: dp: 4 (over y, core), blk: 4 (over z), head: 2 (over x).
Axes of the slice: x: 2, y: 2, z: 4, core: 2. Of those that a mesh axis runs over, the one named last changes fastest.
Arguments:
- inputs: bfloat16 [2048, 4, 2048], P('blk', 'dp', 'head'), may hold values from -32 to 32
- cotangent: bfloat16 [2048, 4, 2048], P('blk', 'dp', 'head'), may hold values from -6 to 6
- lengths: int32 [4, 8], P('dp'), may hold values from 0 to 2048, as said below
- attn_gain: bfloat16 [2048], replicated, may hold values from 0.5 to 1.5
- w_query: bfloat16 [2048, 2048], P(None, 'head'), may hold values from -0.125 to 0.125
- w_key: bfloat16 [2048, 256], P(None, 'head'), may hold values from -0.125 to 0.125
- w_value: bfloat16 [2048, 256], P(None, 'head'), may hold values from -0.125 to 0.125
- w_out: bfloat16 [2048, 2048], P(None, 'head'), may hold values from -1 to 1
- mlp_gain: bfloat16 [2048], replicated, may hold values from 0.5 to 1.5
- gate_weight: bfloat16 [2048, 5632], P(None, 'head'), may hold values from -0.125 to 0.125
- up_weight: bfloat16 [2048, 5632], P(None, 'head'), may hold values from -0.125 to 0.125
- down_weight: bfloat16 [2048, 5632], P(None, 'head'), may hold values from -0.15625 to 0.15625
Outputs:
- output: bfloat16 [2048, 4, 2048], P('blk', 'dp', 'head')
- grad_input: float32 [2048, 4, 2048], P('blk', 'dp', 'head')
- grad_attn_gain: float32 [2048], P(('dp', 'blk'))
- grad_w_query: float32 [2048, 2048], P(('dp', 'blk'), 'head')
- grad_w_key: float32 [2048, 256], P(('dp', 'blk'), 'head')
- grad_w_value: float32 [2048, 256], P(('dp', 'blk'), 'head')
- grad_w_out: float32 [2048, 2048], P(('dp', 'blk'), 'head')
- grad_mlp_gain: float32 [2048], P(('dp', 'blk'))
- grad_w_gate: float32 [2048, 5632], P(('dp', 'blk'), 'head')
- grad_w_up: float32 [2048, 5632], P(('dp', 'blk'), 'head')
- grad_w_down: float32 [2048, 5632], P(('dp', 'blk'), 'head')
- stats: float32 [3], replicated
The draws below stay inside these ranges and needn't reach their ends.
Inputs may be any that keep to these rules, and one draw needn't show every extreme that they name: Each row's 8 lengths are documents laid end to end from position 0; they sum to at most 2048, and the positions past the sum are padding. Among the rows of each index of dp, one holds a single document that starts at position 0 and ends within the last 512 positions; its other lengths are 0. In the rows of the first index of dp that document fills the whole row.
All inputs are finite; a program needn't handle non-finite values.
Results may differ from the reference program's by a relative error of at most 0.02.
Values may be sent and summed in bfloat16 or wider, within the bound.
A program may use at most 320 MiB of HBM per device.

```python
import jax
import jax.numpy as jnp
from jax import lax

D = 2048
HEADS = 32
KVH = 4
HD = 64
FF = 5632
SEQ = 2048
DOCS = 8
ROWS = 1
BLOCK_TOK = 512
BATCH = 4


def draw_inputs(key, part):
    key = jax.random.fold_in(key, 5)
    key_one = jax.random.fold_in(key, 0)
    ramp = 1.0 + 2.0 * jnp.arange(SEQ, dtype=jnp.float32) / SEQ
    row_pos = jnp.arange(BATCH, dtype=jnp.float32) / max(BATCH - 1, 1)
    row_scale = 0.5 + 1.5 * row_pos
    values = jnp.clip(jax.random.normal(key_one, (SEQ, BATCH, D), jnp.float32), -5.0, 5.0) * ramp[:, None, None] * row_scale[None, :, None]
    return values.astype(jnp.bfloat16)


def draw_lengths(key, part):
    key = jax.random.fold_in(key, 9)
    key_a, key_b, key_c, key_d = jax.random.split(key, 4)
    shares = jax.random.randint(key_a, (BATCH, DOCS), 1, 9)
    padding = jax.random.randint(key_b, (BATCH,), 0, SEQ // 4 + 1)
    row_total = SEQ - padding
    climb = jnp.cumsum(shares, axis=1)
    bounds = row_total[:, None] * climb // climb[:, -1:]
    packed = bounds - jnp.concatenate([jnp.zeros((BATCH, 1), jnp.int32), bounds[:, :-1]], axis=1)
    groups = BATCH // ROWS
    chosen = jnp.arange(groups, dtype=jnp.int32) * ROWS + jax.random.randint(key_c, (groups,), 0, ROWS)
    row_index = jnp.arange(BATCH, dtype=jnp.int32)
    marked = jnp.any(row_index[:, None] == chosen[None, :], axis=1)
    tail_pad = jax.random.randint(key_d, (BATCH,), 0, max(BLOCK_TOK // 2, 1))
    tail_pad = jnp.where(row_index < ROWS, 0, tail_pad)
    single = jnp.concatenate([(SEQ - tail_pad)[:, None], jnp.zeros((BATCH, DOCS - 1), jnp.int32)], axis=1)
    return jnp.where(marked[:, None], single, packed).astype(jnp.int32)


def block_levels(stream_key, extent, shards, low, high):
    factor_of, own = 1.0, jax.random.fold_in(stream_key, 6)
    for dim, blocks in shards:
        draws = jnp.exp(jax.random.uniform(jax.random.fold_in(own, dim), (blocks,), jnp.float32, low / len(shards), high / len(shards)))
        factor_of = factor_of * jnp.repeat(draws, extent[dim] // blocks).reshape([-1 if axis == dim else 1 for axis in range(len(extent))])
    return factor_of


def scatter_about(key, extent, deviation, limit, shards=(), kind=jnp.bfloat16):
    values = deviation * jax.random.normal(key, extent, jnp.float32)
    if shards:
        values = values * block_levels(key, extent, shards, -0.22, 0.18)
    return jnp.clip(values, -limit, limit).astype(kind)


def setup_inputs(seed: int = 0) -> dict:
    streams_of = jax.random.split(jax.random.key(seed), 13)
    inputs = draw_inputs(jax.random.fold_in(streams_of[12], 71), 0)
    cotangent = scatter_about(streams_of[1], (SEQ, BATCH, D), 1.0, 6.0, ((0, 4), (1, 4), (2, 2)))
    lengths = draw_lengths(jax.random.fold_in(streams_of[12], 71), 0)
    attn_gain = jnp.clip(1.0 + 0.1 * jax.random.normal(streams_of[3], (D,), jnp.float32), 0.5, 1.5).astype(jnp.bfloat16)
    w_query = scatter_about(streams_of[4], (D, HEADS * HD), D ** -0.5, 0.125, ((1, 2),))
    w_key = scatter_about(streams_of[5], (D, KVH * HD), D ** -0.5, 0.125, ((1, 2),))
    w_value = scatter_about(streams_of[6], (D, KVH * HD), D ** -0.5, 0.125, ((1, 2),))
    w_out = scatter_about(streams_of[7], (D, HEADS * HD), (HEADS * HD // 64) ** -0.5, 1.0, ((1, 2),))
    mlp_gain = jnp.clip(1.0 + 0.1 * jax.random.normal(streams_of[8], (D,), jnp.float32), 0.5, 1.5).astype(jnp.bfloat16)
    gate_weight = scatter_about(streams_of[9], (D, FF), D ** -0.5, 0.125, ((1, 2),))
    up_weight = scatter_about(streams_of[10], (D, FF), D ** -0.5, 0.125, ((1, 2),))
    down_weight = scatter_about(streams_of[11], (D, FF), (FF // 4) ** -0.5, 0.15625, ((1, 2),))
    return {"inputs": inputs, "cotangent": cotangent, "lengths": lengths, "attn_gain": attn_gain, "w_query": w_query, "w_key": w_key, "w_value": w_value, "w_out": w_out, "mlp_gain": mlp_gain, "gate_weight": gate_weight, "up_weight": up_weight, "down_weight": down_weight}


EPS = 1e-05
THETA = 10000.0

@jax.custom_vjp
def low(v):
    return lax.optimization_barrier(v.astype(jnp.bfloat16)).astype(jnp.float32)

@jax.custom_vjp
def low_back(v):
    return v

def low_keep(v):
    return (low(v), None)

def low_pass(kept, grad):
    return (grad,)

def back_keep(v):
    return (v, None)

def back_low(kept, grad):
    return (low(grad),)
low.defvjp(low_keep, low_pass)
low_back.defvjp(back_keep, back_low)

def rms_norm(values, gain_vec):
    return values * lax.rsqrt(lax.optimization_barrier(jnp.mean(values * values, axis=-1, keepdims=True)) + EPS) * gain_vec

def rope_tables(positions):
    idx_freq = jnp.arange(HD // 2, dtype=jnp.float32)
    inv_freq = jnp.power(THETA, -2.0 * idx_freq / HD)
    angles = positions.astype(jnp.float32)[:, None] * inv_freq[None, :]
    return (jnp.cos(angles), jnp.sin(angles))

def rotate(tensor, cos_tab, sin_tab):
    first_h = tensor[..., :HD // 2]
    second_h = tensor[..., HD // 2:]
    cos_b = cos_tab[:, None, :]
    sin_b = sin_tab[:, None, :]
    return jnp.concatenate([first_h * cos_b - second_h * sin_b, second_h * cos_b + first_h * sin_b], axis=-1)

def attend(queries, keys, values, seg_ids, positions):
    block_len = min(512, SEQ)
    block_count = SEQ // block_len
    group = HEADS // KVH
    scale = HD ** (-0.5)

    def one_block(block_args):
        q_block, q_pos, q_seg = block_args
        raw_score = low_back(jnp.einsum('qkgd,skd->qkgs', q_block, keys, precision=lax.Precision.HIGHEST))
        scores = raw_score * scale
        key_mask = (seg_ids[None, :] == q_seg[:, None]) & (positions[None, :] <= q_pos[:, None])
        scores = jnp.where(key_mask[:, None, None, :], scores, -1e+30)
        row_top = lax.optimization_barrier(jnp.max(scores, axis=-1, keepdims=True))
        expo_s = jnp.exp(scores - row_top)
        prob_w = low(expo_s / lax.optimization_barrier(jnp.sum(expo_s, axis=-1, keepdims=True)))
        return jnp.einsum('qkgs,skd->qkgd', prob_w, values, precision=lax.Precision.HIGHEST)
    outs_b = lax.map(jax.checkpoint(one_block), (queries.reshape(block_count, block_len, KVH, group, HD), positions.reshape(block_count, block_len), seg_ids.reshape(block_count, block_len)))
    return outs_b.reshape(SEQ, HEADS * HD)

def row_forward(params, row_in, doc_ends):
    g_one, wq_f, wk_f, wv_f, wo_f, g_two, wg_f, wu_f, wd_f = params
    hp = lax.Precision.HIGHEST
    positions = jnp.arange(SEQ, dtype=jnp.int32)
    seg_ids = lax.optimization_barrier(jnp.sum((doc_ends[None, :] <= positions[:, None]).astype(jnp.int32), axis=1))
    cos_tab, sin_tab = rope_tables(positions)
    a_one = low(rms_norm(row_in, g_one))
    q_lin = jnp.dot(a_one, wq_f, precision=hp).reshape(SEQ, HEADS, HD)
    queries = low(rotate(low_back(q_lin), cos_tab, sin_tab))
    k_lin = jnp.dot(a_one, wk_f, precision=hp).reshape(SEQ, KVH, HD)
    keys = low(rotate(low_back(k_lin), cos_tab, sin_tab))
    values = low(low_back(jnp.dot(a_one, wv_f, precision=hp))).reshape(SEQ, KVH, HD)
    attn_o = attend(queries.reshape(SEQ, KVH, HEADS // KVH, HD), keys, values, seg_ids, positions)
    out_low = low(low_back(attn_o))
    attn = low_back(jnp.dot(out_low, wo_f.T, precision=hp))
    resid = row_in + attn
    second_activation = low(rms_norm(resid, g_two))
    gate_value = low_back(jnp.dot(second_activation, wg_f, precision=hp))
    up_projected = low_back(jnp.dot(second_activation, wu_f, precision=hp))
    hidden_state = low(jax.nn.silu(gate_value) * up_projected)
    mlp = jnp.dot(hidden_state, wd_f.T, precision=hp)
    result = resid + mlp
    valid = (seg_ids < DOCS).astype(jnp.float32)
    sums = jnp.stack([jnp.sum(valid), jnp.sum(valid * lax.optimization_barrier(jnp.sum(row_in * row_in, axis=-1))), jnp.sum(valid * lax.optimization_barrier(jnp.sum(attn * attn, axis=-1))), jnp.sum(valid * lax.optimization_barrier(jnp.sum(mlp * mlp, axis=-1)))])
    return (result, sums)

def reference(inputs, cotangent, lengths, attn_gain, w_query, w_key, w_value, w_out, mlp_gain, gate_weight, up_weight, down_weight):
    params = tuple((p.astype(jnp.float32) for p in (attn_gain, w_query, w_key, w_value, w_out, mlp_gain, gate_weight, up_weight, down_weight)))
    rows_in = jnp.transpose(inputs, (1, 0, 2)).astype(jnp.float32)
    rows_dy = jnp.transpose(cotangent, (1, 0, 2)).astype(jnp.float32)
    doc_ends = jnp.cumsum(lengths, axis=1).astype(jnp.int32)

    def row_step(totals, row_item):
        row_in, row_dy, row_ends = row_item

        def forward(param_set, values_in):
            return row_forward(param_set, values_in, row_ends)
        row_out, pull_back, row_sums = jax.vjp(forward, params, row_in, has_aux=True)
        param_grads, row_dx = pull_back(row_dy)
        new_grads = jax.tree.map(jnp.add, totals[0], param_grads)
        return ((new_grads, totals[1] + row_sums), (row_out, row_dx))
    start_vals = (jax.tree.map(jnp.zeros_like, params), jnp.zeros((4,), jnp.float32))
    (grads, sums), (outs_rows, dx_rows) = lax.scan(row_step, start_vals, (rows_in, rows_dy, doc_ends))
    stats = jnp.sqrt(sums[1:] / (sums[0] * D))
    output = jnp.transpose(outs_rows, (1, 0, 2)).astype(jnp.bfloat16)
    grad_input = jnp.transpose(dx_rows, (1, 0, 2))
    return (output, grad_input, grads[0], grads[1], grads[2], grads[3], grads[4], grads[5], grads[6], grads[7], grads[8], stats)
```

```python
import functools

import jax
import jax.numpy as jnp
from jax import lax
from jax.experimental import pallas as pl
from jax.experimental.pallas import tpu as pltpu
from jax.sharding import PartitionSpec as P

HD = 64
PAIR = 2 * HD
DOCS = 8
EPS = 1e-05
THETA = 10000.0
NEG = -1e30
F32 = jnp.float32
BF16 = jnp.bfloat16
FT = 256


EARLY, LATE = 0.4, 0.4
WEIGHT = [EARLY]


def params(mib):
    return pltpu.CompilerParams(vmem_limit_bytes=mib << 20)


def cost(flops, byte_count, trans=0):
    return pl.CostEstimate(
        flops=int(flops * WEIGHT[0]),
        bytes_accessed=int(byte_count * WEIGHT[0]),
        transcendentals=int(trans * WEIGHT[0]),
    )


CHAIN = []


def in_hbm(x):
    return pltpu.with_memory_space_constraint(x, pltpu.HBM)


def launch(kernel, args, *, grid, in_specs, out_specs, out_shape, mib, estimate, name, scratch=(), prefetch=0, deps=(), pin_in=True, pin_out=True):
    extra = list(CHAIN) + list(deps)
    n_in, n_out = len(args), len(out_shape)

    def wrapped(*refs):
        rest = refs[n_in + len(extra) :]
        kernel(*refs[:n_in], *rest[:n_out], *rest[n_out + 1 :])

    if pin_in:
        args = tuple(args[:prefetch]) + tuple(in_hbm(x) for x in args[prefetch:])
    if pin_out:
        out_shape = [pltpu.HBM(o.shape, o.dtype) for o in out_shape]
    extra = [in_hbm(x) for x in extra]
    *outs, token = pl.pallas_call(
        wrapped,
        grid_spec=pltpu.PrefetchScalarGridSpec(
            num_scalar_prefetch=prefetch,
            grid=grid,
            in_specs=list(in_specs) + [pl.BlockSpec(memory_space=pltpu.HBM)] * len(extra),
            out_specs=list(out_specs) + [pl.BlockSpec(memory_space=pltpu.HBM)],
            scratch_shapes=list(scratch),
        ),
        out_shape=list(out_shape) + [pltpu.HBM((8, 128), F32)],
        compiler_params=params(mib),
        cost_estimate=estimate,
        name=name,
    )(*args, *extra)
    CHAIN[:] = [token]
    return outs


def dot(a, b):
    return jnp.dot(a, b, preferred_element_type=F32)


def dot_nt(a, b):
    return lax.dot_general(a, b, (((1,), (1,)), ((), ())), preferred_element_type=F32)


def dot_tn(a, b):
    return lax.dot_general(a, b, (((0,), (0,)), ((), ())), preferred_element_type=F32)


def swap(x, axis, bit):
    n = lax.axis_size(axis)
    return lax.ppermute(x, axis, [(i, i ^ bit) for i in range(n)])


def lanes(shape):
    return lax.broadcasted_iota(jnp.int32, shape, len(shape) - 1)


def turn(x, cos, sin):
    out = []
    for c in range(x.shape[1] // PAIR):
        v = x[:, c * PAIR : (c + 1) * PAIR]
        low = lanes(v.shape) % HD < HD // 2
        other = jnp.where(low, pltpu.roll(v, PAIR - HD // 2, 1), pltpu.roll(v, HD // 2, 1))
        out.append(v * cos + other * sin)
    return out[0] if len(out) == 1 else jnp.concatenate(out, axis=1)


def project_kernel(h_ref, own, oth, gain, wq, wk, wv, cos, sin, full, a1, q, kv, ssx):
    first = h_ref[0] == 0
    x_own = own[...].astype(F32)
    x_oth = oth[...].astype(F32)
    x = jnp.concatenate(
        [jnp.where(first, x_own, x_oth), jnp.where(first, x_oth, x_own)], axis=1
    )
    width = x.shape[1]
    total = jnp.sum(x * x, axis=1, keepdims=True)
    inv = lax.rsqrt(total * (1.0 / width) + EPS)
    act = (x * inv * gain[...]).astype(BF16)
    full[...] = x.astype(BF16)
    a1[...] = act
    ssx[...] = jnp.broadcast_to(total, ssx.shape)
    q[...] = turn(dot(act, wq[...]), cos[...], sin[...]).astype(BF16) * (HD**-0.5)
    kvw = wk.shape[1]
    kv[:, :kvw] = turn(dot(act, wk[...]), cos[...], sin[...]).astype(BF16)
    kv[:, kvw:] = dot(act, wv[...]).astype(BF16)


def project(h, own, oth, gain, wq, wk, wv, cos, sin):
    n, half = own.shape
    d = 2 * half
    tt = min(n, 256)
    qw, kvw = wq.shape[1], wk.shape[1]
    row = lambda w: pl.BlockSpec((tt, w), lambda i, *_: (i, 0))
    const = lambda a: pl.BlockSpec(a.shape, lambda i, *_: (0, 0), pipeline_mode=pl.Buffered(1))
    return launch(
        project_kernel,
        (h, own, oth, gain, wq, wk, wv, cos, sin),
        prefetch=1,
        grid=(n // tt,),
        in_specs=[row(half), row(half), const(gain), const(wq), const(wk), const(wv)]
        + [row(PAIR), row(PAIR)],
        out_specs=[row(d), row(d), row(qw), row(2 * kvw), row(PAIR)],
        out_shape=[
            jax.ShapeDtypeStruct((n, d), BF16),
            jax.ShapeDtypeStruct((n, d), BF16),
            jax.ShapeDtypeStruct((n, qw), BF16),
            jax.ShapeDtypeStruct((n, 2 * kvw), BF16),
            jax.ShapeDtypeStruct((n, PAIR), F32),
        ],
        mib=32,
        pin_in=False,
        estimate=cost(2 * n * d * (qw + 2 * kvw), 2 * d * (qw + 2 * kvw) + 12 * n * d),
        name="project",
    )


def place(kv, kvh, base):
    x = kv[:, base : base + PAIR].astype(F32)
    x = jnp.where(kvh == 0, x, pltpu.roll(x, HD, 1))
    low = jnp.where(lanes(x.shape) < HD, x, 0.0)
    return low.astype(BF16), pltpu.roll(low, HD, 1).astype(BF16)


def flip_head(kv, kvh, base):
    x = kv[:, base : base + PAIR].astype(F32).T
    return jnp.where(kvh == 0, x[:HD, :], x[HD:, :])


def attend_kernel(step, last, ppk, sc, q_ref, kv_ref, start_ref, *refs):
    refs = list(refs)
    if step:
        acc_in, ml_in = refs[:2]
        refs = refs[2:]
    acc_out, ml_out = refs
    t = q_ref.shape[0]
    kvh = pl.program_id(1)
    blk = sc[0]

    def finish(pair, par, acc, m, l):
        rows = slice(pair * PAIR + par * HD, pair * PAIR + (par + 1) * HD)
        if last:
            acc = acc / l
            m = m + jnp.log(l)
        acc_out[rows, :] = acc
        ml_out[pair, par : par + 1, :] = m
        ml_out[pair, 2 + par : 3 + par, :] = l

    heads = [(pair, par) for pair in range(ppk) for par in range(2)]

    def work():
        u = lax.broadcasted_iota(jnp.int32, (t, t), 0) + (blk - step) * t
        keep = u >= start_ref[0]
        if step == 0:
            keep = keep & (u <= lanes((t, t)) + blk * t)
        bias = jnp.where(keep, 0.0, NEG)
        kv = kv_ref[...]
        kk = place(kv, kvh, 0)
        ones = jnp.where(lax.broadcasted_iota(jnp.int32, (16, t), 0) == 0, 1.0, 0.0)
        vt = jnp.concatenate([flip_head(kv, kvh, PAIR), ones], axis=0).astype(BF16)
        scores = [
            dot_nt(kk[par], q_ref[:, pair * PAIR : (pair + 1) * PAIR]) + bias
            for pair, par in heads
        ]
        for (pair, par), s in zip(heads, scores, strict=True):
            m = jnp.max(s, axis=0, keepdims=True)
            if step:
                old = ml_in[pair, par : par + 1, :]
                m = jnp.maximum(m, old)
            pv = dot(vt, jnp.exp(s - m).astype(BF16))
            acc, l = pv[:HD], pv[HD : HD + 1]
            if step:
                factor = jnp.exp(old - m)
                rows = slice(pair * PAIR + par * HD, pair * PAIR + (par + 1) * HD)
                acc = acc + acc_in[rows, :] * factor
                l = l + ml_in[pair, 2 + par : 3 + par, :] * factor
            finish(pair, par, acc, m, l)

    if step == 0:
        work()
    else:
        pl.when(blk >= step)(work)

        @pl.when(blk < step)
        def _():
            for pair, par in heads:
                rows = slice(pair * PAIR + par * HD, pair * PAIR + (par + 1) * HD)
                m = ml_in[pair, par : par + 1, :]
                finish(pair, par, acc_in[rows, :], m, ml_in[pair, 2 + par : 3 + par, :])


def attend(step, last, sc, q, kv, start, state, rows, deps=()):
    n, qw = q.shape
    t = n // rows
    pairs = qw // PAIR
    kv_heads = kv.shape[1] // 2 // HD
    ppk = pairs // kv_heads
    accspec = pl.BlockSpec((ppk * PAIR, t), lambda r, k, *_: (k, r))
    mlspec = pl.BlockSpec((ppk, 8, t), lambda r, k, *_: (k, 0, r))
    work = n * t * qw
    return launch(
        functools.partial(attend_kernel, step, last, ppk),
        (sc, in_hbm(q), in_hbm(kv), in_hbm(start), *state),
        prefetch=1,
        grid=(rows, kv_heads),
        in_specs=[
            pl.BlockSpec((t, ppk * PAIR), lambda r, k, *_: (r, k)),
            pl.BlockSpec((t, kv.shape[1]), lambda r, k, *_: (r, 0)),
            pl.BlockSpec((1, 1, t), lambda r, k, *_: (r, 0, 0)),
        ]
        + ([accspec, mlspec] if state else []),
        out_specs=[accspec, mlspec],
        out_shape=[
            jax.ShapeDtypeStruct((qw, n), F32),
            jax.ShapeDtypeStruct((pairs, 8, n), F32),
        ],
        mib=28,
        estimate=cost(24 * work, 20 * n * qw, n * t * qw // HD),
        name=f"attend{step}",
        deps=deps,
        pin_in=False,
        pin_out=False,
    )


def flip_kernel(x, out):
    out[...] = x[...].T.astype(BF16)


def flip(x, name="flip"):
    w, n = x.shape
    by_rows = w > n
    step = 512 if max(w, n) % 512 == 0 else max(w, n)
    across = pl.BlockSpec((step, n) if by_rows else (w, step), lambda i: (i, 0) if by_rows else (0, i))
    down = pl.BlockSpec((n, step) if by_rows else (step, w), lambda i: (0, i) if by_rows else (i, 0))
    return launch(
        flip_kernel,
        (x,),
        grid=(max(w, n) // step,),
        in_specs=[across],
        out_specs=[down],
        out_shape=[jax.ShapeDtypeStruct((n, w), BF16)],
        mib=32,
        estimate=cost(8 * n * w, 6 * n * w),
        name=name,
        pin_in=False,
    )[0]


def attend_back_kernel(step, first, last, ppk, sc, q_ref, do_ref, ml_ref, start_ref, kv_ref, *refs):
    refs = list(refs)
    o_ref = refs.pop(0) if first else None
    dq_in, delta_in = (None, None) if first else (refs.pop(0), refs.pop(0))
    cos, sin = (refs.pop(0), refs.pop(0)) if last else (None, None)
    dq_out, dkv_out = refs.pop(0), refs.pop(0)
    delta_out = refs.pop(0) if first else None
    dk_acc, dv_acc, dq_acc = refs
    t = q_ref.shape[0]
    kvh = pl.program_id(1)
    blk = sc[0]
    heads = [(pair, par) for pair in range(ppk) for par in range(2)]

    if first:
        for pair in range(ppk):
            both = slice(pair * PAIR, (pair + 1) * PAIR)
            prod = (do_ref[:, both].astype(F32) * o_ref[:, both].astype(F32)).T
            for par in range(2):
                delta_out[pair, par : par + 1, :] = jnp.sum(
                    prod[par * HD : (par + 1) * HD, :], axis=0, keepdims=True
                )
        dq_acc[...] = jnp.zeros_like(dq_acc)
    else:
        dq_acc[...] = dq_in[...]
    delta = delta_out if first else delta_in

    @pl.when(kvh == 0)
    def _():
        dkv_out[...] = jnp.zeros_like(dkv_out)

    def work():
        u = lax.broadcasted_iota(jnp.int32, (t, t), 0) + (blk - step) * t
        keep = u >= start_ref[0]
        if step == 0:
            keep = keep & (u <= lanes((t, t)) + blk * t)
        bias = jnp.where(keep, 0.0, NEG)
        kv = kv_ref[...]
        kk = place(kv, kvh, 0)
        vv = place(kv, kvh, PAIR)
        kt = flip_head(kv, kvh, 0).astype(BF16)
        dk_acc[...] = jnp.zeros_like(dk_acc)
        dv_acc[...] = jnp.zeros_like(dv_acc)
        for pair, par in heads:
            q = q_ref[:, pair * PAIR : (pair + 1) * PAIR]
            do = do_ref[:, pair * PAIR : (pair + 1) * PAIR]
            st = dot_nt(kk[par], q) + bias
            dp = dot_nt(vv[par], do)
            pt = jnp.exp(st - ml_ref[pair, par : par + 1, :])
            ds = (pt * (dp - delta[pair, par : par + 1, :])).astype(BF16)
            dv_acc[par] += dot(pt.astype(BF16), do)
            dk_acc[par] += dot(ds, q)
            rows = slice(pair * PAIR + par * HD, pair * PAIR + (par + 1) * HD)
            dq_acc[rows, :] += dot(kt, ds)
        low = lanes((t, PAIR)) < HD
        for acc, base in ((dk_acc, 0), (dv_acc, PAIR)):
            both = acc[0] + pltpu.roll(acc[1], HD, 1)
            here = jnp.where(kvh == 0, both, pltpu.roll(both, HD, 1))
            mine = low == (kvh == 0)
            old = dkv_out[:, base : base + PAIR].astype(F32)
            dkv_out[:, base : base + PAIR] = jnp.where(mine, here, old).astype(BF16)

    if step == 0:
        work()
    else:
        pl.when(blk >= step)(work)

    if last:
        for pair in range(ppk):
            rows = slice(pair * PAIR, (pair + 1) * PAIR)
            dq = (dq_acc[rows, :] * (HD**-0.5)).T
            dq_out[:, rows] = turn(dq, cos[...], -sin[...]).astype(BF16)
    else:
        dq_out[...] = dq_acc[...]


def attend_back(step, first, last, sc, q, do, o, ml, start, cos, sin, kv, state, rows, deps=()):
    n, qw = q.shape
    t = n // rows
    pairs = qw // PAIR
    kvw = kv.shape[1]
    kv_heads = kvw // 2 // HD
    ppk = pairs // kv_heads
    width = ppk * PAIR
    pairspec = pl.BlockSpec((t, width), lambda r, k, *_: (r, k))
    accspec = pl.BlockSpec((width, t), lambda r, k, *_: (k, r))
    mlspec = pl.BlockSpec((ppk, 8, t), lambda r, k, *_: (k, 0, r))
    rowspec = lambda w: pl.BlockSpec((t, w), lambda r, k, *_: (r, 0))
    work = n * t * qw
    return launch(
        functools.partial(attend_back_kernel, step, first, last, ppk),
        (sc, q, do, ml, start, kv)
        + ((o,) if first else tuple(state))
        + ((cos, sin) if last else ()),
        prefetch=1,
        grid=(rows, kv_heads),
        in_specs=[pairspec, pairspec, mlspec]
        + [pl.BlockSpec((1, 1, t), lambda r, k, *_: (r, 0, 0))]
        + [rowspec(kvw)]
        + ([pairspec] if first else [accspec, mlspec])
        + ([rowspec(PAIR)] * 2 if last else []),
        out_specs=[pairspec if last else accspec, rowspec(kvw)] + ([mlspec] if first else []),
        scratch=[
            pltpu.VMEM((2, t, PAIR), F32),
            pltpu.VMEM((2, t, PAIR), F32),
            pltpu.VMEM((width, t), F32),
        ],
        out_shape=[
            jax.ShapeDtypeStruct((n, qw), BF16) if last else jax.ShapeDtypeStruct((qw, n), F32),
            jax.ShapeDtypeStruct((n, kvw), BF16),
        ]
        + ([jax.ShapeDtypeStruct((pairs, 8, n), F32)] if first else []),
        mib=40,
        estimate=cost(54 * work, 20 * n * qw, work // HD),
        name=f"attend_back{step}",
        deps=deps,
    )


def gather_dkv_kernel(count, *refs):
    parts = refs[:count]
    cos, sin, out = refs[count:]
    total = parts[0][...].astype(F32)
    for x in parts[1:]:
        total = total + x[...].astype(F32)
    half = total.shape[1] // 2
    out[:, :half] = turn(total[:, :half], cos[...], -sin[...]).astype(BF16)
    out[:, half:] = total[:, half:].astype(BF16)


def gather_dkv(parts, cos, sin, deps=()):
    whole = lambda x: pl.BlockSpec(x.shape, lambda i: (0, 0))
    return launch(
        functools.partial(gather_dkv_kernel, len(parts)),
        (*parts, cos, sin),
        grid=(1,),
        in_specs=[whole(x) for x in (*parts, cos, sin)],
        out_specs=[whole(parts[0])],
        out_shape=[jax.ShapeDtypeStruct(parts[0].shape, BF16)],
        mib=32,
        estimate=cost(10 * parts[0].size, 4 * len(parts) * parts[0].size),
        name="gather_dkv",
        deps=deps,
    )[0]


def merge_kernel(o_own, o_oth, w_own, w_oth, full, gain, h1, a2, a2_t, r2, ssa, held, sums):
    i = pl.program_id(0)
    attn = dot_nt(o_own[...], w_own[...]) + dot_nt(o_oth[...], w_oth[...])
    x = full[...].astype(F32) + attn
    h1[0] = x
    held[i] = x

    @pl.when(i == 0)
    def _():
        sums[...] = jnp.zeros_like(sums)
        ssa[...] = jnp.zeros_like(ssa)

    sums[...] += jnp.sum(x * x, axis=1, keepdims=True)
    ssa[...] += jnp.sum(attn * attn, axis=1, keepdims=True)

    @pl.when(i == pl.num_programs(0) - 1)
    def _():
        count, _, dt = held.shape
        inv = lax.rsqrt(sums[...] * (1.0 / (count * dt)) + EPS)
        r2[...] = inv
        for j in range(count):
            at = slice(j * dt, (j + 1) * dt)
            act = (held[j] * inv[:, :1] * gain[:, at]).astype(BF16)
            a2[:, at] = act
            a2_t[at, :] = act.T


def merge(o_own, o_oth, w_own, w_oth, full, gain, deps=()):
    n, d = full.shape
    dt = 512
    e = o_own.shape[1]
    const = lambda a: pl.BlockSpec(a.shape, lambda i: (0, 0), pipeline_mode=pl.Buffered(1))
    return launch(
        merge_kernel,
        (o_own, o_oth, w_own, w_oth, full, gain),
        grid=(d // dt,),
        in_specs=[
            const(o_own),
            const(o_oth),
            pl.BlockSpec((dt, e), lambda i: (i, 0)),
            pl.BlockSpec((dt, e), lambda i: (i, 0)),
            pl.BlockSpec((n, dt), lambda i: (0, i)),
            const(gain),
        ],
        out_specs=[
            pl.BlockSpec((1, n, dt), lambda i: (i, 0, 0)),
            pl.BlockSpec((n, d), lambda i: (0, 0)),
            pl.BlockSpec((d, n), lambda i: (0, 0)),
            pl.BlockSpec((n, PAIR), lambda i: (0, 0)),
            pl.BlockSpec((n, PAIR), lambda i: (0, 0)),
        ],
        out_shape=[
            jax.ShapeDtypeStruct((d // dt, n, dt), F32),
            jax.ShapeDtypeStruct((n, d), BF16),
            jax.ShapeDtypeStruct((d, n), BF16),
            jax.ShapeDtypeStruct((n, PAIR), F32),
            jax.ShapeDtypeStruct((n, PAIR), F32),
        ],
        scratch=[pltpu.VMEM((d // dt, n, dt), F32), pltpu.VMEM((n, PAIR), F32)],
        mib=48,
        estimate=cost(3 * n * d * d, 2 * d * d + 12 * n * d),
        name="merge",
        deps=deps,
    )


def units_kernel(a2, g, wg, wu, wd, out):
    gate = dot(a2[...], wg[...])
    up = dot(a2[...], wu[...])
    dh = dot(g[...], wd[...])
    sig = jax.nn.sigmoid(gate)
    act = gate * sig
    out[0] = (act * up).astype(BF16)
    out[1] = (dh * up * sig * (1.0 + gate * (1.0 - sig))).astype(BF16)
    out[2] = (dh * act).astype(BF16)


def units(a2, g, wg, wu, wd, first, count):
    n, d = a2.shape
    const = pl.BlockSpec((n, d), lambda i: (0, 0), pipeline_mode=pl.Buffered(1))
    wspec = pl.BlockSpec((d, FT), lambda i: (0, first + i))
    return launch(
        units_kernel,
        (a2, g, wg, wu, wd),
        grid=(count,),
        in_specs=[const, const, wspec, wspec, wspec],
        out_specs=[pl.BlockSpec((3, n, FT), lambda i: (0, 0, i))],
        out_shape=[jax.ShapeDtypeStruct((3, n, count * FT), BF16)],
        mib=58,
        estimate=cost(10 * n * d * FT * count, 6 * d * FT * count, n * FT * count),
        name=f"units{first}",
    )[0]


def back_kernel(plan, split, *refs):
    acts = refs[: len(plan)]
    weights = refs[len(plan) : -1]
    out = refs[-1]
    total = None
    for act, (w, at) in zip(acts, plan, strict=True):
        term = dot_nt(act[0], weights[w][:, at : at + act.shape[2]])
        total = term if total is None else total + term
    if split:
        out[0] = total.astype(BF16)
    else:
        out[...] = total.astype(BF16)


def back(groups, split, name):
    acts, specs, plan = [], [], []
    for w, (members, _) in enumerate(groups):
        at = 0
        for x, i in members:
            acts.append(x)
            specs.append(
                pl.BlockSpec(
                    (1,) + x.shape[1:], lambda j, i=i: (i, 0, 0), pipeline_mode=pl.Buffered(1)
                )
            )
            plan.append((w, at))
            at += x.shape[2]
    weights = [w for _, w in groups]
    n = acts[0].shape[1]
    d = weights[0].shape[0]
    dt = 256
    per = d // 2 // dt
    if split:
        ospec = pl.BlockSpec((1, n, dt), lambda i: (i // per, 0, i % per))
        oshape = (2, n, d // 2)
    else:
        ospec = pl.BlockSpec((n, dt), lambda i: (0, i))
        oshape = (n, d)
    ktotal = sum(w.shape[1] for w in weights)
    return launch(
        functools.partial(back_kernel, tuple(plan), split),
        (*acts, *weights),
        grid=(d // dt,),
        in_specs=specs + [pl.BlockSpec((dt, w.shape[1]), lambda i: (i, 0)) for w in weights],
        out_specs=[ospec],
        out_shape=[jax.ShapeDtypeStruct(oshape, BF16)],
        mib=58,
        estimate=cost(4 * n * d * ktotal, 2 * d * ktotal + 2 * n * (d + ktotal)),
        name=name,
    )[0]


def stream_kernel(da_own, da_oth, h1, r2, gain, g, w_out, dh1, dattn_t, dout, gsum):
    da = da_own[...].astype(F32) + da_oth[...].astype(F32)
    inv = r2[:, :1]
    norm = jnp.concatenate([h1[j] for j in range(h1.shape[0])], axis=1) * inv
    grad = da * norm

    @pl.when(pl.program_id(0) == 0)
    def _():
        gsum[...] = jnp.zeros_like(gsum)

    gsum[...] += jnp.sum(grad, axis=0, keepdims=True)
    e2 = da * gain[...]
    mean = jnp.sum(e2 * norm, axis=1, keepdims=True) * (1.0 / da.shape[1])
    dh = g[...].astype(F32) + inv * (e2 - norm * mean)
    dh1[...] = dh
    low = dh.astype(BF16)
    dattn_t[...] = low.T
    dout[...] = dot(low, w_out[...]).astype(BF16)


def stream(da_own, da_oth, h1, r2, gain, g, w_out, deps=()):
    parts, n, dt = h1.shape
    d = parts * dt
    tt = min(n, 128)
    ew = w_out.shape[1]
    row = lambda w: pl.BlockSpec((tt, w), lambda i: (i, 0))
    const = lambda a: pl.BlockSpec(a.shape, lambda i: (0, 0), pipeline_mode=pl.Buffered(1))
    return launch(
        stream_kernel,
        (da_own, da_oth, h1, r2, gain, g, w_out),
        grid=(n // tt,),
        in_specs=[
            row(d),
            row(d),
            pl.BlockSpec((parts, tt, dt), lambda i: (0, i, 0)),
            row(PAIR),
            const(gain),
            row(d),
            const(w_out),
        ],
        out_specs=[
            row(d),
            pl.BlockSpec((d, tt), lambda i: (0, i)),
            row(ew),
            pl.BlockSpec((1, d), lambda i: (0, 0)),
        ],
        out_shape=[
            jax.ShapeDtypeStruct((n, d), F32),
            jax.ShapeDtypeStruct((d, n), BF16),
            jax.ShapeDtypeStruct((n, ew), BF16),
            jax.ShapeDtypeStruct((1, d), F32),
        ],
        mib=56,
        estimate=cost(2 * n * d * ew, 2 * d * ew + 20 * n * d),
        name="stream",
        deps=deps,
    )


def entry_kernel(dq, dkv, wq, wk, wv, full, ssx, gain, part, gsum, rsum):
    kvw = wk.shape[1]
    da = dot_nt(dq[...], wq[...])
    da = da + dot_nt(dkv[:, :kvw], wk[...]) + dot_nt(dkv[:, kvw:], wv[...])
    width = pl.num_programs(0) * da.shape[1]
    inv = lax.rsqrt(ssx[:, :1] * (1.0 / width) + EPS)
    grad = da * (full[...].astype(F32) * inv)
    gsum[...] = jnp.sum(grad, axis=0, keepdims=True)

    @pl.when(pl.program_id(0) == 0)
    def _():
        rsum[...] = jnp.zeros_like(rsum)

    rsum[...] += jnp.sum(grad * gain[...], axis=1, keepdims=True)
    part[0] = da.astype(BF16)


def entry(dq, dkv, wq, wk, wv, full, ssx, gain):
    n, d = full.shape
    dt = 256
    per = d // 2 // dt
    const = lambda a: pl.BlockSpec(a.shape, lambda i: (0, 0), pipeline_mode=pl.Buffered(1))
    wspec = lambda w: pl.BlockSpec((dt, w.shape[1]), lambda i: (i, 0))
    return launch(
        entry_kernel,
        (dq, dkv, wq, wk, wv, full, ssx, gain),
        grid=(d // dt,),
        in_specs=[const(dq), const(dkv), wspec(wq), wspec(wk), wspec(wv)]
        + [
            pl.BlockSpec((n, dt), lambda i: (0, i)),
            const(ssx),
            pl.BlockSpec((1, dt), lambda i: (0, i)),
        ],
        out_specs=[
            pl.BlockSpec((1, n, dt), lambda i: (i // per, 0, i % per)),
            pl.BlockSpec((1, dt), lambda i: (0, i)),
            pl.BlockSpec((n, PAIR), lambda i: (0, 0)),
        ],
        out_shape=[
            jax.ShapeDtypeStruct((2, n, d // 2), BF16),
            jax.ShapeDtypeStruct((1, d), F32),
            jax.ShapeDtypeStruct((n, PAIR), F32),
        ],
        mib=56,
        estimate=cost(2 * n * d * (wq.shape[1] + 2 * wk.shape[1]), 20 * n * d),
        name="entry",
    )


def outer_kernel(shares, count, parts, adds, sc, *refs):
    k = 0
    lefts, rights = [], []
    for share in shares:
        lefts.append((refs[k : k + count], refs[k + count : k + 2 * count]))
        k += 2 * count
        rights.append([(refs[k + 2 * i], refs[k + 2 * i + 1]) for i in range(share)])
        k += 2 * share
    got = refs[k] if adds else None
    outs = refs[k + adds :]

    def work(out):
        m = 0
        for (left_own, left_oth), group in zip(lefts, rights, strict=True):
            rows = left_own[0].shape[0]
            for own, oth in group:
                at = slice(m * FT, (m + 1) * FT)
                for i in range(count):
                    part = slice(i * rows, (i + 1) * rows)
                    total = dot(left_own[i][...], own[0]) + dot(left_oth[i][...], oth[0])
                    if adds:
                        total = total + got[part, at].astype(F32)
                    out[part, at] = total.astype(BF16)
                m += 1

    if len(parts) == 1:
        work(outs[0])
        return
    step = pl.program_id(0)
    start = 0
    for out, size in zip(outs, parts, strict=True):
        pl.when((step >= start) & (step < start + size))(functools.partial(work, out))
        start += size


def outer(sc, groups, rows, first, parts, name, got=None, deps=()):
    n = groups[0][0].shape[1]
    count = sc.shape[0]
    number = sum(parts)
    shares = tuple(len(g[2]) for g in groups)
    ins, specs = [], []
    for own, oth, rights in groups:
        ins += [own] * count + [oth] * count
        for i in range(count):
            specs.append(pl.BlockSpec((rows, n), lambda j, s, i=i: (s[i], 0)))
        specs += specs[-count:]
        for r_own, r_oth, at in rights:
            ins += [r_own, r_oth]
            specs += [pl.BlockSpec((1, n, FT), lambda i, s, at=at: (at, 0, first + i))] * 2
    members = sum(shares)
    height = count * rows
    ospecs, start = [], 0
    for size in parts:
        ospecs.append(
            pl.BlockSpec(
                (height, members * FT),
                lambda i, s, start=start, size=size: (0, jnp.clip(i - start, 0, size - 1)),
            )
        )
        start += size
    if got is not None:
        ins.append(got)
        specs.append(ospecs[0])
    c = number * FT
    return launch(
        functools.partial(outer_kernel, shares, count, tuple(parts), int(got is not None)),
        (sc, *ins),
        prefetch=1,
        grid=(number,),
        in_specs=specs,
        out_specs=ospecs,
        out_shape=[jax.ShapeDtypeStruct((height, members * size * FT), BF16) for size in parts],
        mib=48,
        estimate=cost(8 * n * height * c * members, members * c * (4 * n + 2 * height)),
        name=name,
        deps=deps,
    )


def finish_kernel(count, *refs):
    parts = refs[:count]
    outs = refs[count:]
    at = 0
    for part in parts:
        for tile in range(part.shape[2] // (3 * FT)):
            for m in range(3):
                columns = slice((3 * tile + m) * FT, (3 * tile + m + 1) * FT)
                total = part[0, :, columns].astype(F32)
                for b in range(1, part.shape[0]):
                    total = total + part[b, :, columns].astype(F32)
                outs[m][:, at : at + FT] = total
            at += FT


def finish(parts, nblk):
    parts = [x.reshape(nblk, x.shape[0] // nblk, x.shape[1]) for x in parts]
    rows = parts[0].shape[1]
    width = sum(x.shape[2] for x in parts) // 3
    whole = lambda shape: pl.BlockSpec(shape, lambda i: (0,) * len(shape))
    return launch(
        functools.partial(finish_kernel, len(parts)),
        tuple(parts),
        grid=(1,),
        in_specs=[whole(x.shape) for x in parts],
        out_specs=[whole((rows, width))] * 3,
        out_shape=[jax.ShapeDtypeStruct((rows, width), F32)] * 3,
        mib=48,
        estimate=cost(0, 8 * nblk * rows * width),
        name="finish",
    )


def body(
    inputs,
    cotangent,
    lengths,
    attn_gain,
    w_query,
    w_key,
    w_value,
    w_out,
    mlp_gain,
    gate_weight,
    up_weight,
    down_weight,
):
    t, rows, half = inputs.shape
    n = t * rows
    heads = lax.axis_size("head")
    nblk = lax.axis_size("blk")
    ndp = lax.axis_size("dp")
    d = half * heads
    h = lax.axis_index("head").astype(jnp.int32)
    blk = lax.axis_index("blk").astype(jnp.int32)
    dp = lax.axis_index("dp").astype(jnp.int32)
    sc_h = h.reshape(1)
    sc_blk = blk.reshape(1)

    def flat(x):
        return jnp.transpose(x, (1, 0, 2)).reshape(n, x.shape[2])

    def unflat(x):
        return jnp.transpose(x.reshape(rows, t, x.shape[1]), (1, 0, 2))

    x_own = flat(inputs)
    g_own = flat(cotangent)
    gain_one = attn_gain.astype(F32).reshape(1, d)
    gain_two = mlp_gain.astype(F32).reshape(1, d)

    pos = blk * t + jnp.arange(t, dtype=jnp.int32)
    ends = jnp.cumsum(lengths, axis=1)
    passed = ends[:, None, :] <= pos[None, :, None]
    start = jnp.max(jnp.where(passed, ends[:, None, :], 0), axis=2)
    valid = (jnp.sum(passed.astype(jnp.int32), axis=2) < DOCS).astype(F32).reshape(n)
    start_rows = start.reshape(rows, 1, t)
    freq = jnp.power(THETA, -2.0 * jnp.arange(HD // 2, dtype=F32) / HD)
    angles = pos.astype(F32)[:, None] * freq[None, :]
    cos_h, sin_h = jnp.cos(angles), jnp.sin(angles)
    cos = jnp.tile(jnp.concatenate([cos_h, cos_h, cos_h, cos_h], axis=1), (rows, 1))
    sin = jnp.tile(jnp.concatenate([-sin_h, sin_h, -sin_h, sin_h], axis=1), (rows, 1))

    CHAIN.clear()
    WEIGHT[0] = EARLY

    def tie(x, *also):
        return lax.optimization_barrier((x, *also))[0]

    def by_head(x):
        return jnp.where(h == 0, x[:, :half], x[:, half:])

    def gate(x):
        x, CHAIN[0] = lax.optimization_barrier((x, CHAIN[0]))
        return x

    def mate(x):
        return swap(x, "dp", 1)

    x_oth = swap(x_own, "head", 1)
    share = w_out.shape[0] // ndp
    piece = lax.dynamic_slice_in_dim(w_out, dp * share, share, 0)
    x_oth, piece, g_own, cos, sin, start_rows = lax.optimization_barrier(
        (x_oth, piece, g_own, cos, sin, start_rows)
    )
    piece = swap(piece, "head", 1)
    full, a_one, queries, kv, ssx = project(
        sc_h, x_own, x_oth, gain_one, w_query, w_key, w_value, cos, sin
    )

    kvs, state = [kv], ()
    for s in range(nblk):
        if s + 1 < nblk:
            steps = [(i, i + 1) for i in range(s, nblk - 1)]
            kvs.append(lax.ppermute(kvs[s], "blk", steps))
        state = attend(s, s == nblk - 1, sc_blk, queries, kvs[s], start_rows, state, rows)
        if s + 1 < nblk - 1:
            kvs[s + 1] = gate(kvs[s + 1])
        if s == 0:
            a_one_t = flip(a_one, "flip_a")
            piece = gate(piece)
            w_out_oth = lax.all_gather(piece, "dp", axis=0, tiled=True)
            g_own, piece = lax.optimization_barrier((g_own, piece))
            g_oth = swap(g_own, "head", 1)
    acc, ml = state
    o_own = flip(acc)
    o_oth = swap(o_own, "head", 1)
    g_full = jnp.concatenate(
        [jnp.where(h == 0, g_own, g_oth), jnp.where(h == 0, g_oth, g_own)], axis=1
    )
    g_t = flip(g_full, "flip_g")
    o_mate, g_mate = mate(o_own), mate(g_t)
    h_one, a_two, a_two_t, inv_two, ssa = merge(
        o_own, o_oth, w_out, w_out_oth, full, gain_two
    )
    a_two_mate = mate(a_two_t)

    low_bit = dp & 1
    block_rows = d // ndp
    sc_send = (dp ^ 2).reshape(1)
    sc_keep = dp.reshape(1)
    sc_both = jnp.stack([2 * i + low_bit for i in range(ndp // 2)])
    y_groups = [[0, 2], [1, 3]]

    def both_halves(groups, parts, name, deps=()):
        return [
            lax.psum_scatter(
                x, "dp", scatter_dimension=0, axis_index_groups=y_groups, tiled=True
            )
            for x in outer(sc_both, groups, block_rows, 0, parts, name, deps=deps)
        ]

    def over_blk(x):
        return lax.all_to_all(x, "blk", split_axis=0, concat_axis=0, tiled=True)

    tiles = gate_weight.shape[1] // FT
    head_tiles = tiles // 4 + 1
    rest = tiles - head_tiles
    third = (rest + 2) // 3

    def unit_part(first, count):
        x = units(a_two, g_full, gate_weight, up_weight, down_weight, first, count)
        x_mate = mate(x)
        return x, [
            (g_t, g_mate, [(x, x_mate, 0)]),
            (a_two_t, a_two_mate, [(x, x_mate, 1), (x, x_mate, 2)]),
        ]

    part_a, groups_a = unit_part(0, head_tiles)
    (sum0,) = both_halves(groups_a, (head_tiles,), "mlp0")
    part_b, groups_b = unit_part(head_tiles, rest)

    da_own = back(
        [
            ([(part_a, 1), (part_b, 1)], gate_weight),
            ([(part_a, 2), (part_b, 2)], up_weight),
        ],
        False,
        "da_two",
    )
    da_oth = swap(da_own, "head", 1)
    sum1, sum2, sum3 = both_halves(groups_b, (third, third, rest - 2 * third), "mlp1")
    all0 = over_blk(gate(sum0))
    dh_one, d_attn_t, d_out, gain_two_sum = stream(
        da_own, da_oth, h_one, inv_two, gain_two, g_full, w_out
    )
    WEIGHT[0] = LATE
    d_attn_mate, a_one_mate = mate(d_attn_t), mate(gate(a_one_t))
    out_groups = [(d_attn_t, d_attn_mate, [(o_own[None], o_mate[None], 0)])]
    out_parts = (o_own.shape[1] // FT,)
    (first_out,) = outer(
        sc_send, out_groups, block_rows, 0, out_parts, "out_send", deps=(a_one_mate, all0)
    )
    got_out = swap(first_out, "dp", 2)
    all1 = over_blk(gate(sum1))
    branch = back([([(part_a, 0), (part_b, 0)], down_weight)], True, "branch")
    to_other = gate(lax.dynamic_index_in_dim(branch, 1 - h, 0, keepdims=False))
    branch_oth = swap(to_other, "head", 1)

    state, parts = (), []
    for s in reversed(range(nblk)):
        out = attend_back(
            s, s == nblk - 1, s == 0, sc_blk, queries, d_out, o_own, ml, start_rows, cos, sin,
            kvs[s], state, rows, deps=(),
        )
        state = (out[0], out[2] if s == nblk - 1 else state[1])
        part = out[1]
        parts.append(
            lax.ppermute(part, "blk", [(i, i - s) for i in range(s, nblk)]) if s else part
        )
        if s == 1:
            (keep_out,) = outer(
                sc_keep, out_groups, block_rows, 0, out_parts, "out_keep", got_out, deps=(all1,)
            )
            all2 = over_blk(gate(sum2))
            sum_out = lax.psum_scatter(keep_out, "blk", scatter_dimension=0, tiled=True)
    d_q = state[0]
    d_kv_own = gather_dkv(parts, cos, sin, deps=(branch_oth,))
    h_late, d_kv_own = lax.optimization_barrier((h_one, d_kv_own))
    h_half = jnp.concatenate(
        [
            jnp.where(h == 0, h_late[i], h_late[i + h_late.shape[0] // 2])
            for i in range(h_late.shape[0] // 2)
        ],
        axis=1,
    )
    mlp_half = lax.dynamic_index_in_dim(branch, h, 0, keepdims=False).astype(F32) + (
        branch_oth.astype(F32)
    )
    output = unflat((h_half + mlp_half).astype(BF16))
    d_qkv = jnp.concatenate([d_q, d_kv_own], axis=1)
    d_qkv_mate = mate(d_qkv)
    d_part, gain_one_sum, row_sum = entry(
        d_q, d_kv_own, w_query, w_key, w_value, full, ssx, gain_one
    )
    qkv_groups = [(a_one_t, a_one_mate, [(d_qkv[None], d_qkv_mate[None], 0)])]
    (sum_qkv,) = both_halves(qkv_groups, (d_qkv.shape[1] // FT,), "qkv", deps=(sum3,))
    sum3, all2 = lax.optimization_barrier((sum3, all2))
    all3 = over_blk(sum3)
    d_send = lax.dynamic_index_in_dim(d_part, 1 - h, 0, keepdims=False)
    d_send, row_sum, gain_one_sum, CHAIN[0] = lax.optimization_barrier(
        (d_send, row_sum, gain_one_sum, CHAIN[0])
    )
    d_other = swap(d_send, "head", 1)
    row_total = row_sum + swap(row_sum, "head", 1)
    sum_qkv = lax.psum_scatter(sum_qkv, "blk", scatter_dimension=0, tiled=True)
    grad_down, grad_gate, grad_up = finish([all0, all1, all2, all3], nblk)
    sum_out, sum_qkv = sum_out.astype(F32), sum_qkv.astype(F32)
    qw, kvw = w_query.shape[1], w_key.shape[1]

    inv_one = lax.rsqrt(ssx[:, :1] * (1.0 / d) + EPS)
    d_one = lax.dynamic_index_in_dim(d_part, h, 0, keepdims=False).astype(F32) + d_other.astype(F32)
    norm_half = x_own.astype(F32) * inv_one
    grad_input = by_head(tie(dh_one, d_other)) + inv_one * (
        d_one * by_head(gain_one) - norm_half * (row_total[:, :1] * (1.0 / d))
    )

    per_head = 1.0 / heads
    tail = jnp.stack(
        [
            jnp.sum(valid) * per_head,
            jnp.sum(valid * ssx[:, 0]) * per_head,
            jnp.sum(valid * ssa[:, 0]) * per_head,
            jnp.sum(valid[:, None] * mlp_half * mlp_half),
        ]
    )
    small = jnp.concatenate(
        [gain_one_sum[0], gain_two_sum[0] * per_head, tail, jnp.zeros((PAIR - 4,), F32)]
    ).reshape(-1, PAIR)
    for axis in ("head", "dp", "blk"):
        for i in range(lax.axis_size(axis).bit_length() - 1):
            small = small + swap(small, axis, 1 << i)
    small = small.reshape(-1)
    at = (dp * nblk + blk) * (d // (ndp * nblk))
    size = d // (ndp * nblk)
    grad_attn_gain = lax.dynamic_slice_in_dim(small, at, size, 0)
    grad_mlp_gain = lax.dynamic_slice_in_dim(small, d + at, size, 0)
    sums4 = small[2 * d : 2 * d + 4]
    stats = jnp.sqrt(sums4[1:] / (sums4[0] * d))

    return (
        output,
        unflat(grad_input),
        grad_attn_gain,
        sum_qkv[:, :qw],
        sum_qkv[:, qw : qw + kvw],
        sum_qkv[:, qw + kvw :],
        sum_out,
        grad_mlp_gain,
        grad_gate,
        grad_up,
        grad_down,
        stats,
    )


def solution(mesh):
    tokens = P("blk", "dp", "head")
    split = P(None, "head")
    in_specs = (tokens, tokens, P("dp", None), P()) + (split,) * 4 + (P(),) + (split,) * 3
    vec, mat = P(("dp", "blk")), P(("dp", "blk"), "head")
    out_specs = (tokens, tokens, vec, mat, mat, mat, mat, vec, mat, mat, mat, P())
    return jax.shard_map(body, mesh=mesh, in_specs=in_specs, out_specs=out_specs, check_vma=False)
```

```python
import functools

import jax
import jax.numpy as jnp
from jax import lax
from jax.experimental import pallas as pl
from jax.experimental.pallas import tpu as pltpu
from jax.sharding import PartitionSpec as P

HD = 64
PAIR = 2 * HD
DOCS = 8
EPS = 1e-05
THETA = 10000.0
NEG = -1e30
F32 = jnp.float32
BF16 = jnp.bfloat16
FT = 256


EARLY, LATE = 0.4, 0.4
WEIGHT = [EARLY]


def params(mib, collective=None):
    if collective is None:
        return pltpu.CompilerParams(vmem_limit_bytes=mib << 20)
    return pltpu.CompilerParams(
        vmem_limit_bytes=mib << 20, collective_id=collective, has_side_effects=True
    )


def cost(flops, byte_count, trans=0):
    return pl.CostEstimate(
        flops=int(flops * WEIGHT[0]),
        bytes_accessed=int(byte_count * WEIGHT[0]),
        transcendentals=int(trans * WEIGHT[0]),
    )


CHAIN = []


def in_hbm(x):
    return pltpu.with_memory_space_constraint(x, pltpu.HBM)


def launch(kernel, args, *, grid, in_specs, out_specs, out_shape, mib, estimate, name, scratch=(), prefetch=0, deps=(), pin_in=True, pin_out=True, collective=None):
    extra = list(CHAIN) + list(deps)
    n_in, n_out = len(args), len(out_shape)

    def wrapped(*refs):
        rest = refs[n_in + len(extra) :]
        kernel(*refs[:n_in], *rest[:n_out], *rest[n_out + 1 :])

    if pin_in:
        args = tuple(args[:prefetch]) + tuple(in_hbm(x) for x in args[prefetch:])
    if pin_out:
        out_shape = [pltpu.HBM(o.shape, o.dtype) for o in out_shape]
    extra = [in_hbm(x) for x in extra]
    *outs, token = pl.pallas_call(
        wrapped,
        grid_spec=pltpu.PrefetchScalarGridSpec(
            num_scalar_prefetch=prefetch,
            grid=grid,
            in_specs=list(in_specs) + [pl.BlockSpec(memory_space=pltpu.HBM)] * len(extra),
            out_specs=list(out_specs) + [pl.BlockSpec(memory_space=pltpu.HBM)],
            scratch_shapes=list(scratch),
        ),
        out_shape=list(out_shape) + [pltpu.HBM((8, 128), F32)],
        compiler_params=params(mib, collective),
        cost_estimate=estimate,
        name=name,
    )(*args, *extra)
    CHAIN[:] = [token]
    return outs


def dot(a, b):
    return jnp.dot(a, b, preferred_element_type=F32)


def dot_nt(a, b):
    return lax.dot_general(a, b, (((1,), (1,)), ((), ())), preferred_element_type=F32)


def dot_tn(a, b):
    return lax.dot_general(a, b, (((0,), (0,)), ((), ())), preferred_element_type=F32)


def swap(x, axis, bit):
    n = lax.axis_size(axis)
    return lax.ppermute(x, axis, [(i, i ^ bit) for i in range(n)])


def lanes(shape):
    return lax.broadcasted_iota(jnp.int32, shape, len(shape) - 1)


def turn(x, cos, sin):
    out = []
    for c in range(x.shape[1] // PAIR):
        v = x[:, c * PAIR : (c + 1) * PAIR]
        low = lanes(v.shape) % HD < HD // 2
        other = jnp.where(low, pltpu.roll(v, PAIR - HD // 2, 1), pltpu.roll(v, HD // 2, 1))
        out.append(v * cos + other * sin)
    return out[0] if len(out) == 1 else jnp.concatenate(out, axis=1)


def project_kernel(h_ref, own, oth, gain, wq, wk, wv, cos, sin, full, a1, q, kv, ssx):
    first = h_ref[0] == 0
    x_own = own[...].astype(F32)
    x_oth = oth[...].astype(F32)
    x = jnp.concatenate(
        [jnp.where(first, x_own, x_oth), jnp.where(first, x_oth, x_own)], axis=1
    )
    width = x.shape[1]
    total = jnp.sum(x * x, axis=1, keepdims=True)
    inv = lax.rsqrt(total * (1.0 / width) + EPS)
    act = (x * inv * gain[...]).astype(BF16)
    full[...] = x.astype(BF16)
    a1[...] = act
    ssx[...] = jnp.broadcast_to(total, ssx.shape)
    q[...] = turn(dot(act, wq[...]), cos[...], sin[...]).astype(BF16) * (HD**-0.5)
    kvw = wk.shape[1]
    kv[:, :kvw] = turn(dot(act, wk[...]), cos[...], sin[...]).astype(BF16)
    kv[:, kvw:] = dot(act, wv[...]).astype(BF16)


def project(h, own, oth, gain, wq, wk, wv, cos, sin):
    n, half = own.shape
    d = 2 * half
    tt = min(n, 256)
    qw, kvw = wq.shape[1], wk.shape[1]
    row = lambda w: pl.BlockSpec((tt, w), lambda i, *_: (i, 0))
    const = lambda a: pl.BlockSpec(a.shape, lambda i, *_: (0, 0), pipeline_mode=pl.Buffered(1))
    return launch(
        project_kernel,
        (h, own, oth, gain, wq, wk, wv, cos, sin),
        prefetch=1,
        grid=(n // tt,),
        in_specs=[row(half), row(half), const(gain), const(wq), const(wk), const(wv)]
        + [row(PAIR), row(PAIR)],
        out_specs=[row(d), row(d), row(qw), row(2 * kvw), row(PAIR)],
        out_shape=[
            jax.ShapeDtypeStruct((n, d), BF16),
            jax.ShapeDtypeStruct((n, d), BF16),
            jax.ShapeDtypeStruct((n, qw), BF16),
            jax.ShapeDtypeStruct((n, 2 * kvw), BF16),
            jax.ShapeDtypeStruct((n, PAIR), F32),
        ],
        mib=32,
        pin_in=False,
        estimate=cost(2 * n * d * (qw + 2 * kvw), 2 * d * (qw + 2 * kvw) + 12 * n * d),
        name="project",
    )


def place(kv, kvh, base):
    x = kv[:, base : base + PAIR].astype(F32)
    x = jnp.where(kvh == 0, x, pltpu.roll(x, HD, 1))
    low = jnp.where(lanes(x.shape) < HD, x, 0.0)
    return low.astype(BF16), pltpu.roll(low, HD, 1).astype(BF16)


def flip_head(kv, kvh, base):
    x = kv[:, base : base + PAIR].astype(F32).T
    return jnp.where(kvh == 0, x[:HD, :], x[HD:, :])


def attend_kernel(step, last, ppk, sc, q_ref, kv_ref, start_ref, *refs):
    refs = list(refs)
    if step:
        acc_in, ml_in = refs[:2]
        refs = refs[2:]
    acc_out, ml_out = refs
    t = q_ref.shape[0]
    kvh = pl.program_id(1)
    blk = sc[0]

    def finish(pair, par, acc, m, l):
        rows = slice(pair * PAIR + par * HD, pair * PAIR + (par + 1) * HD)
        if last:
            acc = acc / l
            m = m + jnp.log(l)
        acc_out[rows, :] = acc
        ml_out[pair, par : par + 1, :] = m
        ml_out[pair, 2 + par : 3 + par, :] = l

    heads = [(pair, par) for pair in range(ppk) for par in range(2)]

    def work():
        u = lax.broadcasted_iota(jnp.int32, (t, t), 0) + (blk - step) * t
        keep = u >= start_ref[0]
        if step == 0:
            keep = keep & (u <= lanes((t, t)) + blk * t)
        bias = jnp.where(keep, 0.0, NEG)
        kv = kv_ref[...]
        kk = place(kv, kvh, 0)
        ones = jnp.where(lax.broadcasted_iota(jnp.int32, (16, t), 0) == 0, 1.0, 0.0)
        vt = jnp.concatenate([flip_head(kv, kvh, PAIR), ones], axis=0).astype(BF16)
        scores = [
            dot_nt(kk[par], q_ref[:, pair * PAIR : (pair + 1) * PAIR]) + bias
            for pair, par in heads
        ]
        for (pair, par), s in zip(heads, scores, strict=True):
            m = jnp.max(s, axis=0, keepdims=True)
            if step:
                old = ml_in[pair, par : par + 1, :]
                m = jnp.maximum(m, old)
            pv = dot(vt, jnp.exp(s - m).astype(BF16))
            acc, l = pv[:HD], pv[HD : HD + 1]
            if step:
                factor = jnp.exp(old - m)
                rows = slice(pair * PAIR + par * HD, pair * PAIR + (par + 1) * HD)
                acc = acc + acc_in[rows, :] * factor
                l = l + ml_in[pair, 2 + par : 3 + par, :] * factor
            finish(pair, par, acc, m, l)

    if step == 0:
        work()
    else:
        pl.when(blk >= step)(work)

        @pl.when(blk < step)
        def _():
            for pair, par in heads:
                rows = slice(pair * PAIR + par * HD, pair * PAIR + (par + 1) * HD)
                m = ml_in[pair, par : par + 1, :]
                finish(pair, par, acc_in[rows, :], m, ml_in[pair, 2 + par : 3 + par, :])


def attend(step, last, sc, q, kv, start, state, rows, deps=()):
    n, qw = q.shape
    t = n // rows
    pairs = qw // PAIR
    kv_heads = kv.shape[1] // 2 // HD
    ppk = pairs // kv_heads
    accspec = pl.BlockSpec((ppk * PAIR, t), lambda r, k, *_: (k, r))
    mlspec = pl.BlockSpec((ppk, 8, t), lambda r, k, *_: (k, 0, r))
    work = n * t * qw
    return launch(
        functools.partial(attend_kernel, step, last, ppk),
        (sc, in_hbm(q), in_hbm(kv), in_hbm(start), *state),
        prefetch=1,
        grid=(rows, kv_heads),
        in_specs=[
            pl.BlockSpec((t, ppk * PAIR), lambda r, k, *_: (r, k)),
            pl.BlockSpec((t, kv.shape[1]), lambda r, k, *_: (r, 0)),
            pl.BlockSpec((1, 1, t), lambda r, k, *_: (r, 0, 0)),
        ]
        + ([accspec, mlspec] if state else []),
        out_specs=[accspec, mlspec],
        out_shape=[
            jax.ShapeDtypeStruct((qw, n), F32),
            jax.ShapeDtypeStruct((pairs, 8, n), F32),
        ],
        mib=28,
        estimate=cost(24 * work, 20 * n * qw, n * t * qw // HD),
        name=f"attend{step}",
        deps=deps,
        pin_in=False,
        pin_out=False,
    )


def flip_kernel(x, out):
    out[...] = x[...].T.astype(BF16)


def flip(x, name="flip"):
    w, n = x.shape
    by_rows = w > n
    step = 512 if max(w, n) % 512 == 0 else max(w, n)
    across = pl.BlockSpec((step, n) if by_rows else (w, step), lambda i: (i, 0) if by_rows else (0, i))
    down = pl.BlockSpec((n, step) if by_rows else (step, w), lambda i: (0, i) if by_rows else (i, 0))
    return launch(
        flip_kernel,
        (x,),
        grid=(max(w, n) // step,),
        in_specs=[across],
        out_specs=[down],
        out_shape=[jax.ShapeDtypeStruct((n, w), BF16)],
        mib=32,
        estimate=cost(8 * n * w, 6 * n * w),
        name=name,
        pin_in=False,
    )[0]


def attend_back_kernel(step, first, last, ppk, sc, q_ref, do_ref, ml_ref, start_ref, kv_ref, *refs):
    refs = list(refs)
    o_ref = refs.pop(0) if first else None
    dq_in, delta_in = (None, None) if first else (refs.pop(0), refs.pop(0))
    cos, sin = (refs.pop(0), refs.pop(0)) if last else (None, None)
    dq_out, dkv_out = refs.pop(0), refs.pop(0)
    delta_out = refs.pop(0) if first else None
    dk_acc, dv_acc, dq_acc = refs
    t = q_ref.shape[0]
    kvh = pl.program_id(1)
    blk = sc[0]
    heads = [(pair, par) for pair in range(ppk) for par in range(2)]

    if first:
        for pair in range(ppk):
            both = slice(pair * PAIR, (pair + 1) * PAIR)
            prod = (do_ref[:, both].astype(F32) * o_ref[:, both].astype(F32)).T
            for par in range(2):
                delta_out[pair, par : par + 1, :] = jnp.sum(
                    prod[par * HD : (par + 1) * HD, :], axis=0, keepdims=True
                )
        dq_acc[...] = jnp.zeros_like(dq_acc)
    else:
        dq_acc[...] = dq_in[...]
    delta = delta_out if first else delta_in

    @pl.when(kvh == 0)
    def _():
        dkv_out[...] = jnp.zeros_like(dkv_out)

    def work():
        u = lax.broadcasted_iota(jnp.int32, (t, t), 0) + (blk - step) * t
        keep = u >= start_ref[0]
        if step == 0:
            keep = keep & (u <= lanes((t, t)) + blk * t)
        bias = jnp.where(keep, 0.0, NEG)
        kv = kv_ref[...]
        kk = place(kv, kvh, 0)
        vv = place(kv, kvh, PAIR)
        kt = flip_head(kv, kvh, 0).astype(BF16)
        dk_acc[...] = jnp.zeros_like(dk_acc)
        dv_acc[...] = jnp.zeros_like(dv_acc)
        for pair, par in heads:
            q = q_ref[:, pair * PAIR : (pair + 1) * PAIR]
            do = do_ref[:, pair * PAIR : (pair + 1) * PAIR]
            st = dot_nt(kk[par], q) + bias
            dp = dot_nt(vv[par], do)
            pt = jnp.exp(st - ml_ref[pair, par : par + 1, :])
            ds = (pt * (dp - delta[pair, par : par + 1, :])).astype(BF16)
            dv_acc[par] += dot(pt.astype(BF16), do)
            dk_acc[par] += dot(ds, q)
            rows = slice(pair * PAIR + par * HD, pair * PAIR + (par + 1) * HD)
            dq_acc[rows, :] += dot(kt, ds)
        low = lanes((t, PAIR)) < HD
        for acc, base in ((dk_acc, 0), (dv_acc, PAIR)):
            both = acc[0] + pltpu.roll(acc[1], HD, 1)
            here = jnp.where(kvh == 0, both, pltpu.roll(both, HD, 1))
            mine = low == (kvh == 0)
            old = dkv_out[:, base : base + PAIR].astype(F32)
            dkv_out[:, base : base + PAIR] = jnp.where(mine, here, old).astype(BF16)

    if step == 0:
        work()
    else:
        pl.when(blk >= step)(work)

    if last:
        for pair in range(ppk):
            rows = slice(pair * PAIR, (pair + 1) * PAIR)
            dq = (dq_acc[rows, :] * (HD**-0.5)).T
            dq_out[:, rows] = turn(dq, cos[...], -sin[...]).astype(BF16)
    else:
        dq_out[...] = dq_acc[...]


def attend_back(step, first, last, sc, q, do, o, ml, start, cos, sin, kv, state, rows, deps=()):
    n, qw = q.shape
    t = n // rows
    pairs = qw // PAIR
    kvw = kv.shape[1]
    kv_heads = kvw // 2 // HD
    ppk = pairs // kv_heads
    width = ppk * PAIR
    pairspec = pl.BlockSpec((t, width), lambda r, k, *_: (r, k))
    accspec = pl.BlockSpec((width, t), lambda r, k, *_: (k, r))
    mlspec = pl.BlockSpec((ppk, 8, t), lambda r, k, *_: (k, 0, r))
    rowspec = lambda w: pl.BlockSpec((t, w), lambda r, k, *_: (r, 0))
    work = n * t * qw
    return launch(
        functools.partial(attend_back_kernel, step, first, last, ppk),
        (sc, q, do, ml, start, kv)
        + ((o,) if first else tuple(state))
        + ((cos, sin) if last else ()),
        prefetch=1,
        grid=(rows, kv_heads),
        in_specs=[pairspec, pairspec, mlspec]
        + [pl.BlockSpec((1, 1, t), lambda r, k, *_: (r, 0, 0))]
        + [rowspec(kvw)]
        + ([pairspec] if first else [accspec, mlspec])
        + ([rowspec(PAIR)] * 2 if last else []),
        out_specs=[pairspec if last else accspec, rowspec(kvw)] + ([mlspec] if first else []),
        scratch=[
            pltpu.VMEM((2, t, PAIR), F32),
            pltpu.VMEM((2, t, PAIR), F32),
            pltpu.VMEM((width, t), F32),
        ],
        out_shape=[
            jax.ShapeDtypeStruct((n, qw), BF16) if last else jax.ShapeDtypeStruct((qw, n), F32),
            jax.ShapeDtypeStruct((n, kvw), BF16),
        ]
        + ([jax.ShapeDtypeStruct((pairs, 8, n), F32)] if first else []),
        mib=40,
        estimate=cost(54 * work, 20 * n * qw, work // HD),
        name=f"attend_back{step}",
        deps=deps,
    )


def gather_dkv_kernel(count, *refs):
    parts = refs[:count]
    cos, sin, out = refs[count:]
    total = parts[0][...].astype(F32)
    for x in parts[1:]:
        total = total + x[...].astype(F32)
    half = total.shape[1] // 2
    out[:, :half] = turn(total[:, :half], cos[...], -sin[...]).astype(BF16)
    out[:, half:] = total[:, half:].astype(BF16)


def gather_dkv(parts, cos, sin, deps=()):
    whole = lambda x: pl.BlockSpec(x.shape, lambda i: (0, 0))
    return launch(
        functools.partial(gather_dkv_kernel, len(parts)),
        (*parts, cos, sin),
        grid=(1,),
        in_specs=[whole(x) for x in (*parts, cos, sin)],
        out_specs=[whole(parts[0])],
        out_shape=[jax.ShapeDtypeStruct(parts[0].shape, BF16)],
        mib=32,
        estimate=cost(10 * parts[0].size, 4 * len(parts) * parts[0].size),
        name="gather_dkv",
        deps=deps,
    )[0]


def merge_kernel(o_own, o_oth, w_own, w_oth, full, gain, h1, a2, a2_t, r2, ssa, held, sums):
    i = pl.program_id(0)
    attn = dot_nt(o_own[...], w_own[...]) + dot_nt(o_oth[...], w_oth[...])
    x = full[...].astype(F32) + attn
    h1[0] = x
    held[i] = x

    @pl.when(i == 0)
    def _():
        sums[...] = jnp.zeros_like(sums)
        ssa[...] = jnp.zeros_like(ssa)

    sums[...] += jnp.sum(x * x, axis=1, keepdims=True)
    ssa[...] += jnp.sum(attn * attn, axis=1, keepdims=True)

    @pl.when(i == pl.num_programs(0) - 1)
    def _():
        count, _, dt = held.shape
        inv = lax.rsqrt(sums[...] * (1.0 / (count * dt)) + EPS)
        r2[...] = inv
        for j in range(count):
            at = slice(j * dt, (j + 1) * dt)
            act = (held[j] * inv[:, :1] * gain[:, at]).astype(BF16)
            a2[:, at] = act
            a2_t[at, :] = act.T


def merge(o_own, o_oth, w_own, w_oth, full, gain, deps=()):
    n, d = full.shape
    dt = 512
    e = o_own.shape[1]
    const = lambda a: pl.BlockSpec(a.shape, lambda i: (0, 0), pipeline_mode=pl.Buffered(1))
    return launch(
        merge_kernel,
        (o_own, o_oth, w_own, w_oth, full, gain),
        grid=(d // dt,),
        in_specs=[
            const(o_own),
            const(o_oth),
            pl.BlockSpec((dt, e), lambda i: (i, 0)),
            pl.BlockSpec((dt, e), lambda i: (i, 0)),
            pl.BlockSpec((n, dt), lambda i: (0, i)),
            const(gain),
        ],
        out_specs=[
            pl.BlockSpec((1, n, dt), lambda i: (i, 0, 0)),
            pl.BlockSpec((n, d), lambda i: (0, 0)),
            pl.BlockSpec((d, n), lambda i: (0, 0)),
            pl.BlockSpec((n, PAIR), lambda i: (0, 0)),
            pl.BlockSpec((n, PAIR), lambda i: (0, 0)),
        ],
        out_shape=[
            jax.ShapeDtypeStruct((d // dt, n, dt), F32),
            jax.ShapeDtypeStruct((n, d), BF16),
            jax.ShapeDtypeStruct((d, n), BF16),
            jax.ShapeDtypeStruct((n, PAIR), F32),
            jax.ShapeDtypeStruct((n, PAIR), F32),
        ],
        scratch=[pltpu.VMEM((d // dt, n, dt), F32), pltpu.VMEM((n, PAIR), F32)],
        mib=48,
        estimate=cost(3 * n * d * d, 2 * d * d + 12 * n * d),
        name="merge",
        deps=deps,
    )


def units_kernel(a2, g, wg, wu, wd, out):
    gate = dot(a2[...], wg[...])
    up = dot(a2[...], wu[...])
    dh = dot(g[...], wd[...])
    sig = jax.nn.sigmoid(gate)
    act = gate * sig
    out[0] = (act * up).astype(BF16)
    out[1] = (dh * up * sig * (1.0 + gate * (1.0 - sig))).astype(BF16)
    out[2] = (dh * act).astype(BF16)


def units(a2, g, wg, wu, wd, first, count, deps=()):
    n, d = a2.shape
    const = pl.BlockSpec((n, d), lambda i: (0, 0), pipeline_mode=pl.Buffered(1))
    wspec = pl.BlockSpec((d, FT), lambda i: (0, first + i))
    return launch(
        units_kernel,
        (a2, g, wg, wu, wd),
        grid=(count,),
        in_specs=[const, const, wspec, wspec, wspec],
        out_specs=[pl.BlockSpec((3, n, FT), lambda i: (0, 0, i))],
        out_shape=[jax.ShapeDtypeStruct((3, n, count * FT), BF16)],
        mib=58,
        estimate=cost(10 * n * d * FT * count, 6 * d * FT * count, n * FT * count),
        name=f"units{first}",
        deps=deps,
    )[0]


def exchange_kernel(count, tiles, nblk, *refs):
    acts = refs[: 3 * count]
    wg, wu, wd, early, total, branch, shares = refs[3 * count : 3 * count + 7]
    mine, theirs, send_sem, recv_sem, z_send, z_recv, own_sem = refs[3 * count + 7 :]
    i = pl.program_id(0)
    other = 1 - lax.axis_index("head")
    blk = lax.axis_index("blk")
    rows = early.shape[0] // nblk

    def copy(j):
        return pltpu.make_async_remote_copy(
            src_ref=mine.at[j],
            dst_ref=theirs.at[j],
            send_sem=send_sem.at[j],
            recv_sem=recv_sem.at[j],
            device_id={"head": other},
            device_id_type=pl.DeviceIdType.MESH,
        )

    def block(b):
        return early.at[pl.ds(pl.multiple_of(b * rows, rows), rows), :]

    def share(k):
        to = lax.rem(blk + k, nblk)
        return pltpu.make_async_remote_copy(
            src_ref=block(to),
            dst_ref=shares.at[blk],
            send_sem=z_send.at[k],
            recv_sem=z_recv.at[k],
            device_id={"blk": to},
            device_id_type=pl.DeviceIdType.MESH,
        )

    def keep():
        return pltpu.make_async_copy(block(blk), shares.at[blk], own_sem)

    def product(m, weight):
        out, at = None, 0
        for act in acts[m * count : (m + 1) * count]:
            term = dot_nt(act[0], weight[:, at : at + act.shape[2]])
            out = term if out is None else out + term
            at += act.shape[2]
        return out

    @pl.when(i == 0)
    def _():
        barrier = pltpu.get_barrier_semaphore()
        pl.semaphore_signal(
            barrier, inc=1, device_id={"head": other}, device_id_type=pl.DeviceIdType.MESH
        )
        for k in range(1, nblk):
            pl.semaphore_signal(
                barrier,
                inc=1,
                device_id={"blk": lax.rem(blk + k, nblk)},
                device_id_type=pl.DeviceIdType.MESH,
            )
        pl.semaphore_wait(barrier, nblk)
        for k in range(1, nblk):
            share(k).start()
        keep().start()

    @pl.when(i < tiles)
    def _():
        mine[i] = (product(1, wg) + product(2, wu)).astype(BF16)
        copy(i).start()

    @pl.when(i >= tiles)
    def _():
        branch[0] = product(0, wd).astype(BF16)

    @pl.when(i == 2 * tiles - 1)
    def _():
        width = mine.shape[2]
        for j in range(tiles):
            copy(j).wait()
            total[:, j * width : (j + 1) * width] = mine[j].astype(F32) + theirs[j].astype(F32)
        for k in range(1, nblk):
            share(k).wait()
        keep().wait()


def exchange(stacks, wg, wu, wd, early, nblk, name):
    n = stacks[0].shape[1]
    d, ff = wg.shape
    dt = 256
    tiles = d // dt
    per = tiles // 2
    acts = [x for _ in range(3) for x in stacks]
    specs = [
        pl.BlockSpec((1,) + x.shape[1:], lambda i, m=m: (m, 0, 0), pipeline_mode=pl.Buffered(1))
        for m in range(3)
        for x in stacks
    ]
    first = pl.BlockSpec((dt, ff), lambda i: (jnp.minimum(i, tiles - 1), 0))
    second = pl.BlockSpec((dt, ff), lambda i: (jnp.maximum(i - tiles, 0), 0))
    place_hbm = pl.BlockSpec(memory_space=pltpu.HBM)

    def branch_at(i):
        j = jnp.maximum(i - tiles, 0)
        return (j // per, 0, j % per)

    return launch(
        functools.partial(exchange_kernel, len(stacks), tiles, nblk),
        (*acts, wg, wu, wd, early),
        grid=(2 * tiles,),
        in_specs=specs + [first, first, second, place_hbm],
        out_specs=[
            pl.BlockSpec((n, d), lambda i: (0, 0)),
            pl.BlockSpec((1, n, dt), branch_at),
            place_hbm,
        ],
        out_shape=[
            jax.ShapeDtypeStruct((n, d), F32),
            jax.ShapeDtypeStruct((2, n, d // 2), BF16),
            jax.ShapeDtypeStruct((nblk, early.shape[0] // nblk, early.shape[1]), BF16),
        ],
        scratch=[
            pltpu.VMEM((tiles, n, dt), BF16),
            pltpu.VMEM((tiles, n, dt), BF16),
            pltpu.SemaphoreType.DMA((tiles,)),
            pltpu.SemaphoreType.DMA((tiles,)),
            pltpu.SemaphoreType.DMA((nblk,)),
            pltpu.SemaphoreType.DMA((nblk,)),
            pltpu.SemaphoreType.DMA,
        ],
        mib=58,
        estimate=cost(6 * n * d * ff, 6 * d * ff),
        name=name,
        collective=1,
    )


def stream_kernel(da_sum, h1, r2, gain, g, w_out, dh1, dattn_t, dout, gsum):
    da = da_sum[...]
    inv = r2[:, :1]
    norm = jnp.concatenate([h1[j] for j in range(h1.shape[0])], axis=1) * inv
    grad = da * norm

    @pl.when(pl.program_id(0) == 0)
    def _():
        gsum[...] = jnp.zeros_like(gsum)

    gsum[...] += jnp.sum(grad, axis=0, keepdims=True)
    e2 = da * gain[...]
    mean = jnp.sum(e2 * norm, axis=1, keepdims=True) * (1.0 / da.shape[1])
    dh = g[...].astype(F32) + inv * (e2 - norm * mean)
    dh1[...] = dh
    low = dh.astype(BF16)
    dattn_t[...] = low.T
    dout[...] = dot(low, w_out[...]).astype(BF16)


def stream(da, h1, r2, gain, g, w_out, deps=()):
    parts, n, dt = h1.shape
    d = parts * dt
    tt = min(n, 128)
    ew = w_out.shape[1]
    row = lambda w: pl.BlockSpec((tt, w), lambda i: (i, 0))
    const = lambda a: pl.BlockSpec(a.shape, lambda i: (0, 0), pipeline_mode=pl.Buffered(1))
    return launch(
        stream_kernel,
        (da, h1, r2, gain, g, w_out),
        grid=(n // tt,),
        in_specs=[
            row(d),
            pl.BlockSpec((parts, tt, dt), lambda i: (0, i, 0)),
            row(PAIR),
            const(gain),
            row(d),
            const(w_out),
        ],
        out_specs=[
            row(d),
            pl.BlockSpec((d, tt), lambda i: (0, i)),
            row(ew),
            pl.BlockSpec((1, d), lambda i: (0, 0)),
        ],
        out_shape=[
            jax.ShapeDtypeStruct((n, d), F32),
            jax.ShapeDtypeStruct((d, n), BF16),
            jax.ShapeDtypeStruct((n, ew), BF16),
            jax.ShapeDtypeStruct((1, d), F32),
        ],
        mib=56,
        estimate=cost(2 * n * d * ew, 2 * d * ew + 20 * n * d),
        name="stream",
        deps=deps,
    )


def entry_kernel(dq, dkv, wq, wk, wv, full, ssx, gain, part, gsum, rsum):
    kvw = wk.shape[1]
    da = dot_nt(dq[...], wq[...])
    da = da + dot_nt(dkv[:, :kvw], wk[...]) + dot_nt(dkv[:, kvw:], wv[...])
    width = pl.num_programs(0) * da.shape[1]
    inv = lax.rsqrt(ssx[:, :1] * (1.0 / width) + EPS)
    grad = da * (full[...].astype(F32) * inv)
    gsum[...] = jnp.sum(grad, axis=0, keepdims=True)

    @pl.when(pl.program_id(0) == 0)
    def _():
        rsum[...] = jnp.zeros_like(rsum)

    rsum[...] += jnp.sum(grad * gain[...], axis=1, keepdims=True)
    part[0] = da.astype(BF16)


def entry(dq, dkv, wq, wk, wv, full, ssx, gain):
    n, d = full.shape
    dt = 256
    per = d // 2 // dt
    const = lambda a: pl.BlockSpec(a.shape, lambda i: (0, 0), pipeline_mode=pl.Buffered(1))
    wspec = lambda w: pl.BlockSpec((dt, w.shape[1]), lambda i: (i, 0))
    return launch(
        entry_kernel,
        (dq, dkv, wq, wk, wv, full, ssx, gain),
        grid=(d // dt,),
        in_specs=[const(dq), const(dkv), wspec(wq), wspec(wk), wspec(wv)]
        + [
            pl.BlockSpec((n, dt), lambda i: (0, i)),
            const(ssx),
            pl.BlockSpec((1, dt), lambda i: (0, i)),
        ],
        out_specs=[
            pl.BlockSpec((1, n, dt), lambda i: (i // per, 0, i % per)),
            pl.BlockSpec((1, dt), lambda i: (0, i)),
            pl.BlockSpec((n, PAIR), lambda i: (0, 0)),
        ],
        out_shape=[
            jax.ShapeDtypeStruct((2, n, d // 2), BF16),
            jax.ShapeDtypeStruct((1, d), F32),
            jax.ShapeDtypeStruct((n, PAIR), F32),
        ],
        mib=56,
        estimate=cost(2 * n * d * (wq.shape[1] + 2 * wk.shape[1]), 20 * n * d),
        name="entry",
    )


def outer_kernel(shares, count, parts, adds, spread, sc, *refs):
    k = 0
    lefts, rights = [], []
    for share in shares:
        lefts.append((refs[k : k + count], refs[k + count : k + 2 * count]))
        k += 2 * count
        rights.append([(refs[k + 2 * i], refs[k + 2 * i + 1]) for i in range(share)])
        k += 2 * share
    got = refs[k] if adds else None
    outs = refs[k + adds :]

    def work(out):
        m = 0
        for (left_own, left_oth), group in zip(lefts, rights, strict=True):
            rows = left_own[0].shape[0]
            for own, oth in group:
                at = slice(m * FT, (m + 1) * FT)
                for i in range(count):
                    part = slice(i * rows, (i + 1) * rows)
                    total = dot(left_own[i][...], own[0]) + dot(left_oth[i][...], oth[0])
                    if adds:
                        total = total + got[part, at].astype(F32)
                    if spread == 1:
                        out[part, at] = total.astype(BF16)
                    else:
                        size = rows // spread
                        for b in range(spread):
                            to = slice((b * count + i) * size, (b * count + i + 1) * size)
                            out[to, at] = total[b * size : (b + 1) * size, :].astype(BF16)
                m += 1

    if len(parts) == 1:
        work(outs[0])
        return
    step = pl.program_id(0)
    start = 0
    for out, size in zip(outs, parts, strict=True):
        pl.when((step >= start) & (step < start + size))(functools.partial(work, out))
        start += size


def outer(sc, groups, rows, first, parts, name, got=None, deps=(), spread=1):
    n = groups[0][0].shape[1]
    count = sc.shape[0]
    number = sum(parts)
    shares = tuple(len(g[2]) for g in groups)
    ins, specs = [], []
    for own, oth, rights in groups:
        ins += [own] * count + [oth] * count
        for i in range(count):
            specs.append(pl.BlockSpec((rows, n), lambda j, s, i=i: (s[i], 0)))
        specs += specs[-count:]
        for r_own, r_oth, at in rights:
            ins += [r_own, r_oth]
            specs += [pl.BlockSpec((1, n, FT), lambda i, s, at=at: (at, 0, first + i))] * 2
    members = sum(shares)
    height = count * rows
    ospecs, start = [], 0
    for size in parts:
        ospecs.append(
            pl.BlockSpec(
                (height, members * FT),
                lambda i, s, start=start, size=size: (0, jnp.clip(i - start, 0, size - 1)),
            )
        )
        start += size
    if got is not None:
        ins.append(got)
        specs.append(ospecs[0])
    c = number * FT
    return launch(
        functools.partial(outer_kernel, shares, count, tuple(parts), int(got is not None), spread),
        (sc, *ins),
        prefetch=1,
        grid=(number,),
        in_specs=specs,
        out_specs=ospecs,
        out_shape=[jax.ShapeDtypeStruct((height, members * size * FT), BF16) for size in parts],
        mib=48,
        estimate=cost(8 * n * height * c * members, members * c * (4 * n + 2 * height)),
        name=name,
        deps=deps,
    )


def finish_kernel(count, *refs):
    parts = refs[:count]
    outs = refs[count:]
    at = 0
    for part in parts:
        for tile in range(part.shape[2] // (3 * FT)):
            for m in range(3):
                columns = slice((3 * tile + m) * FT, (3 * tile + m + 1) * FT)
                total = part[0, :, columns].astype(F32)
                for b in range(1, part.shape[0]):
                    total = total + part[b, :, columns].astype(F32)
                outs[m][:, at : at + FT] = total
            at += FT


def finish(parts):
    parts = [x.reshape(count, x.shape[0] // count, x.shape[1]) for x, count in parts]
    rows = parts[0].shape[1]
    width = sum(x.shape[2] for x in parts) // 3
    whole = lambda shape: pl.BlockSpec(shape, lambda i: (0,) * len(shape))
    return launch(
        functools.partial(finish_kernel, len(parts)),
        tuple(parts),
        grid=(1,),
        in_specs=[whole(x.shape) for x in parts],
        out_specs=[whole((rows, width))] * 3,
        out_shape=[jax.ShapeDtypeStruct((rows, width), F32)] * 3,
        mib=48,
        estimate=cost(0, 8 * parts[0].shape[0] * rows * width),
        name="finish",
    )


def body(
    inputs,
    cotangent,
    lengths,
    attn_gain,
    w_query,
    w_key,
    w_value,
    w_out,
    mlp_gain,
    gate_weight,
    up_weight,
    down_weight,
):
    t, rows, half = inputs.shape
    n = t * rows
    heads = lax.axis_size("head")
    nblk = lax.axis_size("blk")
    ndp = lax.axis_size("dp")
    d = half * heads
    h = lax.axis_index("head").astype(jnp.int32)
    blk = lax.axis_index("blk").astype(jnp.int32)
    dp = lax.axis_index("dp").astype(jnp.int32)
    sc_h = h.reshape(1)
    sc_blk = blk.reshape(1)

    def flat(x):
        return jnp.transpose(x, (1, 0, 2)).reshape(n, x.shape[2])

    def unflat(x):
        return jnp.transpose(x.reshape(rows, t, x.shape[1]), (1, 0, 2))

    x_own = flat(inputs)
    g_own = flat(cotangent)
    gain_one = attn_gain.astype(F32).reshape(1, d)
    gain_two = mlp_gain.astype(F32).reshape(1, d)

    pos = blk * t + jnp.arange(t, dtype=jnp.int32)
    ends = jnp.cumsum(lengths, axis=1)
    passed = ends[:, None, :] <= pos[None, :, None]
    start = jnp.max(jnp.where(passed, ends[:, None, :], 0), axis=2)
    valid = (jnp.sum(passed.astype(jnp.int32), axis=2) < DOCS).astype(F32).reshape(n)
    start_rows = start.reshape(rows, 1, t)
    freq = jnp.power(THETA, -2.0 * jnp.arange(HD // 2, dtype=F32) / HD)
    angles = pos.astype(F32)[:, None] * freq[None, :]
    cos_h, sin_h = jnp.cos(angles), jnp.sin(angles)
    cos = jnp.tile(jnp.concatenate([cos_h, cos_h, cos_h, cos_h], axis=1), (rows, 1))
    sin = jnp.tile(jnp.concatenate([-sin_h, sin_h, -sin_h, sin_h], axis=1), (rows, 1))

    CHAIN.clear()
    WEIGHT[0] = EARLY

    def tie(x, *also):
        return lax.optimization_barrier((x, *also))[0]

    def by_head(x):
        return jnp.where(h == 0, x[:, :half], x[:, half:])

    def gate(x):
        x, CHAIN[0] = lax.optimization_barrier((x, CHAIN[0]))
        return x

    def mate(x):
        return swap(x, "dp", 1)

    x_oth = swap(x_own, "head", 1)
    share = w_out.shape[0] // ndp
    piece = lax.dynamic_slice_in_dim(w_out, dp * share, share, 0)
    x_oth, piece, g_own, cos, sin, start_rows = lax.optimization_barrier(
        (x_oth, piece, g_own, cos, sin, start_rows)
    )
    piece = swap(piece, "head", 1)
    full, a_one, queries, kv, ssx = project(
        sc_h, x_own, x_oth, gain_one, w_query, w_key, w_value, cos, sin
    )

    kvs, state = [kv], ()
    for s in range(nblk):
        if s + 1 < nblk:
            steps = [(i, i + 1) for i in range(s, nblk - 1)]
            kvs.append(lax.ppermute(kvs[s], "blk", steps))
        state = attend(s, s == nblk - 1, sc_blk, queries, kvs[s], start_rows, state, rows)
        if s + 1 < nblk - 1:
            kvs[s + 1] = gate(kvs[s + 1])
        if s == 0:
            a_one_t = flip(a_one, "flip_a")
            piece = gate(piece)
            w_out_oth = lax.all_gather(piece, "dp", axis=0, tiled=True)
            g_own, piece = lax.optimization_barrier((g_own, piece))
            g_oth = swap(g_own, "head", 1)
    acc, ml = state
    o_own = flip(acc)
    o_oth = swap(o_own, "head", 1)
    g_full = jnp.concatenate(
        [jnp.where(h == 0, g_own, g_oth), jnp.where(h == 0, g_oth, g_own)], axis=1
    )
    g_t = flip(g_full, "flip_g")
    o_mate, g_mate = mate(o_own), mate(g_t)
    h_one, a_two, a_two_t, inv_two, ssa = merge(
        o_own, o_oth, w_out, w_out_oth, full, gain_two
    )
    a_two_mate = mate(a_two_t)

    low_bit = dp & 1
    block_rows = d // ndp
    sc_send = (dp ^ 2).reshape(1)
    sc_keep = dp.reshape(1)
    sc_both = jnp.stack([2 * i + low_bit for i in range(ndp // 2)])
    y_groups = [[0, 2], [1, 3]]

    def both_halves(groups, parts, name, deps=()):
        return [
            lax.psum_scatter(
                x, "dp", scatter_dimension=0, axis_index_groups=y_groups, tiled=True
            )
            for x in outer(sc_both, groups, block_rows, 0, parts, name, deps=deps)
        ]

    def over_blk(x):
        return lax.all_to_all(x, "blk", split_axis=0, concat_axis=0, tiled=True)

    tiles = gate_weight.shape[1] // FT
    size_a = max(1, tiles // 5)
    size_b = (tiles - size_a + 1) // 3
    size_c = tiles - size_a - size_b

    def unit_part(first, count, deps=()):
        x = units(a_two, g_full, gate_weight, up_weight, down_weight, first, count, deps)
        x_mate = mate(x)
        return x, [
            (g_t, g_mate, [(x, x_mate, 0)]),
            (a_two_t, a_two_mate, [(x, x_mate, 1), (x, x_mate, 2)]),
        ]

    part_a, groups_a = unit_part(0, size_a)
    (sum0,) = both_halves(groups_a, (size_a,), "mlp0")
    part_b, groups_b = unit_part(size_a, size_b)
    part_c, groups_c = unit_part(size_a + size_b, size_c)
    (sum1,) = both_halves(groups_b, (size_b,), "mlp1")

    da, branch, all0 = exchange(
        [part_a, part_b, part_c], gate_weight, up_weight, down_weight, sum0, nblk, "exchange"
    )
    WEIGHT[0] = LATE
    sum2, sum3 = both_halves(groups_c, (size_c - size_c // 2, size_c // 2), "mlp2")
    all1 = over_blk(gate(sum1))
    dh_one, d_attn_t, d_out, gain_two_sum = stream(
        da, h_one, inv_two, gain_two, g_full, w_out
    )
    d_attn_mate, a_one_mate = mate(d_attn_t), mate(gate(a_one_t))
    out_groups = [(d_attn_t, d_attn_mate, [(o_own[None], o_mate[None], 0)])]
    out_parts = (o_own.shape[1] // FT,)
    (first_out,) = outer(
        sc_send, out_groups, block_rows, 0, out_parts, "out_send", deps=(a_one_mate,)
    )
    got_out = swap(first_out, "dp", 2)
    to_other = gate(lax.dynamic_index_in_dim(branch, 1 - h, 0, keepdims=False))
    branch_oth = swap(to_other, "head", 1)

    state, parts = (), []
    for s in reversed(range(nblk)):
        out = attend_back(
            s, s == nblk - 1, s == 0, sc_blk, queries, d_out, o_own, ml, start_rows, cos, sin,
            kvs[s], state, rows, deps=(),
        )
        state = (out[0], out[2] if s == nblk - 1 else state[1])
        part = out[1]
        parts.append(
            lax.ppermute(part, "blk", [(i, i - s) for i in range(s, nblk)]) if s else part
        )
        if s == min(1, nblk - 1):
            (keep_out,) = outer(
                sc_keep, out_groups, block_rows, 0, out_parts, "out_keep", got_out,
                deps=(all1,) + tuple(parts[:2]) * (nblk > 2),
            )
    d_q = state[0]
    d_kv_own = gather_dkv(parts, cos, sin, deps=(branch_oth,))
    all2 = over_blk(gate(sum2))
    h_late, d_kv_own = lax.optimization_barrier((h_one, d_kv_own))
    h_half = jnp.concatenate(
        [
            jnp.where(h == 0, h_late[i], h_late[i + h_late.shape[0] // 2])
            for i in range(h_late.shape[0] // 2)
        ],
        axis=1,
    )
    mlp_half = lax.dynamic_index_in_dim(branch, h, 0, keepdims=False).astype(F32) + (
        branch_oth.astype(F32)
    )
    output = unflat((h_half + mlp_half).astype(BF16))
    d_qkv = jnp.concatenate([d_q, d_kv_own], axis=1)
    d_qkv_mate = mate(d_qkv)
    d_part, gain_one_sum, row_sum = entry(
        d_q, d_kv_own, w_query, w_key, w_value, full, ssx, gain_one
    )
    qkv_groups = [(a_one_t, a_one_mate, [(d_qkv[None], d_qkv_mate[None], 0)])]
    qkv_parts = (d_qkv.shape[1] // FT,)
    (first_qkv,) = outer(sc_send, qkv_groups, block_rows, 0, qkv_parts, "qkv_send")
    got_qkv = swap(first_qkv, "dp", 2)
    sum3 = lax.psum_scatter(gate(sum3), "blk", scatter_dimension=0, tiled=True)
    d_send = lax.dynamic_index_in_dim(d_part, 1 - h, 0, keepdims=False)
    d_send, row_sum, gain_one_sum, CHAIN[0] = lax.optimization_barrier(
        (d_send, row_sum, gain_one_sum, CHAIN[0])
    )
    d_other = swap(d_send, "head", 1)
    row_total = row_sum + swap(row_sum, "head", 1)
    (keep_qkv,) = outer(
        sc_keep, qkv_groups, block_rows, 0, qkv_parts, "qkv_keep", got_qkv, deps=(all2,)
    )
    per_head = 1.0 / heads
    tail = jnp.stack(
        [
            jnp.sum(valid) * per_head,
            jnp.sum(valid * ssx[:, 0]) * per_head,
            jnp.sum(valid * ssa[:, 0]) * per_head,
            jnp.sum(valid[:, None] * mlp_half * mlp_half),
        ]
    )
    small = jnp.concatenate(
        [gain_one_sum[0], gain_two_sum[0] * per_head, tail, jnp.zeros((PAIR - 4,), F32)]
    ).reshape(-1, PAIR)
    for axis in ("head", "dp"):
        for i in range(lax.axis_size(axis).bit_length() - 1):
            small = small + swap(small, axis, 1 << i)
    small = small.reshape(-1)
    mine = [
        lax.dynamic_slice_in_dim(small, at + dp * block_rows, block_rows, 0)[:, None]
        for at in (0, d)
    ]
    sums4 = jnp.broadcast_to(small[None, 2 * d : 2 * d + 4], (block_rows, 4))
    exact = jnp.concatenate(mine + [sums4], axis=1)
    coarse = exact.astype(BF16)
    fine = (exact - coarse.astype(F32)).astype(BF16)
    extra = jnp.concatenate(
        [coarse, fine, jnp.zeros((block_rows, PAIR - 12), BF16)], axis=1
    )
    all_qkv = over_blk(jnp.concatenate([keep_qkv, extra, keep_out], axis=1))
    grad_down, grad_gate, grad_up = finish([(all0.reshape(-1, all0.shape[2]), nblk), (all1, nblk), (all2, nblk), (sum3, 1)])
    own_rows = lambda x: jnp.sum(x.reshape(nblk, -1, x.shape[1]).astype(F32), axis=0)
    sum_qkv = own_rows(all_qkv)
    sum_out = sum_qkv[:, sum_qkv.shape[1] - o_own.shape[1] :]
    qw, kvw = w_query.shape[1], w_key.shape[1]

    inv_one = lax.rsqrt(ssx[:, :1] * (1.0 / d) + EPS)
    d_one = lax.dynamic_index_in_dim(d_part, h, 0, keepdims=False).astype(F32) + d_other.astype(F32)
    norm_half = x_own.astype(F32) * inv_one
    grad_input = by_head(tie(dh_one, d_other)) + inv_one * (
        d_one * by_head(gain_one) - norm_half * (row_total[:, :1] * (1.0 / d))
    )

    width = qw + 2 * kvw
    small = sum_qkv[:, width : width + 6] + sum_qkv[:, width + 6 : width + 12]
    grad_attn_gain, grad_mlp_gain = small[:, 0], small[:, 1]
    stats = jnp.sqrt(small[0, 3:6] / (small[0, 2] * d))

    return (
        output,
        unflat(grad_input),
        grad_attn_gain,
        sum_qkv[:, :qw],
        sum_qkv[:, qw : qw + kvw],
        sum_qkv[:, qw + kvw : width],
        sum_out,
        grad_mlp_gain,
        grad_gate,
        grad_up,
        grad_down,
        stats,
    )


def solution(mesh):
    tokens = P("blk", "dp", "head")
    split = P(None, "head")
    in_specs = (tokens, tokens, P("dp", None), P()) + (split,) * 4 + (P(),) + (split,) * 3
    vec, mat = P(("dp", "blk")), P(("dp", "blk"), "head")
    out_specs = (tokens, tokens, vec, mat, mat, mat, mat, vec, mat, mat, mat, P())
    return jax.shard_map(body, mesh=mesh, in_specs=in_specs, out_specs=out_specs, check_vma=False)
```

```python
import functools

import jax
import jax.numpy as jnp
from jax import lax
from jax.experimental import pallas as pl
from jax.experimental.pallas import tpu as pltpu
from jax.sharding import PartitionSpec as P

HD = 64
PAIR = 2 * HD
DOCS = 8
EPS = 1e-05
THETA = 10000.0
NEG = -1e30
F32 = jnp.float32
BF16 = jnp.bfloat16
FT = 256


EARLY, LATE = 0.4, 0.4
WEIGHT = [EARLY]


def params(mib, collective=None):
    if collective is None:
        return pltpu.CompilerParams(vmem_limit_bytes=mib << 20)
    return pltpu.CompilerParams(
        vmem_limit_bytes=mib << 20, collective_id=collective, has_side_effects=True
    )


def cost(flops, byte_count, trans=0):
    return pl.CostEstimate(
        flops=int(flops * WEIGHT[0]),
        bytes_accessed=int(byte_count * WEIGHT[0]),
        transcendentals=int(trans * WEIGHT[0]),
    )


CHAIN = []


def in_hbm(x):
    return pltpu.with_memory_space_constraint(x, pltpu.HBM)


def launch(kernel, args, *, grid, in_specs, out_specs, out_shape, mib, estimate, name, scratch=(), prefetch=0, deps=(), pin_in=True, pin_out=True, collective=None):
    extra = list(CHAIN) + list(deps)
    n_in, n_out = len(args), len(out_shape)

    def wrapped(*refs):
        rest = refs[n_in + len(extra) :]
        kernel(*refs[:n_in], *rest[:n_out], *rest[n_out + 1 :])

    if pin_in:
        args = tuple(args[:prefetch]) + tuple(in_hbm(x) for x in args[prefetch:])
    if pin_out:
        out_shape = [pltpu.HBM(o.shape, o.dtype) for o in out_shape]
    extra = [in_hbm(x) for x in extra]
    *outs, token = pl.pallas_call(
        wrapped,
        grid_spec=pltpu.PrefetchScalarGridSpec(
            num_scalar_prefetch=prefetch,
            grid=grid,
            in_specs=list(in_specs) + [pl.BlockSpec(memory_space=pltpu.HBM)] * len(extra),
            out_specs=list(out_specs) + [pl.BlockSpec(memory_space=pltpu.HBM)],
            scratch_shapes=list(scratch),
        ),
        out_shape=list(out_shape) + [pltpu.HBM((8, 128), F32)],
        compiler_params=params(mib, collective),
        cost_estimate=estimate,
        name=name,
    )(*args, *extra)
    CHAIN[:] = [token]
    return outs


def dot(a, b):
    return jnp.dot(a, b, preferred_element_type=F32)


def dot_nt(a, b):
    return lax.dot_general(a, b, (((1,), (1,)), ((), ())), preferred_element_type=F32)


def dot_tn(a, b):
    return lax.dot_general(a, b, (((0,), (0,)), ((), ())), preferred_element_type=F32)


def swap(x, axis, bit):
    n = lax.axis_size(axis)
    return lax.ppermute(x, axis, [(i, i ^ bit) for i in range(n)])


def lanes(shape):
    return lax.broadcasted_iota(jnp.int32, shape, len(shape) - 1)


def turn(x, cos, sin):
    out = []
    for c in range(x.shape[1] // PAIR):
        v = x[:, c * PAIR : (c + 1) * PAIR]
        low = lanes(v.shape) % HD < HD // 2
        other = jnp.where(low, pltpu.roll(v, PAIR - HD // 2, 1), pltpu.roll(v, HD // 2, 1))
        out.append(v * cos + other * sin)
    return out[0] if len(out) == 1 else jnp.concatenate(out, axis=1)


def project_kernel(h_ref, own, oth, gain, wq, wk, wv, cos, sin, full, a1, q, kv, ssx):
    first = h_ref[0] == 0
    x_own = own[...].astype(F32)
    x_oth = oth[...].astype(F32)
    x = jnp.concatenate(
        [jnp.where(first, x_own, x_oth), jnp.where(first, x_oth, x_own)], axis=1
    )
    width = x.shape[1]
    total = jnp.sum(x * x, axis=1, keepdims=True)
    inv = lax.rsqrt(total * (1.0 / width) + EPS)
    act = (x * inv * gain[...]).astype(BF16)
    full[...] = x.astype(BF16)
    a1[...] = act
    ssx[...] = jnp.broadcast_to(total, ssx.shape)
    q[...] = turn(dot(act, wq[...]), cos[...], sin[...]).astype(BF16) * (HD**-0.5)
    kvw = wk.shape[1]
    kv[:, :kvw] = turn(dot(act, wk[...]), cos[...], sin[...]).astype(BF16)
    kv[:, kvw:] = dot(act, wv[...]).astype(BF16)


def project(h, own, oth, gain, wq, wk, wv, cos, sin):
    n, half = own.shape
    d = 2 * half
    tt = min(n, 256)
    qw, kvw = wq.shape[1], wk.shape[1]
    row = lambda w: pl.BlockSpec((tt, w), lambda i, *_: (i, 0))
    const = lambda a: pl.BlockSpec(a.shape, lambda i, *_: (0, 0), pipeline_mode=pl.Buffered(1))
    return launch(
        project_kernel,
        (h, own, oth, gain, wq, wk, wv, cos, sin),
        prefetch=1,
        grid=(n // tt,),
        in_specs=[row(half), row(half), const(gain), const(wq), const(wk), const(wv)]
        + [row(PAIR), row(PAIR)],
        out_specs=[row(d), row(d), row(qw), row(2 * kvw), row(PAIR)],
        out_shape=[
            jax.ShapeDtypeStruct((n, d), BF16),
            jax.ShapeDtypeStruct((n, d), BF16),
            jax.ShapeDtypeStruct((n, qw), BF16),
            jax.ShapeDtypeStruct((n, 2 * kvw), BF16),
            jax.ShapeDtypeStruct((n, PAIR), F32),
        ],
        mib=32,
        pin_in=False,
        estimate=cost(2 * n * d * (qw + 2 * kvw), 2 * d * (qw + 2 * kvw) + 12 * n * d),
        name="project",
    )


def place(kv, kvh, base):
    x = kv[:, base : base + PAIR].astype(F32)
    x = jnp.where(kvh == 0, x, pltpu.roll(x, HD, 1))
    low = jnp.where(lanes(x.shape) < HD, x, 0.0)
    return low.astype(BF16), pltpu.roll(low, HD, 1).astype(BF16)


def flip_head(kv, kvh, base):
    x = kv[:, base : base + PAIR].astype(F32).T
    return jnp.where(kvh == 0, x[:HD, :], x[HD:, :])


def attend_kernel(step, last, ppk, sc, q_ref, kv_ref, start_ref, *refs):
    refs = list(refs)
    if step:
        acc_in, ml_in = refs[:2]
        refs = refs[2:]
    acc_out, ml_out = refs
    t = q_ref.shape[0]
    kvh = pl.program_id(1)
    blk = sc[0]

    def finish(pair, par, acc, m, l):
        rows = slice(pair * PAIR + par * HD, pair * PAIR + (par + 1) * HD)
        if last:
            acc = acc / l
            m = m + jnp.log(l)
        acc_out[rows, :] = acc
        ml_out[pair, par : par + 1, :] = m
        ml_out[pair, 2 + par : 3 + par, :] = l

    heads = [(pair, par) for pair in range(ppk) for par in range(2)]

    def work():
        u = lax.broadcasted_iota(jnp.int32, (t, t), 0) + (blk - step) * t
        keep = u >= start_ref[0]
        if step == 0:
            keep = keep & (u <= lanes((t, t)) + blk * t)
        bias = jnp.where(keep, 0.0, NEG)
        kv = kv_ref[...]
        kk = place(kv, kvh, 0)
        ones = jnp.where(lax.broadcasted_iota(jnp.int32, (16, t), 0) == 0, 1.0, 0.0)
        vt = jnp.concatenate([flip_head(kv, kvh, PAIR), ones], axis=0).astype(BF16)
        scores = [
            dot_nt(kk[par], q_ref[:, pair * PAIR : (pair + 1) * PAIR]) + bias
            for pair, par in heads
        ]
        for (pair, par), s in zip(heads, scores, strict=True):
            m = jnp.max(s, axis=0, keepdims=True)
            if step:
                old = ml_in[pair, par : par + 1, :]
                m = jnp.maximum(m, old)
            pv = dot(vt, jnp.exp(s - m).astype(BF16))
            acc, l = pv[:HD], pv[HD : HD + 1]
            if step:
                factor = jnp.exp(old - m)
                rows = slice(pair * PAIR + par * HD, pair * PAIR + (par + 1) * HD)
                acc = acc + acc_in[rows, :] * factor
                l = l + ml_in[pair, 2 + par : 3 + par, :] * factor
            finish(pair, par, acc, m, l)

    if step == 0:
        work()
    else:
        pl.when(blk >= step)(work)

        @pl.when(blk < step)
        def _():
            for pair, par in heads:
                rows = slice(pair * PAIR + par * HD, pair * PAIR + (par + 1) * HD)
                m = ml_in[pair, par : par + 1, :]
                finish(pair, par, acc_in[rows, :], m, ml_in[pair, 2 + par : 3 + par, :])


def attend(step, last, sc, q, kv, start, state, rows, deps=()):
    n, qw = q.shape
    t = n // rows
    pairs = qw // PAIR
    kv_heads = kv.shape[1] // 2 // HD
    ppk = pairs // kv_heads
    accspec = pl.BlockSpec((ppk * PAIR, t), lambda r, k, *_: (k, r))
    mlspec = pl.BlockSpec((ppk, 8, t), lambda r, k, *_: (k, 0, r))
    work = n * t * qw
    return launch(
        functools.partial(attend_kernel, step, last, ppk),
        (sc, in_hbm(q), in_hbm(kv), in_hbm(start), *state),
        prefetch=1,
        grid=(rows, kv_heads),
        in_specs=[
            pl.BlockSpec((t, ppk * PAIR), lambda r, k, *_: (r, k)),
            pl.BlockSpec((t, kv.shape[1]), lambda r, k, *_: (r, 0)),
            pl.BlockSpec((1, 1, t), lambda r, k, *_: (r, 0, 0)),
        ]
        + ([accspec, mlspec] if state else []),
        out_specs=[accspec, mlspec],
        out_shape=[
            jax.ShapeDtypeStruct((qw, n), F32),
            jax.ShapeDtypeStruct((pairs, 8, n), F32),
        ],
        mib=28,
        estimate=cost(24 * work, 20 * n * qw, n * t * qw // HD),
        name=f"attend{step}",
        deps=deps,
        pin_in=False,
        pin_out=False,
    )


def flip_kernel(x, out):
    out[...] = x[...].T.astype(BF16)


def flip(x, name="flip"):
    w, n = x.shape
    by_rows = w > n
    step = 512 if max(w, n) % 512 == 0 else max(w, n)
    across = pl.BlockSpec((step, n) if by_rows else (w, step), lambda i: (i, 0) if by_rows else (0, i))
    down = pl.BlockSpec((n, step) if by_rows else (step, w), lambda i: (0, i) if by_rows else (i, 0))
    return launch(
        flip_kernel,
        (x,),
        grid=(max(w, n) // step,),
        in_specs=[across],
        out_specs=[down],
        out_shape=[jax.ShapeDtypeStruct((n, w), BF16)],
        mib=32,
        estimate=cost(8 * n * w, 6 * n * w),
        name=name,
        pin_in=False,
    )[0]


def attend_back_kernel(step, first, last, ppk, sc, q_ref, do_ref, ml_ref, start_ref, kv_ref, *refs):
    refs = list(refs)
    o_ref = refs.pop(0) if first else None
    dq_in, delta_in = (None, None) if first else (refs.pop(0), refs.pop(0))
    cos, sin = (refs.pop(0), refs.pop(0)) if last else (None, None)
    dq_out, dkv_out = refs.pop(0), refs.pop(0)
    delta_out = refs.pop(0) if first else None
    dk_acc, dv_acc, dq_acc = refs
    t = q_ref.shape[0]
    kvh = pl.program_id(1)
    blk = sc[0]
    heads = [(pair, par) for pair in range(ppk) for par in range(2)]

    if first:
        for pair in range(ppk):
            both = slice(pair * PAIR, (pair + 1) * PAIR)
            prod = (do_ref[:, both].astype(F32) * o_ref[:, both].astype(F32)).T
            for par in range(2):
                delta_out[pair, par : par + 1, :] = jnp.sum(
                    prod[par * HD : (par + 1) * HD, :], axis=0, keepdims=True
                )
        dq_acc[...] = jnp.zeros_like(dq_acc)
    else:
        dq_acc[...] = dq_in[...]
    delta = delta_out if first else delta_in

    @pl.when(kvh == 0)
    def _():
        dkv_out[...] = jnp.zeros_like(dkv_out)

    def work():
        u = lax.broadcasted_iota(jnp.int32, (t, t), 0) + (blk - step) * t
        keep = u >= start_ref[0]
        if step == 0:
            keep = keep & (u <= lanes((t, t)) + blk * t)
        bias = jnp.where(keep, 0.0, NEG)
        kv = kv_ref[...]
        kk = place(kv, kvh, 0)
        vv = place(kv, kvh, PAIR)
        kt = flip_head(kv, kvh, 0).astype(BF16)
        dk_acc[...] = jnp.zeros_like(dk_acc)
        dv_acc[...] = jnp.zeros_like(dv_acc)
        for pair, par in heads:
            q = q_ref[:, pair * PAIR : (pair + 1) * PAIR]
            do = do_ref[:, pair * PAIR : (pair + 1) * PAIR]
            st = dot_nt(kk[par], q) + bias
            dp = dot_nt(vv[par], do)
            pt = jnp.exp(st - ml_ref[pair, par : par + 1, :])
            ds = (pt * (dp - delta[pair, par : par + 1, :])).astype(BF16)
            dv_acc[par] += dot(pt.astype(BF16), do)
            dk_acc[par] += dot(ds, q)
            rows = slice(pair * PAIR + par * HD, pair * PAIR + (par + 1) * HD)
            dq_acc[rows, :] += dot(kt, ds)
        low = lanes((t, PAIR)) < HD
        for acc, base in ((dk_acc, 0), (dv_acc, PAIR)):
            both = acc[0] + pltpu.roll(acc[1], HD, 1)
            here = jnp.where(kvh == 0, both, pltpu.roll(both, HD, 1))
            mine = low == (kvh == 0)
            old = dkv_out[:, base : base + PAIR].astype(F32)
            dkv_out[:, base : base + PAIR] = jnp.where(mine, here, old).astype(BF16)

    if step == 0:
        work()
    else:
        pl.when(blk >= step)(work)

    if last:
        for pair in range(ppk):
            rows = slice(pair * PAIR, (pair + 1) * PAIR)
            dq = (dq_acc[rows, :] * (HD**-0.5)).T
            dq_out[:, rows] = turn(dq, cos[...], -sin[...]).astype(BF16)
    else:
        dq_out[...] = dq_acc[...]


def attend_back(step, first, last, sc, q, do, o, ml, start, cos, sin, kv, state, rows, deps=()):
    n, qw = q.shape
    t = n // rows
    pairs = qw // PAIR
    kvw = kv.shape[1]
    kv_heads = kvw // 2 // HD
    ppk = pairs // kv_heads
    width = ppk * PAIR
    pairspec = pl.BlockSpec((t, width), lambda r, k, *_: (r, k))
    accspec = pl.BlockSpec((width, t), lambda r, k, *_: (k, r))
    mlspec = pl.BlockSpec((ppk, 8, t), lambda r, k, *_: (k, 0, r))
    rowspec = lambda w: pl.BlockSpec((t, w), lambda r, k, *_: (r, 0))
    work = n * t * qw
    return launch(
        functools.partial(attend_back_kernel, step, first, last, ppk),
        (sc, q, do, ml, start, kv)
        + ((o,) if first else tuple(state))
        + ((cos, sin) if last else ()),
        prefetch=1,
        grid=(rows, kv_heads),
        in_specs=[pairspec, pairspec, mlspec]
        + [pl.BlockSpec((1, 1, t), lambda r, k, *_: (r, 0, 0))]
        + [rowspec(kvw)]
        + ([pairspec] if first else [accspec, mlspec])
        + ([rowspec(PAIR)] * 2 if last else []),
        out_specs=[pairspec if last else accspec, rowspec(kvw)] + ([mlspec] if first else []),
        scratch=[
            pltpu.VMEM((2, t, PAIR), F32),
            pltpu.VMEM((2, t, PAIR), F32),
            pltpu.VMEM((width, t), F32),
        ],
        out_shape=[
            jax.ShapeDtypeStruct((n, qw), BF16) if last else jax.ShapeDtypeStruct((qw, n), F32),
            jax.ShapeDtypeStruct((n, kvw), BF16),
        ]
        + ([jax.ShapeDtypeStruct((pairs, 8, n), F32)] if first else []),
        mib=40,
        estimate=cost(54 * work, 20 * n * qw, work // HD),
        name=f"attend_back{step}",
        deps=deps,
    )


def gather_dkv_kernel(count, *refs):
    parts = refs[:count]
    cos, sin, out = refs[count:]
    total = parts[0][...].astype(F32)
    for x in parts[1:]:
        total = total + x[...].astype(F32)
    half = total.shape[1] // 2
    out[:, :half] = turn(total[:, :half], cos[...], -sin[...]).astype(BF16)
    out[:, half:] = total[:, half:].astype(BF16)


def gather_dkv(parts, cos, sin, deps=()):
    whole = lambda x: pl.BlockSpec(x.shape, lambda i: (0, 0))
    return launch(
        functools.partial(gather_dkv_kernel, len(parts)),
        (*parts, cos, sin),
        grid=(1,),
        in_specs=[whole(x) for x in (*parts, cos, sin)],
        out_specs=[whole(parts[0])],
        out_shape=[jax.ShapeDtypeStruct(parts[0].shape, BF16)],
        mib=32,
        estimate=cost(10 * parts[0].size, 4 * len(parts) * parts[0].size),
        name="gather_dkv",
        deps=deps,
    )[0]


def merge_kernel(o_own, o_oth, w_own, w_oth, full, gain, h1, a2, a2_t, r2, ssa, held, sums):
    i = pl.program_id(0)
    attn = dot_nt(o_own[...], w_own[...]) + dot_nt(o_oth[...], w_oth[...])
    x = full[...].astype(F32) + attn
    h1[0] = x
    held[i] = x

    @pl.when(i == 0)
    def _():
        sums[...] = jnp.zeros_like(sums)
        ssa[...] = jnp.zeros_like(ssa)

    sums[...] += jnp.sum(x * x, axis=1, keepdims=True)
    ssa[...] += jnp.sum(attn * attn, axis=1, keepdims=True)

    @pl.when(i == pl.num_programs(0) - 1)
    def _():
        count, _, dt = held.shape
        inv = lax.rsqrt(sums[...] * (1.0 / (count * dt)) + EPS)
        r2[...] = inv
        for j in range(count):
            at = slice(j * dt, (j + 1) * dt)
            act = (held[j] * inv[:, :1] * gain[:, at]).astype(BF16)
            a2[:, at] = act
            a2_t[at, :] = act.T


def merge(o_own, o_oth, w_own, w_oth, full, gain, deps=()):
    n, d = full.shape
    dt = 512
    e = o_own.shape[1]
    const = lambda a: pl.BlockSpec(a.shape, lambda i: (0, 0), pipeline_mode=pl.Buffered(1))
    return launch(
        merge_kernel,
        (o_own, o_oth, w_own, w_oth, full, gain),
        grid=(d // dt,),
        in_specs=[
            const(o_own),
            const(o_oth),
            pl.BlockSpec((dt, e), lambda i: (i, 0)),
            pl.BlockSpec((dt, e), lambda i: (i, 0)),
            pl.BlockSpec((n, dt), lambda i: (0, i)),
            const(gain),
        ],
        out_specs=[
            pl.BlockSpec((1, n, dt), lambda i: (i, 0, 0)),
            pl.BlockSpec((n, d), lambda i: (0, 0)),
            pl.BlockSpec((d, n), lambda i: (0, 0)),
            pl.BlockSpec((n, PAIR), lambda i: (0, 0)),
            pl.BlockSpec((n, PAIR), lambda i: (0, 0)),
        ],
        out_shape=[
            jax.ShapeDtypeStruct((d // dt, n, dt), F32),
            jax.ShapeDtypeStruct((n, d), BF16),
            jax.ShapeDtypeStruct((d, n), BF16),
            jax.ShapeDtypeStruct((n, PAIR), F32),
            jax.ShapeDtypeStruct((n, PAIR), F32),
        ],
        scratch=[pltpu.VMEM((d // dt, n, dt), F32), pltpu.VMEM((n, PAIR), F32)],
        mib=48,
        estimate=cost(3 * n * d * d, 2 * d * d + 12 * n * d),
        name="merge",
        deps=deps,
    )


def units_kernel(a2, g, wg, wu, wd, out):
    gate = dot(a2[...], wg[...])
    up = dot(a2[...], wu[...])
    dh = dot(g[...], wd[...])
    sig = jax.nn.sigmoid(gate)
    act = gate * sig
    out[0] = (act * up).astype(BF16)
    out[1] = (dh * up * sig * (1.0 + gate * (1.0 - sig))).astype(BF16)
    out[2] = (dh * act).astype(BF16)


def units(a2, g, wg, wu, wd, first, count, deps=()):
    n, d = a2.shape
    const = pl.BlockSpec((n, d), lambda i: (0, 0), pipeline_mode=pl.Buffered(1))
    wspec = pl.BlockSpec((d, FT), lambda i: (0, first + i))
    return launch(
        units_kernel,
        (a2, g, wg, wu, wd),
        grid=(count,),
        in_specs=[const, const, wspec, wspec, wspec],
        out_specs=[pl.BlockSpec((3, n, FT), lambda i: (0, 0, i))],
        out_shape=[jax.ShapeDtypeStruct((3, n, count * FT), BF16)],
        mib=58,
        estimate=cost(10 * n * d * FT * count, 6 * d * FT * count, n * FT * count),
        name=f"units{first}",
        deps=deps,
    )[0]


def exchange_kernel(count, tiles, nblk, *refs):
    acts = refs[: 3 * count]
    wg, wu, wd, early, total, branch, shares = refs[3 * count : 3 * count + 7]
    mine, theirs, send_sem, recv_sem, z_send, z_recv, own_sem = refs[3 * count + 7 :]
    i = pl.program_id(0)
    other = 1 - lax.axis_index("head")
    blk = lax.axis_index("blk")
    rows = early.shape[0] // nblk

    def copy(j):
        return pltpu.make_async_remote_copy(
            src_ref=mine.at[j],
            dst_ref=theirs.at[j],
            send_sem=send_sem.at[j],
            recv_sem=recv_sem.at[j],
            device_id={"head": other},
            device_id_type=pl.DeviceIdType.MESH,
        )

    def block(b):
        return early.at[pl.ds(pl.multiple_of(b * rows, rows), rows), :]

    def share(k):
        to = lax.rem(blk + k, nblk)
        return pltpu.make_async_remote_copy(
            src_ref=block(to),
            dst_ref=shares.at[blk],
            send_sem=z_send.at[k],
            recv_sem=z_recv.at[k],
            device_id={"blk": to},
            device_id_type=pl.DeviceIdType.MESH,
        )

    def keep():
        return pltpu.make_async_copy(block(blk), shares.at[blk], own_sem)

    def product(m, weight):
        out, at = None, 0
        for act in acts[m * count : (m + 1) * count]:
            term = dot_nt(act[0], weight[:, at : at + act.shape[2]])
            out = term if out is None else out + term
            at += act.shape[2]
        return out

    @pl.when(i == 0)
    def _():
        barrier = pltpu.get_barrier_semaphore()
        pl.semaphore_signal(
            barrier, inc=1, device_id={"head": other}, device_id_type=pl.DeviceIdType.MESH
        )
        for k in range(1, nblk):
            pl.semaphore_signal(
                barrier,
                inc=1,
                device_id={"blk": lax.rem(blk + k, nblk)},
                device_id_type=pl.DeviceIdType.MESH,
            )
        pl.semaphore_wait(barrier, nblk)
        for k in range(1, nblk):
            share(k).start()
        keep().start()

    @pl.when(i < tiles)
    def _():
        mine[i] = (product(1, wg) + product(2, wu)).astype(BF16)
        copy(i).start()

    @pl.when(i >= tiles)
    def _():
        branch[0] = product(0, wd).astype(BF16)

    @pl.when(i == 2 * tiles - 1)
    def _():
        width = mine.shape[2]
        for j in range(tiles):
            copy(j).wait()
            total[:, j * width : (j + 1) * width] = mine[j].astype(F32) + theirs[j].astype(F32)
        for k in range(1, nblk):
            share(k).wait()
        keep().wait()


def exchange(stacks, wg, wu, wd, early, nblk, name):
    n = stacks[0].shape[1]
    d, ff = wg.shape
    dt = 256
    tiles = d // dt
    per = tiles // 2
    acts = [x for _ in range(3) for x in stacks]
    specs = [
        pl.BlockSpec((1,) + x.shape[1:], lambda i, m=m: (m, 0, 0), pipeline_mode=pl.Buffered(1))
        for m in range(3)
        for x in stacks
    ]
    first = pl.BlockSpec((dt, ff), lambda i: (jnp.minimum(i, tiles - 1), 0))
    second = pl.BlockSpec((dt, ff), lambda i: (jnp.maximum(i - tiles, 0), 0))
    place_hbm = pl.BlockSpec(memory_space=pltpu.HBM)

    def branch_at(i):
        j = jnp.maximum(i - tiles, 0)
        return (j // per, 0, j % per)

    return launch(
        functools.partial(exchange_kernel, len(stacks), tiles, nblk),
        (*acts, wg, wu, wd, early),
        grid=(2 * tiles,),
        in_specs=specs + [first, first, second, place_hbm],
        out_specs=[
            pl.BlockSpec((n, d), lambda i: (0, 0)),
            pl.BlockSpec((1, n, dt), branch_at),
            place_hbm,
        ],
        out_shape=[
            jax.ShapeDtypeStruct((n, d), F32),
            jax.ShapeDtypeStruct((2, n, d // 2), BF16),
            jax.ShapeDtypeStruct((nblk, early.shape[0] // nblk, early.shape[1]), BF16),
        ],
        scratch=[
            pltpu.VMEM((tiles, n, dt), BF16),
            pltpu.VMEM((tiles, n, dt), BF16),
            pltpu.SemaphoreType.DMA((tiles,)),
            pltpu.SemaphoreType.DMA((tiles,)),
            pltpu.SemaphoreType.DMA((nblk,)),
            pltpu.SemaphoreType.DMA((nblk,)),
            pltpu.SemaphoreType.DMA,
        ],
        mib=58,
        estimate=cost(6 * n * d * ff, 6 * d * ff),
        name=name,
        collective=1,
    )


def stream_kernel(da_sum, h1, r2, gain, g, w_out, dh1, dattn_t, dout, gsum):
    da = da_sum[...]
    inv = r2[:, :1]
    norm = jnp.concatenate([h1[j] for j in range(h1.shape[0])], axis=1) * inv
    grad = da * norm

    @pl.when(pl.program_id(0) == 0)
    def _():
        gsum[...] = jnp.zeros_like(gsum)

    gsum[...] += jnp.sum(grad, axis=0, keepdims=True)
    e2 = da * gain[...]
    mean = jnp.sum(e2 * norm, axis=1, keepdims=True) * (1.0 / da.shape[1])
    dh = g[...].astype(F32) + inv * (e2 - norm * mean)
    dh1[...] = dh
    low = dh.astype(BF16)
    dattn_t[...] = low.T
    dout[...] = dot(low, w_out[...]).astype(BF16)


def stream(da, h1, r2, gain, g, w_out, deps=()):
    parts, n, dt = h1.shape
    d = parts * dt
    tt = min(n, 128)
    ew = w_out.shape[1]
    row = lambda w: pl.BlockSpec((tt, w), lambda i: (i, 0))
    const = lambda a: pl.BlockSpec(a.shape, lambda i: (0, 0), pipeline_mode=pl.Buffered(1))
    return launch(
        stream_kernel,
        (da, h1, r2, gain, g, w_out),
        grid=(n // tt,),
        in_specs=[
            row(d),
            pl.BlockSpec((parts, tt, dt), lambda i: (0, i, 0)),
            row(PAIR),
            const(gain),
            row(d),
            const(w_out),
        ],
        out_specs=[
            row(d),
            pl.BlockSpec((d, tt), lambda i: (0, i)),
            row(ew),
            pl.BlockSpec((1, d), lambda i: (0, 0)),
        ],
        out_shape=[
            jax.ShapeDtypeStruct((n, d), F32),
            jax.ShapeDtypeStruct((d, n), BF16),
            jax.ShapeDtypeStruct((n, ew), BF16),
            jax.ShapeDtypeStruct((1, d), F32),
        ],
        mib=56,
        estimate=cost(2 * n * d * ew, 2 * d * ew + 20 * n * d),
        name="stream",
        deps=deps,
    )


def entry_kernel(dq, dkv, wq, wk, wv, full, ssx, gain, part, gsum, rsum):
    kvw = wk.shape[1]
    da = dot_nt(dq[...], wq[...])
    da = da + dot_nt(dkv[:, :kvw], wk[...]) + dot_nt(dkv[:, kvw:], wv[...])
    width = pl.num_programs(0) * da.shape[1]
    inv = lax.rsqrt(ssx[:, :1] * (1.0 / width) + EPS)
    grad = da * (full[...].astype(F32) * inv)
    gsum[...] = jnp.sum(grad, axis=0, keepdims=True)

    @pl.when(pl.program_id(0) == 0)
    def _():
        rsum[...] = jnp.zeros_like(rsum)

    rsum[...] += jnp.sum(grad * gain[...], axis=1, keepdims=True)
    part[0] = da.astype(BF16)


def entry(dq, dkv, wq, wk, wv, full, ssx, gain):
    n, d = full.shape
    dt = 256
    per = d // 2 // dt
    const = lambda a: pl.BlockSpec(a.shape, lambda i: (0, 0), pipeline_mode=pl.Buffered(1))
    wspec = lambda w: pl.BlockSpec((dt, w.shape[1]), lambda i: (i, 0))
    return launch(
        entry_kernel,
        (dq, dkv, wq, wk, wv, full, ssx, gain),
        grid=(d // dt,),
        in_specs=[const(dq), const(dkv), wspec(wq), wspec(wk), wspec(wv)]
        + [
            pl.BlockSpec((n, dt), lambda i: (0, i)),
            const(ssx),
            pl.BlockSpec((1, dt), lambda i: (0, i)),
        ],
        out_specs=[
            pl.BlockSpec((1, n, dt), lambda i: (i // per, 0, i % per)),
            pl.BlockSpec((1, dt), lambda i: (0, i)),
            pl.BlockSpec((n, PAIR), lambda i: (0, 0)),
        ],
        out_shape=[
            jax.ShapeDtypeStruct((2, n, d // 2), BF16),
            jax.ShapeDtypeStruct((1, d), F32),
            jax.ShapeDtypeStruct((n, PAIR), F32),
        ],
        mib=56,
        estimate=cost(2 * n * d * (wq.shape[1] + 2 * wk.shape[1]), 20 * n * d),
        name="entry",
    )


def outer_kernel(shares, count, parts, adds, spread, sc, *refs):
    k = 0
    lefts, rights = [], []
    for share in shares:
        lefts.append((refs[k : k + count], refs[k + count : k + 2 * count]))
        k += 2 * count
        rights.append([(refs[k + 2 * i], refs[k + 2 * i + 1]) for i in range(share)])
        k += 2 * share
    got = refs[k] if adds else None
    outs = refs[k + adds :]

    def work(out):
        m = 0
        for (left_own, left_oth), group in zip(lefts, rights, strict=True):
            rows = left_own[0].shape[0]
            for own, oth in group:
                at = slice(m * FT, (m + 1) * FT)
                for i in range(count):
                    part = slice(i * rows, (i + 1) * rows)
                    total = dot(left_own[i][...], own[0]) + dot(left_oth[i][...], oth[0])
                    if adds:
                        total = total + got[part, at].astype(F32)
                    if spread == 1:
                        out[part, at] = total.astype(BF16)
                    else:
                        size = rows // spread
                        for b in range(spread):
                            to = slice((b * count + i) * size, (b * count + i + 1) * size)
                            out[to, at] = total[b * size : (b + 1) * size, :].astype(BF16)
                m += 1

    if len(parts) == 1:
        work(outs[0])
        return
    step = pl.program_id(0)
    start = 0
    for out, size in zip(outs, parts, strict=True):
        pl.when((step >= start) & (step < start + size))(functools.partial(work, out))
        start += size


def outer(sc, groups, rows, first, parts, name, got=None, deps=(), spread=1):
    n = groups[0][0].shape[1]
    count = sc.shape[0]
    number = sum(parts)
    shares = tuple(len(g[2]) for g in groups)
    ins, specs = [], []
    for own, oth, rights in groups:
        ins += [own] * count + [oth] * count
        for i in range(count):
            specs.append(pl.BlockSpec((rows, n), lambda j, s, i=i: (s[i], 0)))
        specs += specs[-count:]
        for r_own, r_oth, at in rights:
            ins += [r_own, r_oth]
            specs += [pl.BlockSpec((1, n, FT), lambda i, s, at=at: (at, 0, first + i))] * 2
    members = sum(shares)
    height = count * rows
    ospecs, start = [], 0
    for size in parts:
        ospecs.append(
            pl.BlockSpec(
                (height, members * FT),
                lambda i, s, start=start, size=size: (0, jnp.clip(i - start, 0, size - 1)),
            )
        )
        start += size
    if got is not None:
        ins.append(got)
        specs.append(ospecs[0])
    c = number * FT
    return launch(
        functools.partial(outer_kernel, shares, count, tuple(parts), int(got is not None), spread),
        (sc, *ins),
        prefetch=1,
        grid=(number,),
        in_specs=specs,
        out_specs=ospecs,
        out_shape=[jax.ShapeDtypeStruct((height, members * size * FT), BF16) for size in parts],
        mib=48,
        estimate=cost(8 * n * height * c * members, members * c * (4 * n + 2 * height)),
        name=name,
        deps=deps,
    )


def finish_kernel(count, *refs):
    parts = refs[:count]
    outs = refs[count:]
    at = 0
    for part in parts:
        for tile in range(part.shape[2] // (3 * FT)):
            for m in range(3):
                columns = slice((3 * tile + m) * FT, (3 * tile + m + 1) * FT)
                total = part[0, :, columns].astype(F32)
                for b in range(1, part.shape[0]):
                    total = total + part[b, :, columns].astype(F32)
                outs[m][:, at : at + FT] = total
            at += FT


def finish(parts):
    parts = [x.reshape(count, x.shape[0] // count, x.shape[1]) for x, count in parts]
    rows = parts[0].shape[1]
    width = sum(x.shape[2] for x in parts) // 3
    whole = lambda shape: pl.BlockSpec(shape, lambda i: (0,) * len(shape))
    return launch(
        functools.partial(finish_kernel, len(parts)),
        tuple(parts),
        grid=(1,),
        in_specs=[whole(x.shape) for x in parts],
        out_specs=[whole((rows, width))] * 3,
        out_shape=[jax.ShapeDtypeStruct((rows, width), F32)] * 3,
        mib=48,
        estimate=cost(0, 8 * parts[0].shape[0] * rows * width),
        name="finish",
    )


def body(
    inputs,
    cotangent,
    lengths,
    attn_gain,
    w_query,
    w_key,
    w_value,
    w_out,
    mlp_gain,
    gate_weight,
    up_weight,
    down_weight,
):
    t, rows, half = inputs.shape
    n = t * rows
    heads = lax.axis_size("head")
    nblk = lax.axis_size("blk")
    ndp = lax.axis_size("dp")
    d = half * heads
    h = lax.axis_index("head").astype(jnp.int32)
    blk = lax.axis_index("blk").astype(jnp.int32)
    dp = lax.axis_index("dp").astype(jnp.int32)
    sc_h = h.reshape(1)
    sc_blk = blk.reshape(1)

    def flat(x):
        return jnp.transpose(x, (1, 0, 2)).reshape(n, x.shape[2])

    def unflat(x):
        return jnp.transpose(x.reshape(rows, t, x.shape[1]), (1, 0, 2))

    x_own = flat(inputs)
    g_own = flat(cotangent)
    gain_one = attn_gain.astype(F32).reshape(1, d)
    gain_two = mlp_gain.astype(F32).reshape(1, d)

    pos = blk * t + jnp.arange(t, dtype=jnp.int32)
    ends = jnp.cumsum(lengths, axis=1)
    passed = ends[:, None, :] <= pos[None, :, None]
    start = jnp.max(jnp.where(passed, ends[:, None, :], 0), axis=2)
    valid = (jnp.sum(passed.astype(jnp.int32), axis=2) < DOCS).astype(F32).reshape(n)
    start_rows = start.reshape(rows, 1, t)
    freq = jnp.power(THETA, -2.0 * jnp.arange(HD // 2, dtype=F32) / HD)
    angles = pos.astype(F32)[:, None] * freq[None, :]
    cos_h, sin_h = jnp.cos(angles), jnp.sin(angles)
    cos = jnp.tile(jnp.concatenate([cos_h, cos_h, cos_h, cos_h], axis=1), (rows, 1))
    sin = jnp.tile(jnp.concatenate([-sin_h, sin_h, -sin_h, sin_h], axis=1), (rows, 1))

    CHAIN.clear()
    WEIGHT[0] = EARLY

    def tie(x, *also):
        return lax.optimization_barrier((x, *also))[0]

    def by_head(x):
        return jnp.where(h == 0, x[:, :half], x[:, half:])

    def gate(x):
        x, CHAIN[0] = lax.optimization_barrier((x, CHAIN[0]))
        return x

    def mate(x):
        return swap(x, "dp", 1)

    x_oth = swap(x_own, "head", 1)
    share = w_out.shape[0] // ndp
    piece = lax.dynamic_slice_in_dim(w_out, dp * share, share, 0)
    x_oth, piece, g_own, cos, sin, start_rows = lax.optimization_barrier(
        (x_oth, piece, g_own, cos, sin, start_rows)
    )
    piece = swap(piece, "head", 1)
    full, a_one, queries, kv, ssx = project(
        sc_h, x_own, x_oth, gain_one, w_query, w_key, w_value, cos, sin
    )

    kvs, state = [kv], ()
    for s in range(nblk):
        if s + 1 < nblk:
            steps = [(i, i + 1) for i in range(s, nblk - 1)]
            kvs.append(lax.ppermute(kvs[s], "blk", steps))
        state = attend(s, s == nblk - 1, sc_blk, queries, kvs[s], start_rows, state, rows)
        if s + 1 < nblk - 1:
            kvs[s + 1] = gate(kvs[s + 1])
        if s == 0:
            a_one_t = flip(a_one, "flip_a")
            piece = gate(piece)
            w_out_oth = lax.all_gather(piece, "dp", axis=0, tiled=True)
            g_own, piece = lax.optimization_barrier((g_own, piece))
            g_oth = swap(g_own, "head", 1)
    acc, ml = state
    o_own = flip(acc)
    o_oth = swap(o_own, "head", 1)
    g_full = jnp.concatenate(
        [jnp.where(h == 0, g_own, g_oth), jnp.where(h == 0, g_oth, g_own)], axis=1
    )
    g_t = flip(g_full, "flip_g")
    o_mate, g_mate = mate(o_own), mate(g_t)
    h_one, a_two, a_two_t, inv_two, ssa = merge(
        o_own, o_oth, w_out, w_out_oth, full, gain_two
    )
    a_two_mate = mate(a_two_t)

    low_bit = dp & 1
    block_rows = d // ndp
    sc_send = (dp ^ 2).reshape(1)
    sc_keep = dp.reshape(1)
    sc_both = jnp.stack([2 * i + low_bit for i in range(ndp // 2)])
    y_groups = [[0, 2], [1, 3]]

    def both_halves(groups, parts, name, deps=()):
        return [
            lax.psum_scatter(
                x, "dp", scatter_dimension=0, axis_index_groups=y_groups, tiled=True
            )
            for x in outer(sc_both, groups, block_rows, 0, parts, name, deps=deps)
        ]

    def over_blk(x):
        return lax.all_to_all(x, "blk", split_axis=0, concat_axis=0, tiled=True)

    tiles = gate_weight.shape[1] // FT
    size_a = max(1, tiles // 5)
    size_b = (tiles - size_a + 1) // 3
    size_c = tiles - size_a - size_b

    def unit_part(first, count, deps=()):
        x = units(a_two, g_full, gate_weight, up_weight, down_weight, first, count, deps)
        x_mate = mate(x)
        return x, [
            (g_t, g_mate, [(x, x_mate, 0)]),
            (a_two_t, a_two_mate, [(x, x_mate, 1), (x, x_mate, 2)]),
        ]

    part_a, groups_a = unit_part(0, size_a)
    (sum0,) = both_halves(groups_a, (size_a,), "mlp0")
    part_b, groups_b = unit_part(size_a, size_b)
    part_c, groups_c = unit_part(size_a + size_b, size_c)
    (sum1,) = both_halves(groups_b, (size_b,), "mlp1")

    da, branch, all0 = exchange(
        [part_a, part_b, part_c], gate_weight, up_weight, down_weight, sum0, nblk, "exchange"
    )
    WEIGHT[0] = LATE
    sum2, sum3 = both_halves(groups_c, (size_c - size_c // 2, size_c // 2), "mlp2")
    all1 = over_blk(gate(sum1))
    dh_one, d_attn_t, d_out, gain_two_sum = stream(
        da, h_one, inv_two, gain_two, g_full, w_out
    )
    d_attn_mate, a_one_mate = mate(d_attn_t), mate(gate(a_one_t))
    out_groups = [(d_attn_t, d_attn_mate, [(o_own[None], o_mate[None], 0)])]
    out_parts = (o_own.shape[1] // FT,)
    (first_out,) = outer(
        sc_send, out_groups, block_rows, 0, out_parts, "out_send", deps=(a_one_mate,)
    )
    got_out = swap(first_out, "dp", 2)
    to_other = gate(lax.dynamic_index_in_dim(branch, 1 - h, 0, keepdims=False))
    branch_oth = swap(to_other, "head", 1)

    state, parts = (), []
    for s in reversed(range(nblk)):
        out = attend_back(
            s, s == nblk - 1, s == 0, sc_blk, queries, d_out, o_own, ml, start_rows, cos, sin,
            kvs[s], state, rows, deps=(),
        )
        state = (out[0], out[2] if s == nblk - 1 else state[1])
        part = out[1]
        parts.append(
            lax.ppermute(part, "blk", [(i, i - s) for i in range(s, nblk)]) if s else part
        )
        if s == min(1, nblk - 1):
            (keep_out,) = outer(
                sc_keep, out_groups, block_rows, 0, out_parts, "out_keep", got_out,
                deps=(all1,) + tuple(parts[: nblk - 1]),
            )
            all2 = over_blk(gate(sum2))
    d_q = state[0]
    d_kv_own = gather_dkv(parts, cos, sin)
    d_qkv = jnp.concatenate([d_q, d_kv_own], axis=1)
    d_qkv_mate = mate(d_qkv)
    d_part, gain_one_sum, row_sum = entry(
        d_q, d_kv_own, w_query, w_key, w_value, full, ssx, gain_one
    )
    qkv_groups = [(a_one_t, a_one_mate, [(d_qkv[None], d_qkv_mate[None], 0)])]
    qkv_parts = (d_qkv.shape[1] // FT,)
    (first_qkv,) = outer(sc_send, qkv_groups, block_rows, 0, qkv_parts, "qkv_send")
    got_qkv = swap(first_qkv, "dp", 2)
    sum3 = lax.psum_scatter(gate(sum3), "blk", scatter_dimension=0, tiled=True)
    d_send = lax.dynamic_index_in_dim(d_part, 1 - h, 0, keepdims=False)
    d_send, row_sum, gain_one_sum, CHAIN[0] = lax.optimization_barrier(
        (d_send, row_sum, gain_one_sum, CHAIN[0])
    )
    h_late, branch_late = gate(h_one), gate(branch)
    h_half = jnp.concatenate(
        [
            jnp.where(h == 0, h_late[i], h_late[i + h_late.shape[0] // 2])
            for i in range(h_late.shape[0] // 2)
        ],
        axis=1,
    )
    mlp_half = lax.dynamic_index_in_dim(branch_late, h, 0, keepdims=False).astype(F32) + (
        branch_oth.astype(F32)
    )
    output = unflat((h_half + mlp_half).astype(BF16))
    d_other = swap(d_send, "head", 1)
    row_total = row_sum + swap(row_sum, "head", 1)
    (keep_qkv,) = outer(
        sc_keep, qkv_groups, block_rows, 0, qkv_parts, "qkv_keep", got_qkv, deps=(all2, branch_oth)
    )
    per_head = 1.0 / heads
    tail = jnp.stack(
        [
            jnp.sum(valid) * per_head,
            jnp.sum(valid * ssx[:, 0]) * per_head,
            jnp.sum(valid * ssa[:, 0]) * per_head,
            jnp.sum(valid[:, None] * mlp_half * mlp_half),
        ]
    )
    small = jnp.concatenate(
        [gain_one_sum[0], gain_two_sum[0] * per_head, tail, jnp.zeros((PAIR - 4,), F32)]
    ).reshape(-1, PAIR)
    for axis in ("head", "dp"):
        for i in range(lax.axis_size(axis).bit_length() - 1):
            small = small + swap(small, axis, 1 << i)
    small = small.reshape(-1)
    mine = [
        lax.dynamic_slice_in_dim(small, at + dp * block_rows, block_rows, 0)[:, None]
        for at in (0, d)
    ]
    sums4 = jnp.broadcast_to(small[None, 2 * d : 2 * d + 4], (block_rows, 4))
    exact = jnp.concatenate(mine + [sums4], axis=1)
    coarse = exact.astype(BF16)
    fine = (exact - coarse.astype(F32)).astype(BF16)
    extra = jnp.concatenate(
        [coarse, fine, jnp.zeros((block_rows, PAIR - 12), BF16)], axis=1
    )
    all_qkv = over_blk(jnp.concatenate([keep_qkv, extra, keep_out], axis=1))
    grad_down, grad_gate, grad_up = finish([(all0.reshape(-1, all0.shape[2]), nblk), (all1, nblk), (all2, nblk), (sum3, 1)])
    own_rows = lambda x: jnp.sum(x.reshape(nblk, -1, x.shape[1]).astype(F32), axis=0)
    sum_qkv = own_rows(all_qkv)
    sum_out = sum_qkv[:, sum_qkv.shape[1] - o_own.shape[1] :]
    qw, kvw = w_query.shape[1], w_key.shape[1]

    inv_one = lax.rsqrt(ssx[:, :1] * (1.0 / d) + EPS)
    d_one = lax.dynamic_index_in_dim(d_part, h, 0, keepdims=False).astype(F32) + d_other.astype(F32)
    norm_half = x_own.astype(F32) * inv_one
    grad_input = by_head(tie(dh_one, d_other)) + inv_one * (
        d_one * by_head(gain_one) - norm_half * (row_total[:, :1] * (1.0 / d))
    )

    width = qw + 2 * kvw
    small = sum_qkv[:, width : width + 6] + sum_qkv[:, width + 6 : width + 12]
    grad_attn_gain, grad_mlp_gain = small[:, 0], small[:, 1]
    stats = jnp.sqrt(small[0, 3:6] / (small[0, 2] * d))

    return (
        output,
        unflat(grad_input),
        grad_attn_gain,
        sum_qkv[:, :qw],
        sum_qkv[:, qw : qw + kvw],
        sum_qkv[:, qw + kvw : width],
        sum_out,
        grad_mlp_gain,
        grad_gate,
        grad_up,
        grad_down,
        stats,
    )


def solution(mesh):
    tokens = P("blk", "dp", "head")
    split = P(None, "head")
    in_specs = (tokens, tokens, P("dp", None), P()) + (split,) * 4 + (P(),) + (split,) * 3
    vec, mat = P(("dp", "blk")), P(("dp", "blk"), "head")
    out_specs = (tokens, tokens, vec, mat, mat, mat, mat, vec, mat, mat, mat, P())
    return jax.shard_map(body, mesh=mesh, in_specs=in_specs, out_specs=out_specs, check_vma=False)
```

```python
import functools

import jax
import jax.numpy as jnp
from jax import lax
from jax.experimental import pallas as pl
from jax.experimental.pallas import tpu as pltpu
from jax.sharding import PartitionSpec as P

HD = 64
PAIR = 2 * HD
DOCS = 8
EPS = 1e-05
THETA = 10000.0
NEG = -1e30
F32 = jnp.float32
BF16 = jnp.bfloat16
FT = 256


EARLY, LATE = 0.4, 0.4
WEIGHT = [EARLY]


def params(mib, collective=None):
    if collective is None:
        return pltpu.CompilerParams(vmem_limit_bytes=mib << 20)
    return pltpu.CompilerParams(
        vmem_limit_bytes=mib << 20, collective_id=collective, has_side_effects=True
    )


def cost(flops, byte_count, trans=0):
    return pl.CostEstimate(
        flops=int(flops * WEIGHT[0]),
        bytes_accessed=int(byte_count * WEIGHT[0]),
        transcendentals=int(trans * WEIGHT[0]),
    )


CHAIN = []


def in_hbm(x):
    return pltpu.with_memory_space_constraint(x, pltpu.HBM)


def launch(kernel, args, *, grid, in_specs, out_specs, out_shape, mib, estimate, name, scratch=(), prefetch=0, deps=(), pin_in=True, pin_out=True, collective=None):
    extra = list(CHAIN) + list(deps)
    n_in, n_out = len(args), len(out_shape)

    def wrapped(*refs):
        rest = refs[n_in + len(extra) :]
        kernel(*refs[:n_in], *rest[:n_out], *rest[n_out + 1 :])

    if pin_in:
        args = tuple(args[:prefetch]) + tuple(in_hbm(x) for x in args[prefetch:])
    if pin_out:
        out_shape = [pltpu.HBM(o.shape, o.dtype) for o in out_shape]
    extra = [in_hbm(x) for x in extra]
    *outs, token = pl.pallas_call(
        wrapped,
        grid_spec=pltpu.PrefetchScalarGridSpec(
            num_scalar_prefetch=prefetch,
            grid=grid,
            in_specs=list(in_specs) + [pl.BlockSpec(memory_space=pltpu.HBM)] * len(extra),
            out_specs=list(out_specs) + [pl.BlockSpec(memory_space=pltpu.HBM)],
            scratch_shapes=list(scratch),
        ),
        out_shape=list(out_shape) + [pltpu.HBM((8, 128), F32)],
        compiler_params=params(mib, collective),
        cost_estimate=estimate,
        name=name,
    )(*args, *extra)
    CHAIN[:] = [token]
    return outs


def dot(a, b):
    return jnp.dot(a, b, preferred_element_type=F32)


def dot_nt(a, b):
    return lax.dot_general(a, b, (((1,), (1,)), ((), ())), preferred_element_type=F32)


def dot_tn(a, b):
    return lax.dot_general(a, b, (((0,), (0,)), ((), ())), preferred_element_type=F32)


def swap(x, axis, bit):
    n = lax.axis_size(axis)
    return lax.ppermute(x, axis, [(i, i ^ bit) for i in range(n)])


def lanes(shape):
    return lax.broadcasted_iota(jnp.int32, shape, len(shape) - 1)


def turn(x, cos, sin):
    out = []
    for c in range(x.shape[1] // PAIR):
        v = x[:, c * PAIR : (c + 1) * PAIR]
        low = lanes(v.shape) % HD < HD // 2
        other = jnp.where(low, pltpu.roll(v, PAIR - HD // 2, 1), pltpu.roll(v, HD // 2, 1))
        out.append(v * cos + other * sin)
    return out[0] if len(out) == 1 else jnp.concatenate(out, axis=1)


def project_kernel(h_ref, own, oth, gain, wq, wk, wv, cos, sin, full, a1, q, kv, ssx):
    first = h_ref[0] == 0
    x_own = own[...].astype(F32)
    x_oth = oth[...].astype(F32)
    x = jnp.concatenate(
        [jnp.where(first, x_own, x_oth), jnp.where(first, x_oth, x_own)], axis=1
    )
    width = x.shape[1]
    total = jnp.sum(x * x, axis=1, keepdims=True)
    inv = lax.rsqrt(total * (1.0 / width) + EPS)
    act = (x * inv * gain[...]).astype(BF16)
    full[...] = x.astype(BF16)
    a1[...] = act
    ssx[...] = jnp.broadcast_to(total, ssx.shape)
    q[...] = turn(dot(act, wq[...]), cos[...], sin[...]).astype(BF16) * (HD**-0.5)
    kvw = wk.shape[1]
    kv[:, :kvw] = turn(dot(act, wk[...]), cos[...], sin[...]).astype(BF16)
    kv[:, kvw:] = dot(act, wv[...]).astype(BF16)


def project(h, own, oth, gain, wq, wk, wv, cos, sin):
    n, half = own.shape
    d = 2 * half
    tt = min(n, 256)
    qw, kvw = wq.shape[1], wk.shape[1]
    row = lambda w: pl.BlockSpec((tt, w), lambda i, *_: (i, 0))
    const = lambda a: pl.BlockSpec(a.shape, lambda i, *_: (0, 0), pipeline_mode=pl.Buffered(1))
    return launch(
        project_kernel,
        (h, own, oth, gain, wq, wk, wv, cos, sin),
        prefetch=1,
        grid=(n // tt,),
        in_specs=[row(half), row(half), const(gain), const(wq), const(wk), const(wv)]
        + [row(PAIR), row(PAIR)],
        out_specs=[row(d), row(d), row(qw), row(2 * kvw), row(PAIR)],
        out_shape=[
            jax.ShapeDtypeStruct((n, d), BF16),
            jax.ShapeDtypeStruct((n, d), BF16),
            jax.ShapeDtypeStruct((n, qw), BF16),
            jax.ShapeDtypeStruct((n, 2 * kvw), BF16),
            jax.ShapeDtypeStruct((n, PAIR), F32),
        ],
        mib=32,
        pin_in=False,
        estimate=cost(2 * n * d * (qw + 2 * kvw), 2 * d * (qw + 2 * kvw) + 12 * n * d),
        name="project",
    )


def place(kv, kvh, base):
    x = kv[:, base : base + PAIR].astype(F32)
    x = jnp.where(kvh == 0, x, pltpu.roll(x, HD, 1))
    low = jnp.where(lanes(x.shape) < HD, x, 0.0)
    return low.astype(BF16), pltpu.roll(low, HD, 1).astype(BF16)


def flip_head(kv, kvh, base):
    x = kv[:, base : base + PAIR].astype(F32).T
    return jnp.where(kvh == 0, x[:HD, :], x[HD:, :])


def attend_kernel(step, last, ppk, sc, q_ref, kv_ref, start_ref, *refs):
    refs = list(refs)
    if step:
        acc_in, ml_in = refs[:2]
        refs = refs[2:]
    acc_out, ml_out = refs
    t = q_ref.shape[0]
    kvh = pl.program_id(1)
    blk = sc[0]

    def finish(pair, par, acc, m, l):
        rows = slice(pair * PAIR + par * HD, pair * PAIR + (par + 1) * HD)
        if last:
            acc = acc / l
            m = m + jnp.log(l)
        acc_out[rows, :] = acc
        ml_out[pair, par : par + 1, :] = m
        ml_out[pair, 2 + par : 3 + par, :] = l

    heads = [(pair, par) for pair in range(ppk) for par in range(2)]

    def work():
        u = lax.broadcasted_iota(jnp.int32, (t, t), 0) + (blk - step) * t
        keep = u >= start_ref[0]
        if step == 0:
            keep = keep & (u <= lanes((t, t)) + blk * t)
        bias = jnp.where(keep, 0.0, NEG)
        kv = kv_ref[...]
        kk = place(kv, kvh, 0)
        ones = jnp.where(lax.broadcasted_iota(jnp.int32, (16, t), 0) == 0, 1.0, 0.0)
        vt = jnp.concatenate([flip_head(kv, kvh, PAIR), ones], axis=0).astype(BF16)
        scores = [
            dot_nt(kk[par], q_ref[:, pair * PAIR : (pair + 1) * PAIR]) + bias
            for pair, par in heads
        ]
        for (pair, par), s in zip(heads, scores, strict=True):
            m = jnp.max(s, axis=0, keepdims=True)
            if step:
                old = ml_in[pair, par : par + 1, :]
                m = jnp.maximum(m, old)
            pv = dot(vt, jnp.exp(s - m).astype(BF16))
            acc, l = pv[:HD], pv[HD : HD + 1]
            if step:
                factor = jnp.exp(old - m)
                rows = slice(pair * PAIR + par * HD, pair * PAIR + (par + 1) * HD)
                acc = acc + acc_in[rows, :] * factor
                l = l + ml_in[pair, 2 + par : 3 + par, :] * factor
            finish(pair, par, acc, m, l)

    if step == 0:
        work()
    else:
        pl.when(blk >= step)(work)

        @pl.when(blk < step)
        def _():
            for pair, par in heads:
                rows = slice(pair * PAIR + par * HD, pair * PAIR + (par + 1) * HD)
                m = ml_in[pair, par : par + 1, :]
                finish(pair, par, acc_in[rows, :], m, ml_in[pair, 2 + par : 3 + par, :])


def attend(step, last, sc, q, kv, start, state, rows, deps=()):
    n, qw = q.shape
    t = n // rows
    pairs = qw // PAIR
    kv_heads = kv.shape[1] // 2 // HD
    ppk = pairs // kv_heads
    accspec = pl.BlockSpec((ppk * PAIR, t), lambda r, k, *_: (k, r))
    mlspec = pl.BlockSpec((ppk, 8, t), lambda r, k, *_: (k, 0, r))
    work = n * t * qw
    return launch(
        functools.partial(attend_kernel, step, last, ppk),
        (sc, in_hbm(q), in_hbm(kv), in_hbm(start), *state),
        prefetch=1,
        grid=(rows, kv_heads),
        in_specs=[
            pl.BlockSpec((t, ppk * PAIR), lambda r, k, *_: (r, k)),
            pl.BlockSpec((t, kv.shape[1]), lambda r, k, *_: (r, 0)),
            pl.BlockSpec((1, 1, t), lambda r, k, *_: (r, 0, 0)),
        ]
        + ([accspec, mlspec] if state else []),
        out_specs=[accspec, mlspec],
        out_shape=[
            jax.ShapeDtypeStruct((qw, n), F32),
            jax.ShapeDtypeStruct((pairs, 8, n), F32),
        ],
        mib=28,
        estimate=cost(24 * work, 20 * n * qw, n * t * qw // HD),
        name=f"attend{step}",
        deps=deps,
        pin_in=False,
        pin_out=False,
    )


def flip_kernel(x, out):
    out[...] = x[...].T.astype(BF16)


def flip(x, name="flip"):
    w, n = x.shape
    by_rows = w > n
    step = 512 if max(w, n) % 512 == 0 else max(w, n)
    across = pl.BlockSpec((step, n) if by_rows else (w, step), lambda i: (i, 0) if by_rows else (0, i))
    down = pl.BlockSpec((n, step) if by_rows else (step, w), lambda i: (0, i) if by_rows else (i, 0))
    return launch(
        flip_kernel,
        (x,),
        grid=(max(w, n) // step,),
        in_specs=[across],
        out_specs=[down],
        out_shape=[jax.ShapeDtypeStruct((n, w), BF16)],
        mib=32,
        estimate=cost(8 * n * w, 6 * n * w),
        name=name,
        pin_in=False,
    )[0]


def attend_back_kernel(step, first, last, ppk, sc, q_ref, do_ref, ml_ref, start_ref, kv_ref, *refs):
    refs = list(refs)
    o_ref = refs.pop(0) if first else None
    dq_in, delta_in = (None, None) if first else (refs.pop(0), refs.pop(0))
    cos, sin = (refs.pop(0), refs.pop(0)) if last else (None, None)
    dq_out, dkv_out = refs.pop(0), refs.pop(0)
    delta_out = refs.pop(0) if first else None
    dk_acc, dv_acc, dq_acc = refs
    t = q_ref.shape[0]
    kvh = pl.program_id(1)
    blk = sc[0]
    heads = [(pair, par) for pair in range(ppk) for par in range(2)]

    if first:
        for pair in range(ppk):
            both = slice(pair * PAIR, (pair + 1) * PAIR)
            prod = (do_ref[:, both].astype(F32) * o_ref[:, both].astype(F32)).T
            for par in range(2):
                delta_out[pair, par : par + 1, :] = jnp.sum(
                    prod[par * HD : (par + 1) * HD, :], axis=0, keepdims=True
                )
        dq_acc[...] = jnp.zeros_like(dq_acc)
    else:
        dq_acc[...] = dq_in[...]
    delta = delta_out if first else delta_in

    @pl.when(kvh == 0)
    def _():
        dkv_out[...] = jnp.zeros_like(dkv_out)

    def work():
        u = lax.broadcasted_iota(jnp.int32, (t, t), 0) + (blk - step) * t
        keep = u >= start_ref[0]
        if step == 0:
            keep = keep & (u <= lanes((t, t)) + blk * t)
        bias = jnp.where(keep, 0.0, NEG)
        kv = kv_ref[...]
        kk = place(kv, kvh, 0)
        vv = place(kv, kvh, PAIR)
        kt = flip_head(kv, kvh, 0).astype(BF16)
        dk_acc[...] = jnp.zeros_like(dk_acc)
        dv_acc[...] = jnp.zeros_like(dv_acc)
        for pair, par in heads:
            q = q_ref[:, pair * PAIR : (pair + 1) * PAIR]
            do = do_ref[:, pair * PAIR : (pair + 1) * PAIR]
            st = dot_nt(kk[par], q) + bias
            dp = dot_nt(vv[par], do)
            pt = jnp.exp(st - ml_ref[pair, par : par + 1, :])
            ds = (pt * (dp - delta[pair, par : par + 1, :])).astype(BF16)
            dv_acc[par] += dot(pt.astype(BF16), do)
            dk_acc[par] += dot(ds, q)
            rows = slice(pair * PAIR + par * HD, pair * PAIR + (par + 1) * HD)
            dq_acc[rows, :] += dot(kt, ds)
        low = lanes((t, PAIR)) < HD
        for acc, base in ((dk_acc, 0), (dv_acc, PAIR)):
            both = acc[0] + pltpu.roll(acc[1], HD, 1)
            here = jnp.where(kvh == 0, both, pltpu.roll(both, HD, 1))
            mine = low == (kvh == 0)
            old = dkv_out[:, base : base + PAIR].astype(F32)
            dkv_out[:, base : base + PAIR] = jnp.where(mine, here, old).astype(BF16)

    if step == 0:
        work()
    else:
        pl.when(blk >= step)(work)

    if last:
        for pair in range(ppk):
            rows = slice(pair * PAIR, (pair + 1) * PAIR)
            dq = (dq_acc[rows, :] * (HD**-0.5)).T
            dq_out[:, rows] = turn(dq, cos[...], -sin[...]).astype(BF16)
    else:
        dq_out[...] = dq_acc[...]


def attend_back(step, first, last, sc, q, do, o, ml, start, cos, sin, kv, state, rows, deps=()):
    n, qw = q.shape
    t = n // rows
    pairs = qw // PAIR
    kvw = kv.shape[1]
    kv_heads = kvw // 2 // HD
    ppk = pairs // kv_heads
    width = ppk * PAIR
    pairspec = pl.BlockSpec((t, width), lambda r, k, *_: (r, k))
    accspec = pl.BlockSpec((width, t), lambda r, k, *_: (k, r))
    mlspec = pl.BlockSpec((ppk, 8, t), lambda r, k, *_: (k, 0, r))
    rowspec = lambda w: pl.BlockSpec((t, w), lambda r, k, *_: (r, 0))
    work = n * t * qw
    return launch(
        functools.partial(attend_back_kernel, step, first, last, ppk),
        (sc, q, do, ml, start, kv)
        + ((o,) if first else tuple(state))
        + ((cos, sin) if last else ()),
        prefetch=1,
        grid=(rows, kv_heads),
        in_specs=[pairspec, pairspec, mlspec]
        + [pl.BlockSpec((1, 1, t), lambda r, k, *_: (r, 0, 0))]
        + [rowspec(kvw)]
        + ([pairspec] if first else [accspec, mlspec])
        + ([rowspec(PAIR)] * 2 if last else []),
        out_specs=[pairspec if last else accspec, rowspec(kvw)] + ([mlspec] if first else []),
        scratch=[
            pltpu.VMEM((2, t, PAIR), F32),
            pltpu.VMEM((2, t, PAIR), F32),
            pltpu.VMEM((width, t), F32),
        ],
        out_shape=[
            jax.ShapeDtypeStruct((n, qw), BF16) if last else jax.ShapeDtypeStruct((qw, n), F32),
            jax.ShapeDtypeStruct((n, kvw), BF16),
        ]
        + ([jax.ShapeDtypeStruct((pairs, 8, n), F32)] if first else []),
        mib=40,
        estimate=cost(54 * work, 20 * n * qw, work // HD),
        name=f"attend_back{step}",
        deps=deps,
    )


def gather_dkv_kernel(count, *refs):
    parts = refs[:count]
    cos, sin, out = refs[count:]
    total = parts[0][...].astype(F32)
    for x in parts[1:]:
        total = total + x[...].astype(F32)
    half = total.shape[1] // 2
    out[:, :half] = turn(total[:, :half], cos[...], -sin[...]).astype(BF16)
    out[:, half:] = total[:, half:].astype(BF16)


def gather_dkv(parts, cos, sin, deps=()):
    whole = lambda x: pl.BlockSpec(x.shape, lambda i: (0, 0))
    return launch(
        functools.partial(gather_dkv_kernel, len(parts)),
        (*parts, cos, sin),
        grid=(1,),
        in_specs=[whole(x) for x in (*parts, cos, sin)],
        out_specs=[whole(parts[0])],
        out_shape=[jax.ShapeDtypeStruct(parts[0].shape, BF16)],
        mib=32,
        estimate=cost(10 * parts[0].size, 4 * len(parts) * parts[0].size),
        name="gather_dkv",
        deps=deps,
    )[0]


def own_part_kernel(o_own, w_own, out):
    out[0] = dot_nt(o_own[...], w_own[...])


def own_part(o_own, w_own):
    n, e = o_own.shape
    d = w_own.shape[0]
    dt = 512
    return launch(
        own_part_kernel,
        (o_own, w_own),
        grid=(d // dt,),
        in_specs=[
            pl.BlockSpec((n, e), lambda i: (0, 0), pipeline_mode=pl.Buffered(1)),
            pl.BlockSpec((dt, e), lambda i: (i, 0)),
        ],
        out_specs=[pl.BlockSpec((1, n, dt), lambda i: (i, 0, 0))],
        out_shape=[jax.ShapeDtypeStruct((d // dt, n, dt), F32)],
        mib=40,
        estimate=cost(n * d * e, 2 * d * e),
        name="own_part",
    )[0]


def merge_kernel(part, o_oth, w_oth, full, gain, h1, a2, a2_t, r2, ssa, held, sums):
    i = pl.program_id(0)
    attn = part[0] + dot_nt(o_oth[...], w_oth[...])
    x = full[...].astype(F32) + attn
    h1[0] = x
    held[i] = x

    @pl.when(i == 0)
    def _():
        sums[...] = jnp.zeros_like(sums)
        ssa[...] = jnp.zeros_like(ssa)

    sums[...] += jnp.sum(x * x, axis=1, keepdims=True)
    ssa[...] += jnp.sum(attn * attn, axis=1, keepdims=True)

    @pl.when(i == pl.num_programs(0) - 1)
    def _():
        count, _, dt = held.shape
        inv = lax.rsqrt(sums[...] * (1.0 / (count * dt)) + EPS)
        r2[...] = inv
        for j in range(count):
            at = slice(j * dt, (j + 1) * dt)
            act = (held[j] * inv[:, :1] * gain[:, at]).astype(BF16)
            a2[:, at] = act
            a2_t[at, :] = act.T


def merge(part, o_oth, w_oth, full, gain, deps=()):
    n, d = full.shape
    dt = 512
    e = o_oth.shape[1]
    const = lambda a: pl.BlockSpec(a.shape, lambda i: (0, 0), pipeline_mode=pl.Buffered(1))
    return launch(
        merge_kernel,
        (part, o_oth, w_oth, full, gain),
        grid=(d // dt,),
        in_specs=[
            pl.BlockSpec((1, n, dt), lambda i: (i, 0, 0)),
            const(o_oth),
            pl.BlockSpec((dt, e), lambda i: (i, 0)),
            pl.BlockSpec((n, dt), lambda i: (0, i)),
            const(gain),
        ],
        out_specs=[
            pl.BlockSpec((1, n, dt), lambda i: (i, 0, 0)),
            pl.BlockSpec((n, d), lambda i: (0, 0)),
            pl.BlockSpec((d, n), lambda i: (0, 0)),
            pl.BlockSpec((n, PAIR), lambda i: (0, 0)),
            pl.BlockSpec((n, PAIR), lambda i: (0, 0)),
        ],
        out_shape=[
            jax.ShapeDtypeStruct((d // dt, n, dt), F32),
            jax.ShapeDtypeStruct((n, d), BF16),
            jax.ShapeDtypeStruct((d, n), BF16),
            jax.ShapeDtypeStruct((n, PAIR), F32),
            jax.ShapeDtypeStruct((n, PAIR), F32),
        ],
        scratch=[pltpu.VMEM((d // dt, n, dt), F32), pltpu.VMEM((n, PAIR), F32)],
        mib=48,
        estimate=cost(3 * n * d * d, 2 * d * d + 12 * n * d),
        name="merge",
        deps=deps,
    )


def units_kernel(a2, g, wg, wu, wd, out):
    gate = dot(a2[...], wg[...])
    up = dot(a2[...], wu[...])
    dh = dot(g[...], wd[...])
    sig = jax.nn.sigmoid(gate)
    act = gate * sig
    out[0] = (act * up).astype(BF16)
    out[1] = (dh * up * sig * (1.0 + gate * (1.0 - sig))).astype(BF16)
    out[2] = (dh * act).astype(BF16)


def units(a2, g, wg, wu, wd, first, count, deps=()):
    n, d = a2.shape
    const = pl.BlockSpec((n, d), lambda i: (0, 0), pipeline_mode=pl.Buffered(1))
    wspec = pl.BlockSpec((d, FT), lambda i: (0, first + i))
    return launch(
        units_kernel,
        (a2, g, wg, wu, wd),
        grid=(count,),
        in_specs=[const, const, wspec, wspec, wspec],
        out_specs=[pl.BlockSpec((3, n, FT), lambda i: (0, 0, i))],
        out_shape=[jax.ShapeDtypeStruct((3, n, count * FT), BF16)],
        mib=58,
        estimate=cost(10 * n * d * FT * count, 6 * d * FT * count, n * FT * count),
        name=f"units{first}",
        deps=deps,
    )[0]


def exchange_kernel(count, tiles, nblk, *refs):
    acts = refs[: 3 * count]
    wg, wu, wd, early, total, branch, shares = refs[3 * count : 3 * count + 7]
    mine, theirs, send_sem, recv_sem, z_send, z_recv, own_sem = refs[3 * count + 7 :]
    i = pl.program_id(0)
    other = 1 - lax.axis_index("head")
    blk = lax.axis_index("blk")
    rows = early.shape[0] // nblk

    def copy(j):
        return pltpu.make_async_remote_copy(
            src_ref=mine.at[j],
            dst_ref=theirs.at[j],
            send_sem=send_sem.at[j],
            recv_sem=recv_sem.at[j],
            device_id={"head": other},
            device_id_type=pl.DeviceIdType.MESH,
        )

    def block(b):
        return early.at[pl.ds(pl.multiple_of(b * rows, rows), rows), :]

    def share(k):
        to = lax.rem(blk + k, nblk)
        return pltpu.make_async_remote_copy(
            src_ref=block(to),
            dst_ref=shares.at[blk],
            send_sem=z_send.at[k],
            recv_sem=z_recv.at[k],
            device_id={"blk": to},
            device_id_type=pl.DeviceIdType.MESH,
        )

    def keep():
        return pltpu.make_async_copy(block(blk), shares.at[blk], own_sem)

    def product(m, weight):
        out, at = None, 0
        for act in acts[m * count : (m + 1) * count]:
            term = dot_nt(act[0], weight[:, at : at + act.shape[2]])
            out = term if out is None else out + term
            at += act.shape[2]
        return out

    @pl.when(i == 0)
    def _():
        barrier = pltpu.get_barrier_semaphore()
        pl.semaphore_signal(
            barrier, inc=1, device_id={"head": other}, device_id_type=pl.DeviceIdType.MESH
        )
        for k in range(1, nblk):
            pl.semaphore_signal(
                barrier,
                inc=1,
                device_id={"blk": lax.rem(blk + k, nblk)},
                device_id_type=pl.DeviceIdType.MESH,
            )
        pl.semaphore_wait(barrier, nblk)
        for k in range(1, nblk):
            share(k).start()
        keep().start()

    @pl.when(i < tiles)
    def _():
        mine[i] = (product(1, wg) + product(2, wu)).astype(BF16)
        copy(i).start()

    @pl.when(i >= tiles)
    def _():
        branch[0] = product(0, wd).astype(BF16)

    @pl.when(i == 2 * tiles - 1)
    def _():
        width = mine.shape[2]
        for j in range(tiles):
            copy(j).wait()
            total[:, j * width : (j + 1) * width] = mine[j].astype(F32) + theirs[j].astype(F32)
        for k in range(1, nblk):
            share(k).wait()
        keep().wait()


def exchange(stacks, wg, wu, wd, early, nblk, name):
    n = stacks[0].shape[1]
    d, ff = wg.shape
    dt = 256
    tiles = d // dt
    per = tiles // 2
    acts = [x for _ in range(3) for x in stacks]
    specs = [
        pl.BlockSpec((1,) + x.shape[1:], lambda i, m=m: (m, 0, 0), pipeline_mode=pl.Buffered(1))
        for m in range(3)
        for x in stacks
    ]
    first = pl.BlockSpec((dt, ff), lambda i: (jnp.minimum(i, tiles - 1), 0))
    second = pl.BlockSpec((dt, ff), lambda i: (jnp.maximum(i - tiles, 0), 0))
    place_hbm = pl.BlockSpec(memory_space=pltpu.HBM)

    def branch_at(i):
        j = jnp.maximum(i - tiles, 0)
        return (j // per, 0, j % per)

    return launch(
        functools.partial(exchange_kernel, len(stacks), tiles, nblk),
        (*acts, wg, wu, wd, early),
        grid=(2 * tiles,),
        in_specs=specs + [first, first, second, place_hbm],
        out_specs=[
            pl.BlockSpec((n, d), lambda i: (0, 0)),
            pl.BlockSpec((1, n, dt), branch_at),
            place_hbm,
        ],
        out_shape=[
            jax.ShapeDtypeStruct((n, d), F32),
            jax.ShapeDtypeStruct((2, n, d // 2), BF16),
            jax.ShapeDtypeStruct((nblk, early.shape[0] // nblk, early.shape[1]), BF16),
        ],
        scratch=[
            pltpu.VMEM((tiles, n, dt), BF16),
            pltpu.VMEM((tiles, n, dt), BF16),
            pltpu.SemaphoreType.DMA((tiles,)),
            pltpu.SemaphoreType.DMA((tiles,)),
            pltpu.SemaphoreType.DMA((nblk,)),
            pltpu.SemaphoreType.DMA((nblk,)),
            pltpu.SemaphoreType.DMA,
        ],
        mib=58,
        estimate=cost(6 * n * d * ff, 6 * d * ff),
        name=name,
        collective=1,
    )


def stream_kernel(da_sum, h1, r2, gain, g, w_out, dh1, dattn_t, dout, gsum):
    da = da_sum[...]
    inv = r2[:, :1]
    norm = jnp.concatenate([h1[j] for j in range(h1.shape[0])], axis=1) * inv
    grad = da * norm

    @pl.when(pl.program_id(0) == 0)
    def _():
        gsum[...] = jnp.zeros_like(gsum)

    gsum[...] += jnp.sum(grad, axis=0, keepdims=True)
    e2 = da * gain[...]
    mean = jnp.sum(e2 * norm, axis=1, keepdims=True) * (1.0 / da.shape[1])
    dh = g[...].astype(F32) + inv * (e2 - norm * mean)
    dh1[...] = dh
    low = dh.astype(BF16)
    dattn_t[...] = low.T
    dout[...] = dot(low, w_out[...]).astype(BF16)


def stream(da, h1, r2, gain, g, w_out, deps=()):
    parts, n, dt = h1.shape
    d = parts * dt
    tt = min(n, 128)
    ew = w_out.shape[1]
    row = lambda w: pl.BlockSpec((tt, w), lambda i: (i, 0))
    const = lambda a: pl.BlockSpec(a.shape, lambda i: (0, 0), pipeline_mode=pl.Buffered(1))
    return launch(
        stream_kernel,
        (da, h1, r2, gain, g, w_out),
        grid=(n // tt,),
        in_specs=[
            row(d),
            pl.BlockSpec((parts, tt, dt), lambda i: (0, i, 0)),
            row(PAIR),
            const(gain),
            row(d),
            const(w_out),
        ],
        out_specs=[
            row(d),
            pl.BlockSpec((d, tt), lambda i: (0, i)),
            row(ew),
            pl.BlockSpec((1, d), lambda i: (0, 0)),
        ],
        out_shape=[
            jax.ShapeDtypeStruct((n, d), F32),
            jax.ShapeDtypeStruct((d, n), BF16),
            jax.ShapeDtypeStruct((n, ew), BF16),
            jax.ShapeDtypeStruct((1, d), F32),
        ],
        mib=56,
        estimate=cost(2 * n * d * ew, 2 * d * ew + 20 * n * d),
        name="stream",
        deps=deps,
    )


def entry_kernel(dq, dkv, wq, wk, wv, full, ssx, gain, part, gsum, rsum):
    kvw = wk.shape[1]
    da = dot_nt(dq[...], wq[...])
    da = da + dot_nt(dkv[:, :kvw], wk[...]) + dot_nt(dkv[:, kvw:], wv[...])
    width = pl.num_programs(0) * da.shape[1]
    inv = lax.rsqrt(ssx[:, :1] * (1.0 / width) + EPS)
    grad = da * (full[...].astype(F32) * inv)
    gsum[...] = jnp.sum(grad, axis=0, keepdims=True)

    @pl.when(pl.program_id(0) == 0)
    def _():
        rsum[...] = jnp.zeros_like(rsum)

    rsum[...] += jnp.sum(grad * gain[...], axis=1, keepdims=True)
    part[0] = da.astype(BF16)


def entry(dq, dkv, wq, wk, wv, full, ssx, gain):
    n, d = full.shape
    dt = 256
    per = d // 2 // dt
    const = lambda a: pl.BlockSpec(a.shape, lambda i: (0, 0), pipeline_mode=pl.Buffered(1))
    wspec = lambda w: pl.BlockSpec((dt, w.shape[1]), lambda i: (i, 0))
    return launch(
        entry_kernel,
        (dq, dkv, wq, wk, wv, full, ssx, gain),
        grid=(d // dt,),
        in_specs=[const(dq), const(dkv), wspec(wq), wspec(wk), wspec(wv)]
        + [
            pl.BlockSpec((n, dt), lambda i: (0, i)),
            const(ssx),
            pl.BlockSpec((1, dt), lambda i: (0, i)),
        ],
        out_specs=[
            pl.BlockSpec((1, n, dt), lambda i: (i // per, 0, i % per)),
            pl.BlockSpec((1, dt), lambda i: (0, i)),
            pl.BlockSpec((n, PAIR), lambda i: (0, 0)),
        ],
        out_shape=[
            jax.ShapeDtypeStruct((2, n, d // 2), BF16),
            jax.ShapeDtypeStruct((1, d), F32),
            jax.ShapeDtypeStruct((n, PAIR), F32),
        ],
        mib=56,
        estimate=cost(2 * n * d * (wq.shape[1] + 2 * wk.shape[1]), 20 * n * d),
        name="entry",
    )


def outer_kernel(shares, count, parts, adds, spread, sc, *refs):
    k = 0
    lefts, rights = [], []
    for share in shares:
        lefts.append((refs[k : k + count], refs[k + count : k + 2 * count]))
        k += 2 * count
        rights.append([(refs[k + 2 * i], refs[k + 2 * i + 1]) for i in range(share)])
        k += 2 * share
    got = refs[k] if adds else None
    outs = refs[k + adds :]

    def work(out):
        m = 0
        for (left_own, left_oth), group in zip(lefts, rights, strict=True):
            rows = left_own[0].shape[0]
            for own, oth in group:
                at = slice(m * FT, (m + 1) * FT)
                for i in range(count):
                    part = slice(i * rows, (i + 1) * rows)
                    total = dot(left_own[i][...], own[0]) + dot(left_oth[i][...], oth[0])
                    if adds:
                        total = total + got[part, at].astype(F32)
                    if spread == 1:
                        out[part, at] = total.astype(BF16)
                    else:
                        size = rows // spread
                        for b in range(spread):
                            to = slice((b * count + i) * size, (b * count + i + 1) * size)
                            out[to, at] = total[b * size : (b + 1) * size, :].astype(BF16)
                m += 1

    if len(parts) == 1:
        work(outs[0])
        return
    step = pl.program_id(0)
    start = 0
    for out, size in zip(outs, parts, strict=True):
        pl.when((step >= start) & (step < start + size))(functools.partial(work, out))
        start += size


def outer(sc, groups, rows, first, parts, name, got=None, deps=(), spread=1):
    n = groups[0][0].shape[1]
    count = sc.shape[0]
    number = sum(parts)
    shares = tuple(len(g[2]) for g in groups)
    ins, specs = [], []
    for own, oth, rights in groups:
        ins += [own] * count + [oth] * count
        for i in range(count):
            specs.append(pl.BlockSpec((rows, n), lambda j, s, i=i: (s[i], 0)))
        specs += specs[-count:]
        for r_own, r_oth, at in rights:
            ins += [r_own, r_oth]
            specs += [pl.BlockSpec((1, n, FT), lambda i, s, at=at: (at, 0, first + i))] * 2
    members = sum(shares)
    height = count * rows
    ospecs, start = [], 0
    for size in parts:
        ospecs.append(
            pl.BlockSpec(
                (height, members * FT),
                lambda i, s, start=start, size=size: (0, jnp.clip(i - start, 0, size - 1)),
            )
        )
        start += size
    if got is not None:
        ins.append(got)
        specs.append(ospecs[0])
    c = number * FT
    return launch(
        functools.partial(outer_kernel, shares, count, tuple(parts), int(got is not None), spread),
        (sc, *ins),
        prefetch=1,
        grid=(number,),
        in_specs=specs,
        out_specs=ospecs,
        out_shape=[jax.ShapeDtypeStruct((height, members * size * FT), BF16) for size in parts],
        mib=48,
        estimate=cost(8 * n * height * c * members, members * c * (4 * n + 2 * height)),
        name=name,
        deps=deps,
    )


def finish_kernel(count, *refs):
    parts = refs[:count]
    outs = refs[count:]
    at = 0
    for part in parts:
        for tile in range(part.shape[2] // (3 * FT)):
            for m in range(3):
                columns = slice((3 * tile + m) * FT, (3 * tile + m + 1) * FT)
                total = part[0, :, columns].astype(F32)
                for b in range(1, part.shape[0]):
                    total = total + part[b, :, columns].astype(F32)
                outs[m][:, at : at + FT] = total
            at += FT


def finish(parts):
    parts = [x.reshape(count, x.shape[0] // count, x.shape[1]) for x, count in parts]
    rows = parts[0].shape[1]
    width = sum(x.shape[2] for x in parts) // 3
    whole = lambda shape: pl.BlockSpec(shape, lambda i: (0,) * len(shape))
    return launch(
        functools.partial(finish_kernel, len(parts)),
        tuple(parts),
        grid=(1,),
        in_specs=[whole(x.shape) for x in parts],
        out_specs=[whole((rows, width))] * 3,
        out_shape=[jax.ShapeDtypeStruct((rows, width), F32)] * 3,
        mib=48,
        estimate=cost(0, 8 * parts[0].shape[0] * rows * width),
        name="finish",
    )


def finish_rows_kernel(shares, *outs):
    at = 0
    for out in outs[:-1]:
        columns = slice(at, at + out.shape[1])
        total = shares[0, :, columns].astype(F32)
        for b in range(1, shares.shape[0]):
            total = total + shares[b, :, columns].astype(F32)
        out[...] = total
        at += out.shape[1]
    total = shares[0, :, at:].astype(F32)
    for b in range(1, shares.shape[0]):
        total = total + shares[b, :, at:].astype(F32)
    outs[-1][...] = total.T


def finish_rows(shares, widths):
    _, rows, columns = shares.shape
    left = columns - sum(widths)
    whole = lambda shape: pl.BlockSpec(shape, lambda i: (0,) * len(shape))
    shapes = [(rows, w) for w in widths] + [(left, rows)]
    return launch(
        finish_rows_kernel,
        (shares,),
        grid=(1,),
        in_specs=[whole(shares.shape)],
        out_specs=[whole(x) for x in shapes],
        out_shape=[jax.ShapeDtypeStruct(x, F32) for x in shapes],
        mib=32,
        estimate=cost(0, 4 * shares.size),
        name="finish_rows",
    )


def body(
    inputs,
    cotangent,
    lengths,
    attn_gain,
    w_query,
    w_key,
    w_value,
    w_out,
    mlp_gain,
    gate_weight,
    up_weight,
    down_weight,
):
    t, rows, half = inputs.shape
    n = t * rows
    heads = lax.axis_size("head")
    nblk = lax.axis_size("blk")
    ndp = lax.axis_size("dp")
    d = half * heads
    h = lax.axis_index("head").astype(jnp.int32)
    blk = lax.axis_index("blk").astype(jnp.int32)
    dp = lax.axis_index("dp").astype(jnp.int32)
    sc_h = h.reshape(1)
    sc_blk = blk.reshape(1)

    def flat(x):
        return jnp.transpose(x, (1, 0, 2)).reshape(n, x.shape[2])

    def unflat(x):
        return jnp.transpose(x.reshape(rows, t, x.shape[1]), (1, 0, 2))

    x_own = flat(inputs)
    g_own = flat(cotangent)
    gain_one = attn_gain.astype(F32).reshape(1, d)
    gain_two = mlp_gain.astype(F32).reshape(1, d)

    pos = blk * t + jnp.arange(t, dtype=jnp.int32)
    ends = jnp.cumsum(lengths, axis=1)
    passed = ends[:, None, :] <= pos[None, :, None]
    start = jnp.max(jnp.where(passed, ends[:, None, :], 0), axis=2)
    valid = (jnp.sum(passed.astype(jnp.int32), axis=2) < DOCS).astype(F32).reshape(n)
    start_rows = start.reshape(rows, 1, t)
    freq = jnp.power(THETA, -2.0 * jnp.arange(HD // 2, dtype=F32) / HD)
    angles = pos.astype(F32)[:, None] * freq[None, :]
    cos_h, sin_h = jnp.cos(angles), jnp.sin(angles)
    cos = jnp.tile(jnp.concatenate([cos_h, cos_h, cos_h, cos_h], axis=1), (rows, 1))
    sin = jnp.tile(jnp.concatenate([-sin_h, sin_h, -sin_h, sin_h], axis=1), (rows, 1))

    CHAIN.clear()
    WEIGHT[0] = EARLY

    def tie(x, *also):
        return lax.optimization_barrier((x, *also))[0]

    def by_head(x):
        return jnp.where(h == 0, x[:, :half], x[:, half:])

    def gate(x):
        x, CHAIN[0] = lax.optimization_barrier((x, CHAIN[0]))
        return x

    def mate(x):
        return swap(x, "dp", 1)

    x_oth = swap(x_own, "head", 1)
    share = w_out.shape[0] // ndp
    piece = lax.dynamic_slice_in_dim(w_out, dp * share, share, 0)
    x_oth, piece, g_own, cos, sin, start_rows = lax.optimization_barrier(
        (x_oth, piece, g_own, cos, sin, start_rows)
    )
    piece = swap(piece, "head", 1)
    full, a_one, queries, kv, ssx = project(
        sc_h, x_own, x_oth, gain_one, w_query, w_key, w_value, cos, sin
    )

    kvs, state = [kv], ()
    for s in range(nblk):
        if s + 1 < nblk:
            steps = [(i, i + 1) for i in range(s, nblk - 1)]
            kvs.append(lax.ppermute(kvs[s], "blk", steps))
        state = attend(s, s == nblk - 1, sc_blk, queries, kvs[s], start_rows, state, rows)
        if s + 1 < nblk - 1:
            kvs[s + 1] = gate(kvs[s + 1])
        if s == 0:
            a_one_t = flip(a_one, "flip_a")
            piece = gate(piece)
            w_out_oth = lax.all_gather(piece, "dp", axis=0, tiled=True)
            g_own, piece = lax.optimization_barrier((g_own, piece))
            g_oth = swap(g_own, "head", 1)
    acc, ml = state
    o_own = flip(acc)
    o_oth = swap(o_own, "head", 1)
    part_own = own_part(o_own, w_out)
    g_full = jnp.concatenate(
        [jnp.where(h == 0, g_own, g_oth), jnp.where(h == 0, g_oth, g_own)], axis=1
    )
    g_t = flip(g_full, "flip_g")
    o_mate, g_mate = mate(o_own), mate(g_t)
    h_one, a_two, a_two_t, inv_two, ssa = merge(
        part_own, o_oth, w_out_oth, full, gain_two
    )
    a_two_mate = mate(a_two_t)

    low_bit = dp & 1
    block_rows = d // ndp
    sc_send = (dp ^ 2).reshape(1)
    sc_keep = dp.reshape(1)
    sc_both = jnp.stack([2 * i + low_bit for i in range(ndp // 2)])
    y_groups = [[0, 2], [1, 3]]

    def both_halves(groups, parts, name, deps=()):
        return [
            lax.psum_scatter(
                x, "dp", scatter_dimension=0, axis_index_groups=y_groups, tiled=True
            )
            for x in outer(sc_both, groups, block_rows, 0, parts, name, deps=deps)
        ]

    def over_blk(x):
        return lax.all_to_all(x, "blk", split_axis=0, concat_axis=0, tiled=True)

    tiles = gate_weight.shape[1] // FT
    size_a = max(1, tiles // 5)
    size_b = (tiles - size_a + 1) // 3
    size_c = tiles - size_a - size_b

    def unit_part(first, count, deps=()):
        x = units(a_two, g_full, gate_weight, up_weight, down_weight, first, count, deps)
        x_mate = mate(x)
        return x, [
            (g_t, g_mate, [(x, x_mate, 0)]),
            (a_two_t, a_two_mate, [(x, x_mate, 1), (x, x_mate, 2)]),
        ]

    part_a, groups_a = unit_part(0, size_a)
    (sum0,) = both_halves(groups_a, (size_a,), "mlp0")
    part_b, groups_b = unit_part(size_a, size_b)
    part_c, groups_c = unit_part(size_a + size_b, size_c)
    (sum1,) = both_halves(groups_b, (size_b,), "mlp1")

    da, branch, all0 = exchange(
        [part_a, part_b, part_c], gate_weight, up_weight, down_weight, sum0, nblk, "exchange"
    )
    WEIGHT[0] = LATE
    sum2, sum3 = both_halves(groups_c, (size_c - size_c // 2, size_c // 2), "mlp2")
    all1 = over_blk(gate(sum1))
    dh_one, d_attn_t, d_out, gain_two_sum = stream(
        da, h_one, inv_two, gain_two, g_full, w_out
    )
    d_attn_mate, a_one_mate = mate(d_attn_t), mate(gate(a_one_t))
    out_groups = [(d_attn_t, d_attn_mate, [(o_own[None], o_mate[None], 0)])]
    out_parts = (o_own.shape[1] // FT,)
    (first_out,) = outer(
        sc_send, out_groups, block_rows, 0, out_parts, "out_send", deps=(a_one_mate,)
    )
    got_out = swap(first_out, "dp", 2)
    to_other = gate(lax.dynamic_index_in_dim(branch, 1 - h, 0, keepdims=False))
    branch_oth = swap(to_other, "head", 1)

    state, parts = (), []
    for s in reversed(range(nblk)):
        out = attend_back(
            s, s == nblk - 1, s == 0, sc_blk, queries, d_out, o_own, ml, start_rows, cos, sin,
            kvs[s], state, rows, deps=(),
        )
        state = (out[0], out[2] if s == nblk - 1 else state[1])
        part = out[1]
        parts.append(
            lax.ppermute(part, "blk", [(i, i - s) for i in range(s, nblk)]) if s else part
        )
        if s == min(1, nblk - 1):
            (keep_out,) = outer(
                sc_keep, out_groups, block_rows, 0, out_parts, "out_keep", got_out,
                deps=(all1,) + tuple(parts[: nblk - 1]),
            )
            all2 = over_blk(gate(sum2))
    d_q = state[0]
    d_kv_own = gather_dkv(parts, cos, sin)
    d_qkv = jnp.concatenate([d_q, d_kv_own], axis=1)
    d_qkv_mate = mate(d_qkv)
    d_part, gain_one_sum, row_sum = entry(
        d_q, d_kv_own, w_query, w_key, w_value, full, ssx, gain_one
    )
    qkv_groups = [(a_one_t, a_one_mate, [(d_qkv[None], d_qkv_mate[None], 0)])]
    qkv_parts = (d_qkv.shape[1] // FT,)
    (first_qkv,) = outer(sc_send, qkv_groups, block_rows, 0, qkv_parts, "qkv_send")
    got_qkv = swap(first_qkv, "dp", 2)
    sum3 = lax.psum_scatter(gate(sum3), "blk", scatter_dimension=0, tiled=True)
    d_send = lax.dynamic_index_in_dim(d_part, 1 - h, 0, keepdims=False)
    d_send, row_sum, gain_one_sum, CHAIN[0] = lax.optimization_barrier(
        (d_send, row_sum, gain_one_sum, CHAIN[0])
    )
    h_late, branch_late = gate(h_one), gate(branch)
    h_half = jnp.concatenate(
        [
            jnp.where(h == 0, h_late[i], h_late[i + h_late.shape[0] // 2])
            for i in range(h_late.shape[0] // 2)
        ],
        axis=1,
    )
    mlp_half = lax.dynamic_index_in_dim(branch_late, h, 0, keepdims=False).astype(F32) + (
        branch_oth.astype(F32)
    )
    output = unflat((h_half + mlp_half).astype(BF16))
    d_other = swap(d_send, "head", 1)
    row_total = row_sum + swap(row_sum, "head", 1)
    (keep_qkv,) = outer(
        sc_keep, qkv_groups, block_rows, 0, qkv_parts, "qkv_keep", got_qkv, deps=(all2, branch_oth)
    )
    per_head = 1.0 / heads
    tail = jnp.stack(
        [
            jnp.sum(valid) * per_head,
            jnp.sum(valid * ssx[:, 0]) * per_head,
            jnp.sum(valid * ssa[:, 0]) * per_head,
            jnp.sum(valid[:, None] * mlp_half * mlp_half),
        ]
    )
    small = jnp.concatenate(
        [gain_one_sum[0], gain_two_sum[0] * per_head, tail, jnp.zeros((PAIR - 4,), F32)]
    ).reshape(-1, PAIR)
    for axis in ("head", "dp"):
        for i in range(lax.axis_size(axis).bit_length() - 1):
            small = small + swap(small, axis, 1 << i)
    small = small.reshape(-1)
    mine = [
        lax.dynamic_slice_in_dim(small, at + dp * block_rows, block_rows, 0)[:, None]
        for at in (0, d)
    ]
    sums4 = jnp.broadcast_to(small[None, 2 * d : 2 * d + 4], (block_rows, 4))
    exact = jnp.concatenate(mine + [sums4], axis=1)
    coarse = exact.astype(BF16)
    fine = (exact - coarse.astype(F32)).astype(BF16)
    extra = jnp.concatenate(
        [coarse, fine, jnp.zeros((block_rows, PAIR - 12), BF16)], axis=1
    )
    all_qkv = over_blk(jnp.concatenate([keep_qkv, keep_out, extra], axis=1))
    grad_down, grad_gate, grad_up = finish([(all0.reshape(-1, all0.shape[2]), nblk), (all1, nblk), (all2, nblk), (sum3, 1)])
    qw, kvw = w_query.shape[1], w_key.shape[1]
    sum_query, sum_key, sum_value, sum_out, small = finish_rows(
        all_qkv.reshape(nblk, -1, all_qkv.shape[1]), (qw, kvw, kvw, o_own.shape[1])
    )

    inv_one = lax.rsqrt(ssx[:, :1] * (1.0 / d) + EPS)
    d_one = lax.dynamic_index_in_dim(d_part, h, 0, keepdims=False).astype(F32) + d_other.astype(F32)
    norm_half = x_own.astype(F32) * inv_one
    grad_input = by_head(tie(dh_one, d_other)) + inv_one * (
        d_one * by_head(gain_one) - norm_half * (row_total[:, :1] * (1.0 / d))
    )

    small = small[:6] + small[6:12]
    grad_attn_gain, grad_mlp_gain = small[0], small[1]
    stats = jnp.sqrt(small[3:6, 0] / (small[2, 0] * d))

    return (
        output,
        unflat(grad_input),
        grad_attn_gain,
        sum_query,
        sum_key,
        sum_value,
        sum_out,
        grad_mlp_gain,
        grad_gate,
        grad_up,
        grad_down,
        stats,
    )


def solution(mesh):
    tokens = P("blk", "dp", "head")
    split = P(None, "head")
    in_specs = (tokens, tokens, P("dp", None), P()) + (split,) * 4 + (P(),) + (split,) * 3
    vec, mat = P(("dp", "blk")), P(("dp", "blk"), "head")
    out_specs = (tokens, tokens, vec, mat, mat, mat, mat, vec, mat, mat, mat, P())
    return jax.shard_map(body, mesh=mesh, in_specs=in_specs, out_specs=out_specs, check_vma=False)
```

```python
import functools

import jax
import jax.numpy as jnp
from jax import lax
from jax.experimental import pallas as pl
from jax.experimental.pallas import tpu as pltpu
from jax.sharding import PartitionSpec as P

HD = 64
PAIR = 2 * HD
DOCS = 8
EPS = 1e-05
THETA = 10000.0
NEG = -1e30
F32 = jnp.float32
BF16 = jnp.bfloat16
FT = 256


EARLY, LATE = 0.4, 0.4
WEIGHT = [EARLY]


def params(mib, collective=None):
    if collective is None:
        return pltpu.CompilerParams(vmem_limit_bytes=mib << 20)
    return pltpu.CompilerParams(
        vmem_limit_bytes=mib << 20, collective_id=collective, has_side_effects=True
    )


def cost(flops, byte_count, trans=0):
    return pl.CostEstimate(
        flops=int(flops * WEIGHT[0]),
        bytes_accessed=int(byte_count * WEIGHT[0]),
        transcendentals=int(trans * WEIGHT[0]),
    )


CHAIN = []


def in_hbm(x):
    return pltpu.with_memory_space_constraint(x, pltpu.HBM)


def launch(kernel, args, *, grid, in_specs, out_specs, out_shape, mib, estimate, name, scratch=(), prefetch=0, deps=(), pin_in=True, pin_out=True, collective=None):
    extra = list(CHAIN) + list(deps)
    n_in, n_out = len(args), len(out_shape)

    def wrapped(*refs):
        rest = refs[n_in + len(extra) :]
        kernel(*refs[:n_in], *rest[:n_out], *rest[n_out + 1 :])

    if pin_in:
        args = tuple(args[:prefetch]) + tuple(in_hbm(x) for x in args[prefetch:])
    if pin_out:
        out_shape = [pltpu.HBM(o.shape, o.dtype) for o in out_shape]
    extra = [in_hbm(x) for x in extra]
    *outs, token = pl.pallas_call(
        wrapped,
        grid_spec=pltpu.PrefetchScalarGridSpec(
            num_scalar_prefetch=prefetch,
            grid=grid,
            in_specs=list(in_specs) + [pl.BlockSpec(memory_space=pltpu.HBM)] * len(extra),
            out_specs=list(out_specs) + [pl.BlockSpec(memory_space=pltpu.HBM)],
            scratch_shapes=list(scratch),
        ),
        out_shape=list(out_shape) + [pltpu.HBM((8, 128), F32)],
        compiler_params=params(mib, collective),
        cost_estimate=estimate,
        name=name,
    )(*args, *extra)
    CHAIN[:] = [token]
    return outs


def dot(a, b):
    return jnp.dot(a, b, preferred_element_type=F32)


def dot_nt(a, b):
    return lax.dot_general(a, b, (((1,), (1,)), ((), ())), preferred_element_type=F32)


def dot_tn(a, b):
    return lax.dot_general(a, b, (((0,), (0,)), ((), ())), preferred_element_type=F32)


def swap(x, axis, bit):
    n = lax.axis_size(axis)
    return lax.ppermute(x, axis, [(i, i ^ bit) for i in range(n)])


def lanes(shape):
    return lax.broadcasted_iota(jnp.int32, shape, len(shape) - 1)


def turn(x, cos, sin):
    out = []
    for c in range(x.shape[1] // PAIR):
        v = x[:, c * PAIR : (c + 1) * PAIR]
        low = lanes(v.shape) % HD < HD // 2
        other = jnp.where(low, pltpu.roll(v, PAIR - HD // 2, 1), pltpu.roll(v, HD // 2, 1))
        out.append(v * cos + other * sin)
    return out[0] if len(out) == 1 else jnp.concatenate(out, axis=1)


def project_kernel(h_ref, own, oth, gain, wq, wk, wv, cos, sin, full, a1, q, kv, ssx):
    first = h_ref[0] == 0
    x_own = own[...].astype(F32)
    x_oth = oth[...].astype(F32)
    x = jnp.concatenate(
        [jnp.where(first, x_own, x_oth), jnp.where(first, x_oth, x_own)], axis=1
    )
    width = x.shape[1]
    total = jnp.sum(x * x, axis=1, keepdims=True)
    inv = lax.rsqrt(total * (1.0 / width) + EPS)
    act = (x * inv * gain[...]).astype(BF16)
    full[...] = x.astype(BF16)
    a1[...] = act
    ssx[...] = jnp.broadcast_to(total, ssx.shape)
    q[...] = turn(dot(act, wq[...]), cos[...], sin[...]).astype(BF16) * (HD**-0.5)
    kvw = wk.shape[1]
    kv[:, :kvw] = turn(dot(act, wk[...]), cos[...], sin[...]).astype(BF16)
    kv[:, kvw:] = dot(act, wv[...]).astype(BF16)


def project(h, own, oth, gain, wq, wk, wv, cos, sin):
    n, half = own.shape
    d = 2 * half
    tt = min(n, 256)
    qw, kvw = wq.shape[1], wk.shape[1]
    row = lambda w: pl.BlockSpec((tt, w), lambda i, *_: (i, 0))
    const = lambda a: pl.BlockSpec(a.shape, lambda i, *_: (0, 0), pipeline_mode=pl.Buffered(1))
    return launch(
        project_kernel,
        (h, own, oth, gain, wq, wk, wv, cos, sin),
        prefetch=1,
        grid=(n // tt,),
        in_specs=[row(half), row(half), const(gain), const(wq), const(wk), const(wv)]
        + [row(PAIR), row(PAIR)],
        out_specs=[row(d), row(d), row(qw), row(2 * kvw), row(PAIR)],
        out_shape=[
            jax.ShapeDtypeStruct((n, d), BF16),
            jax.ShapeDtypeStruct((n, d), BF16),
            jax.ShapeDtypeStruct((n, qw), BF16),
            jax.ShapeDtypeStruct((n, 2 * kvw), BF16),
            jax.ShapeDtypeStruct((n, PAIR), F32),
        ],
        mib=32,
        pin_in=False,
        estimate=cost(2 * n * d * (qw + 2 * kvw), 2 * d * (qw + 2 * kvw) + 12 * n * d),
        name="project",
    )


def place(kv, kvh, base):
    x = kv[:, base : base + PAIR].astype(F32)
    x = jnp.where(kvh == 0, x, pltpu.roll(x, HD, 1))
    low = jnp.where(lanes(x.shape) < HD, x, 0.0)
    return low.astype(BF16), pltpu.roll(low, HD, 1).astype(BF16)


def flip_head(kv, kvh, base):
    x = kv[:, base : base + PAIR].astype(F32).T
    return jnp.where(kvh == 0, x[:HD, :], x[HD:, :])


def attend_kernel(step, last, ppk, sc, q_ref, kv_ref, start_ref, *refs):
    refs = list(refs)
    if step:
        acc_in, ml_in = refs[:2]
        refs = refs[2:]
    acc_out, ml_out = refs
    t = q_ref.shape[0]
    kvh = pl.program_id(1)
    blk = sc[0]

    def finish(pair, par, acc, m, l):
        rows = slice(pair * PAIR + par * HD, pair * PAIR + (par + 1) * HD)
        if last:
            acc = acc / l
            m = m + jnp.log(l)
        acc_out[rows, :] = acc
        ml_out[pair, par : par + 1, :] = m
        ml_out[pair, 2 + par : 3 + par, :] = l

    heads = [(pair, par) for pair in range(ppk) for par in range(2)]

    def work():
        u = lax.broadcasted_iota(jnp.int32, (t, t), 0) + (blk - step) * t
        keep = u >= start_ref[0]
        if step == 0:
            keep = keep & (u <= lanes((t, t)) + blk * t)
        bias = jnp.where(keep, 0.0, NEG)
        kv = kv_ref[...]
        kk = place(kv, kvh, 0)
        ones = jnp.where(lax.broadcasted_iota(jnp.int32, (16, t), 0) == 0, 1.0, 0.0)
        vt = jnp.concatenate([flip_head(kv, kvh, PAIR), ones], axis=0).astype(BF16)
        scores = [
            dot_nt(kk[par], q_ref[:, pair * PAIR : (pair + 1) * PAIR]) + bias
            for pair, par in heads
        ]
        for (pair, par), s in zip(heads, scores, strict=True):
            m = jnp.max(s, axis=0, keepdims=True)
            if step:
                old = ml_in[pair, par : par + 1, :]
                m = jnp.maximum(m, old)
            pv = dot(vt, jnp.exp(s - m).astype(BF16))
            acc, l = pv[:HD], pv[HD : HD + 1]
            if step:
                factor = jnp.exp(old - m)
                rows = slice(pair * PAIR + par * HD, pair * PAIR + (par + 1) * HD)
                acc = acc + acc_in[rows, :] * factor
                l = l + ml_in[pair, 2 + par : 3 + par, :] * factor
            finish(pair, par, acc, m, l)

    if step == 0:
        work()
    else:
        pl.when(blk >= step)(work)

        @pl.when(blk < step)
        def _():
            for pair, par in heads:
                rows = slice(pair * PAIR + par * HD, pair * PAIR + (par + 1) * HD)
                m = ml_in[pair, par : par + 1, :]
                finish(pair, par, acc_in[rows, :], m, ml_in[pair, 2 + par : 3 + par, :])


def attend(step, last, sc, q, kv, start, state, rows, deps=()):
    n, qw = q.shape
    t = n // rows
    pairs = qw // PAIR
    kv_heads = kv.shape[1] // 2 // HD
    ppk = pairs // kv_heads
    accspec = pl.BlockSpec((ppk * PAIR, t), lambda r, k, *_: (k, r))
    mlspec = pl.BlockSpec((ppk, 8, t), lambda r, k, *_: (k, 0, r))
    work = n * t * qw
    return launch(
        functools.partial(attend_kernel, step, last, ppk),
        (sc, in_hbm(q), in_hbm(kv), in_hbm(start), *state),
        prefetch=1,
        grid=(rows, kv_heads),
        in_specs=[
            pl.BlockSpec((t, ppk * PAIR), lambda r, k, *_: (r, k)),
            pl.BlockSpec((t, kv.shape[1]), lambda r, k, *_: (r, 0)),
            pl.BlockSpec((1, 1, t), lambda r, k, *_: (r, 0, 0)),
        ]
        + ([accspec, mlspec] if state else []),
        out_specs=[accspec, mlspec],
        out_shape=[
            jax.ShapeDtypeStruct((qw, n), F32),
            jax.ShapeDtypeStruct((pairs, 8, n), F32),
        ],
        mib=28,
        estimate=cost(24 * work, 20 * n * qw, n * t * qw // HD),
        name=f"attend{step}",
        deps=deps,
        pin_in=False,
        pin_out=False,
    )


def flip_kernel(x, out):
    out[...] = x[...].T.astype(BF16)


def flip(x, name="flip"):
    w, n = x.shape
    by_rows = w > n
    step = 512 if max(w, n) % 512 == 0 else max(w, n)
    across = pl.BlockSpec((step, n) if by_rows else (w, step), lambda i: (i, 0) if by_rows else (0, i))
    down = pl.BlockSpec((n, step) if by_rows else (step, w), lambda i: (0, i) if by_rows else (i, 0))
    return launch(
        flip_kernel,
        (x,),
        grid=(max(w, n) // step,),
        in_specs=[across],
        out_specs=[down],
        out_shape=[jax.ShapeDtypeStruct((n, w), BF16)],
        mib=32,
        estimate=cost(8 * n * w, 6 * n * w),
        name=name,
        pin_in=False,
    )[0]


def attend_back_kernel(step, first, last, ppk, sc, q_ref, do_ref, ml_ref, start_ref, kv_ref, *refs):
    refs = list(refs)
    o_ref = refs.pop(0) if first else None
    dq_in, delta_in = (None, None) if first else (refs.pop(0), refs.pop(0))
    cos, sin = (refs.pop(0), refs.pop(0)) if last else (None, None)
    dq_out, dkv_out = refs.pop(0), refs.pop(0)
    delta_out = refs.pop(0) if first else None
    dk_acc, dv_acc, dq_acc = refs
    t = q_ref.shape[0]
    kvh = pl.program_id(1)
    blk = sc[0]
    heads = [(pair, par) for pair in range(ppk) for par in range(2)]

    if first:
        for pair in range(ppk):
            both = slice(pair * PAIR, (pair + 1) * PAIR)
            prod = (do_ref[:, both].astype(F32) * o_ref[:, both].astype(F32)).T
            for par in range(2):
                delta_out[pair, par : par + 1, :] = jnp.sum(
                    prod[par * HD : (par + 1) * HD, :], axis=0, keepdims=True
                )
        dq_acc[...] = jnp.zeros_like(dq_acc)
    else:
        dq_acc[...] = dq_in[...]
    delta = delta_out if first else delta_in

    @pl.when(kvh == 0)
    def _():
        dkv_out[...] = jnp.zeros_like(dkv_out)

    def work():
        u = lax.broadcasted_iota(jnp.int32, (t, t), 0) + (blk - step) * t
        keep = u >= start_ref[0]
        if step == 0:
            keep = keep & (u <= lanes((t, t)) + blk * t)
        bias = jnp.where(keep, 0.0, NEG)
        kv = kv_ref[...]
        kk = place(kv, kvh, 0)
        vv = place(kv, kvh, PAIR)
        kt = flip_head(kv, kvh, 0).astype(BF16)
        dk_acc[...] = jnp.zeros_like(dk_acc)
        dv_acc[...] = jnp.zeros_like(dv_acc)
        for pair, par in heads:
            q = q_ref[:, pair * PAIR : (pair + 1) * PAIR]
            do = do_ref[:, pair * PAIR : (pair + 1) * PAIR]
            st = dot_nt(kk[par], q) + bias
            dp = dot_nt(vv[par], do)
            pt = jnp.exp(st - ml_ref[pair, par : par + 1, :])
            ds = (pt * (dp - delta[pair, par : par + 1, :])).astype(BF16)
            dv_acc[par] += dot(pt.astype(BF16), do)
            dk_acc[par] += dot(ds, q)
            rows = slice(pair * PAIR + par * HD, pair * PAIR + (par + 1) * HD)
            dq_acc[rows, :] += dot(kt, ds)
        low = lanes((t, PAIR)) < HD
        for acc, base in ((dk_acc, 0), (dv_acc, PAIR)):
            both = acc[0] + pltpu.roll(acc[1], HD, 1)
            here = jnp.where(kvh == 0, both, pltpu.roll(both, HD, 1))
            mine = low == (kvh == 0)
            old = dkv_out[:, base : base + PAIR].astype(F32)
            dkv_out[:, base : base + PAIR] = jnp.where(mine, here, old).astype(BF16)

    if step == 0:
        work()
    else:
        pl.when(blk >= step)(work)

    if last:
        for pair in range(ppk):
            rows = slice(pair * PAIR, (pair + 1) * PAIR)
            dq = (dq_acc[rows, :] * (HD**-0.5)).T
            dq_out[:, rows] = turn(dq, cos[...], -sin[...]).astype(BF16)
    else:
        dq_out[...] = dq_acc[...]


def attend_back(step, first, last, sc, q, do, o, ml, start, cos, sin, kv, state, rows, deps=()):
    n, qw = q.shape
    t = n // rows
    pairs = qw // PAIR
    kvw = kv.shape[1]
    kv_heads = kvw // 2 // HD
    ppk = pairs // kv_heads
    width = ppk * PAIR
    pairspec = pl.BlockSpec((t, width), lambda r, k, *_: (r, k))
    accspec = pl.BlockSpec((width, t), lambda r, k, *_: (k, r))
    mlspec = pl.BlockSpec((ppk, 8, t), lambda r, k, *_: (k, 0, r))
    rowspec = lambda w: pl.BlockSpec((t, w), lambda r, k, *_: (r, 0))
    work = n * t * qw
    return launch(
        functools.partial(attend_back_kernel, step, first, last, ppk),
        (sc, q, do, ml, start, kv)
        + ((o,) if first else tuple(state))
        + ((cos, sin) if last else ()),
        prefetch=1,
        grid=(rows, kv_heads),
        in_specs=[pairspec, pairspec, mlspec]
        + [pl.BlockSpec((1, 1, t), lambda r, k, *_: (r, 0, 0))]
        + [rowspec(kvw)]
        + ([pairspec] if first else [accspec, mlspec])
        + ([rowspec(PAIR)] * 2 if last else []),
        out_specs=[pairspec if last else accspec, rowspec(kvw)] + ([mlspec] if first else []),
        scratch=[
            pltpu.VMEM((2, t, PAIR), F32),
            pltpu.VMEM((2, t, PAIR), F32),
            pltpu.VMEM((width, t), F32),
        ],
        out_shape=[
            jax.ShapeDtypeStruct((n, qw), BF16) if last else jax.ShapeDtypeStruct((qw, n), F32),
            jax.ShapeDtypeStruct((n, kvw), BF16),
        ]
        + ([jax.ShapeDtypeStruct((pairs, 8, n), F32)] if first else []),
        mib=40,
        estimate=cost(54 * work, 20 * n * qw, work // HD),
        name=f"attend_back{step}",
        deps=deps,
    )


def gather_dkv_kernel(count, *refs):
    parts = refs[:count]
    cos, sin, out = refs[count:]
    total = parts[0][...].astype(F32)
    for x in parts[1:]:
        total = total + x[...].astype(F32)
    half = total.shape[1] // 2
    out[:, :half] = turn(total[:, :half], cos[...], -sin[...]).astype(BF16)
    out[:, half:] = total[:, half:].astype(BF16)


def gather_dkv(parts, cos, sin, deps=()):
    whole = lambda x: pl.BlockSpec(x.shape, lambda i: (0, 0))
    return launch(
        functools.partial(gather_dkv_kernel, len(parts)),
        (*parts, cos, sin),
        grid=(1,),
        in_specs=[whole(x) for x in (*parts, cos, sin)],
        out_specs=[whole(parts[0])],
        out_shape=[jax.ShapeDtypeStruct(parts[0].shape, BF16)],
        mib=32,
        estimate=cost(10 * parts[0].size, 4 * len(parts) * parts[0].size),
        name="gather_dkv",
        deps=deps,
    )[0]


def own_part_kernel(o_own, w_own, out):
    out[0] = dot_nt(o_own[...], w_own[...])


def own_part(o_own, w_own):
    n, e = o_own.shape
    d = w_own.shape[0]
    dt = 512
    return launch(
        own_part_kernel,
        (o_own, w_own),
        grid=(d // dt,),
        in_specs=[
            pl.BlockSpec((n, e), lambda i: (0, 0), pipeline_mode=pl.Buffered(1)),
            pl.BlockSpec((dt, e), lambda i: (i, 0)),
        ],
        out_specs=[pl.BlockSpec((1, n, dt), lambda i: (i, 0, 0))],
        out_shape=[jax.ShapeDtypeStruct((d // dt, n, dt), F32)],
        mib=40,
        estimate=cost(n * d * e, 2 * d * e),
        name="own_part",
    )[0]


def merge_kernel(part, o_oth, w_oth, full, gain, h1, a2, a2_t, r2, ssa, held, sums):
    i = pl.program_id(0)
    attn = part[0] + dot_nt(o_oth[...], w_oth[...])
    x = full[...].astype(F32) + attn
    h1[0] = x
    held[i] = x

    @pl.when(i == 0)
    def _():
        sums[...] = jnp.zeros_like(sums)
        ssa[...] = jnp.zeros_like(ssa)

    sums[...] += jnp.sum(x * x, axis=1, keepdims=True)
    ssa[...] += jnp.sum(attn * attn, axis=1, keepdims=True)

    @pl.when(i == pl.num_programs(0) - 1)
    def _():
        count, _, dt = held.shape
        inv = lax.rsqrt(sums[...] * (1.0 / (count * dt)) + EPS)
        r2[...] = inv
        for j in range(count):
            at = slice(j * dt, (j + 1) * dt)
            act = (held[j] * inv[:, :1] * gain[:, at]).astype(BF16)
            a2[:, at] = act
            a2_t[at, :] = act.T


def merge(part, o_oth, w_oth, full, gain, deps=()):
    n, d = full.shape
    dt = 512
    e = o_oth.shape[1]
    const = lambda a: pl.BlockSpec(a.shape, lambda i: (0, 0), pipeline_mode=pl.Buffered(1))
    return launch(
        merge_kernel,
        (part, o_oth, w_oth, full, gain),
        grid=(d // dt,),
        in_specs=[
            pl.BlockSpec((1, n, dt), lambda i: (i, 0, 0)),
            const(o_oth),
            pl.BlockSpec((dt, e), lambda i: (i, 0)),
            pl.BlockSpec((n, dt), lambda i: (0, i)),
            const(gain),
        ],
        out_specs=[
            pl.BlockSpec((1, n, dt), lambda i: (i, 0, 0)),
            pl.BlockSpec((n, d), lambda i: (0, 0)),
            pl.BlockSpec((d, n), lambda i: (0, 0)),
            pl.BlockSpec((n, PAIR), lambda i: (0, 0)),
            pl.BlockSpec((n, PAIR), lambda i: (0, 0)),
        ],
        out_shape=[
            jax.ShapeDtypeStruct((d // dt, n, dt), F32),
            jax.ShapeDtypeStruct((n, d), BF16),
            jax.ShapeDtypeStruct((d, n), BF16),
            jax.ShapeDtypeStruct((n, PAIR), F32),
            jax.ShapeDtypeStruct((n, PAIR), F32),
        ],
        scratch=[pltpu.VMEM((d // dt, n, dt), F32), pltpu.VMEM((n, PAIR), F32)],
        mib=48,
        estimate=cost(3 * n * d * d, 2 * d * d + 12 * n * d),
        name="merge",
        deps=deps,
    )


def units_kernel(a2, g, wg, wu, wd, out):
    gate = dot(a2[...], wg[...])
    up = dot(a2[...], wu[...])
    dh = dot(g[...], wd[...])
    sig = jax.nn.sigmoid(gate)
    act = gate * sig
    out[0] = (act * up).astype(BF16)
    out[1] = (dh * up * sig * (1.0 + gate * (1.0 - sig))).astype(BF16)
    out[2] = (dh * act).astype(BF16)


def units(a2, g, wg, wu, wd, first, count, deps=()):
    n, d = a2.shape
    const = pl.BlockSpec((n, d), lambda i: (0, 0), pipeline_mode=pl.Buffered(1))
    wspec = pl.BlockSpec((d, FT), lambda i: (0, first + i))
    return launch(
        units_kernel,
        (a2, g, wg, wu, wd),
        grid=(count,),
        in_specs=[const, const, wspec, wspec, wspec],
        out_specs=[pl.BlockSpec((3, n, FT), lambda i: (0, 0, i))],
        out_shape=[jax.ShapeDtypeStruct((3, n, count * FT), BF16)],
        mib=58,
        estimate=cost(10 * n * d * FT * count, 6 * d * FT * count, n * FT * count),
        name=f"units{first}",
        deps=deps,
    )[0]


def exchange_kernel(count, tiles, nblk, *refs):
    acts = refs[: 3 * count]
    wg, wu, wd, early, total, branch, shares = refs[3 * count : 3 * count + 7]
    mine, theirs, send_sem, recv_sem, z_send, z_recv, own_sem = refs[3 * count + 7 :]
    i = pl.program_id(0)
    other = 1 - lax.axis_index("head")
    blk = lax.axis_index("blk")
    rows = early.shape[0] // nblk

    def copy(j):
        return pltpu.make_async_remote_copy(
            src_ref=mine.at[j],
            dst_ref=theirs.at[j],
            send_sem=send_sem.at[j],
            recv_sem=recv_sem.at[j],
            device_id={"head": other},
            device_id_type=pl.DeviceIdType.MESH,
        )

    def block(b):
        return early.at[pl.ds(pl.multiple_of(b * rows, rows), rows), :]

    def share(k):
        to = lax.rem(blk + k, nblk)
        return pltpu.make_async_remote_copy(
            src_ref=block(to),
            dst_ref=shares.at[blk],
            send_sem=z_send.at[k],
            recv_sem=z_recv.at[k],
            device_id={"blk": to},
            device_id_type=pl.DeviceIdType.MESH,
        )

    def keep():
        return pltpu.make_async_copy(block(blk), shares.at[blk], own_sem)

    def product(m, weight):
        out, at = None, 0
        for act in acts[m * count : (m + 1) * count]:
            term = dot_nt(act[0], weight[:, at : at + act.shape[2]])
            out = term if out is None else out + term
            at += act.shape[2]
        return out

    @pl.when(i == 0)
    def _():
        barrier = pltpu.get_barrier_semaphore()
        pl.semaphore_signal(
            barrier, inc=1, device_id={"head": other}, device_id_type=pl.DeviceIdType.MESH
        )
        for k in range(1, nblk):
            pl.semaphore_signal(
                barrier,
                inc=1,
                device_id={"blk": lax.rem(blk + k, nblk)},
                device_id_type=pl.DeviceIdType.MESH,
            )
        pl.semaphore_wait(barrier, nblk)
        for k in range(1, nblk):
            share(k).start()
        keep().start()

    @pl.when(i < tiles)
    def _():
        mine[i] = (product(1, wg) + product(2, wu)).astype(BF16)
        copy(i).start()

    @pl.when(i >= tiles)
    def _():
        branch[0] = product(0, wd).astype(BF16)

    @pl.when(i == 2 * tiles - 1)
    def _():
        width = mine.shape[2]
        for j in range(tiles):
            copy(j).wait()
            total[:, j * width : (j + 1) * width] = mine[j].astype(F32) + theirs[j].astype(F32)
        for k in range(1, nblk):
            share(k).wait()
        keep().wait()


def exchange(stacks, wg, wu, wd, early, nblk, name):
    n = stacks[0].shape[1]
    d, ff = wg.shape
    dt = 256
    tiles = d // dt
    per = tiles // 2
    acts = [x for _ in range(3) for x in stacks]
    specs = [
        pl.BlockSpec((1,) + x.shape[1:], lambda i, m=m: (m, 0, 0), pipeline_mode=pl.Buffered(1))
        for m in range(3)
        for x in stacks
    ]
    first = pl.BlockSpec((dt, ff), lambda i: (jnp.minimum(i, tiles - 1), 0))
    second = pl.BlockSpec((dt, ff), lambda i: (jnp.maximum(i - tiles, 0), 0))
    place_hbm = pl.BlockSpec(memory_space=pltpu.HBM)

    def branch_at(i):
        j = jnp.maximum(i - tiles, 0)
        return (j // per, 0, j % per)

    return launch(
        functools.partial(exchange_kernel, len(stacks), tiles, nblk),
        (*acts, wg, wu, wd, early),
        grid=(2 * tiles,),
        in_specs=specs + [first, first, second, place_hbm],
        out_specs=[
            pl.BlockSpec((n, d), lambda i: (0, 0)),
            pl.BlockSpec((1, n, dt), branch_at),
            place_hbm,
        ],
        out_shape=[
            jax.ShapeDtypeStruct((n, d), F32),
            jax.ShapeDtypeStruct((2, n, d // 2), BF16),
            jax.ShapeDtypeStruct((nblk, early.shape[0] // nblk, early.shape[1]), BF16),
        ],
        scratch=[
            pltpu.VMEM((tiles, n, dt), BF16),
            pltpu.VMEM((tiles, n, dt), BF16),
            pltpu.SemaphoreType.DMA((tiles,)),
            pltpu.SemaphoreType.DMA((tiles,)),
            pltpu.SemaphoreType.DMA((nblk,)),
            pltpu.SemaphoreType.DMA((nblk,)),
            pltpu.SemaphoreType.DMA,
        ],
        mib=58,
        estimate=cost(6 * n * d * ff, 6 * d * ff),
        name=name,
        collective=1,
    )


def stream_kernel(da_sum, h1, r2, gain, g, w_out, dh1, dattn_t, dout, gsum):
    da = da_sum[...]
    inv = r2[:, :1]
    norm = jnp.concatenate([h1[j] for j in range(h1.shape[0])], axis=1) * inv
    grad = da * norm

    @pl.when(pl.program_id(0) == 0)
    def _():
        gsum[...] = jnp.zeros_like(gsum)

    gsum[...] += jnp.sum(grad, axis=0, keepdims=True)
    e2 = da * gain[...]
    mean = jnp.sum(e2 * norm, axis=1, keepdims=True) * (1.0 / da.shape[1])
    dh = g[...].astype(F32) + inv * (e2 - norm * mean)
    dh1[...] = dh
    low = dh.astype(BF16)
    dattn_t[...] = low.T
    dout[...] = dot(low, w_out[...]).astype(BF16)


def stream(da, h1, r2, gain, g, w_out, deps=()):
    parts, n, dt = h1.shape
    d = parts * dt
    tt = min(n, 128)
    ew = w_out.shape[1]
    row = lambda w: pl.BlockSpec((tt, w), lambda i: (i, 0))
    const = lambda a: pl.BlockSpec(a.shape, lambda i: (0, 0), pipeline_mode=pl.Buffered(1))
    return launch(
        stream_kernel,
        (da, h1, r2, gain, g, w_out),
        grid=(n // tt,),
        in_specs=[
            row(d),
            pl.BlockSpec((parts, tt, dt), lambda i: (0, i, 0)),
            row(PAIR),
            const(gain),
            row(d),
            const(w_out),
        ],
        out_specs=[
            row(d),
            pl.BlockSpec((d, tt), lambda i: (0, i)),
            row(ew),
            pl.BlockSpec((1, d), lambda i: (0, 0)),
        ],
        out_shape=[
            jax.ShapeDtypeStruct((n, d), F32),
            jax.ShapeDtypeStruct((d, n), BF16),
            jax.ShapeDtypeStruct((n, ew), BF16),
            jax.ShapeDtypeStruct((1, d), F32),
        ],
        mib=56,
        estimate=cost(2 * n * d * ew, 2 * d * ew + 20 * n * d),
        name="stream",
        deps=deps,
    )


def entry_kernel(dq, dkv, wq, wk, wv, full, ssx, gain, part, gsum, rsum):
    kvw = wk.shape[1]
    da = dot_nt(dq[...], wq[...])
    da = da + dot_nt(dkv[:, :kvw], wk[...]) + dot_nt(dkv[:, kvw:], wv[...])
    width = pl.num_programs(0) * da.shape[1]
    inv = lax.rsqrt(ssx[:, :1] * (1.0 / width) + EPS)
    grad = da * (full[...].astype(F32) * inv)
    gsum[...] = jnp.sum(grad, axis=0, keepdims=True)

    @pl.when(pl.program_id(0) == 0)
    def _():
        rsum[...] = jnp.zeros_like(rsum)

    rsum[...] += jnp.sum(grad * gain[...], axis=1, keepdims=True)
    part[0] = da.astype(BF16)


def entry(dq, dkv, wq, wk, wv, full, ssx, gain):
    n, d = full.shape
    dt = 256
    per = d // 2 // dt
    const = lambda a: pl.BlockSpec(a.shape, lambda i: (0, 0), pipeline_mode=pl.Buffered(1))
    wspec = lambda w: pl.BlockSpec((dt, w.shape[1]), lambda i: (i, 0))
    return launch(
        entry_kernel,
        (dq, dkv, wq, wk, wv, full, ssx, gain),
        grid=(d // dt,),
        in_specs=[const(dq), const(dkv), wspec(wq), wspec(wk), wspec(wv)]
        + [
            pl.BlockSpec((n, dt), lambda i: (0, i)),
            const(ssx),
            pl.BlockSpec((1, dt), lambda i: (0, i)),
        ],
        out_specs=[
            pl.BlockSpec((1, n, dt), lambda i: (i // per, 0, i % per)),
            pl.BlockSpec((1, dt), lambda i: (0, i)),
            pl.BlockSpec((n, PAIR), lambda i: (0, 0)),
        ],
        out_shape=[
            jax.ShapeDtypeStruct((2, n, d // 2), BF16),
            jax.ShapeDtypeStruct((1, d), F32),
            jax.ShapeDtypeStruct((n, PAIR), F32),
        ],
        mib=56,
        estimate=cost(2 * n * d * (wq.shape[1] + 2 * wk.shape[1]), 20 * n * d),
        name="entry",
    )


def outer_kernel(shares, count, parts, adds, spread, sc, *refs):
    k = 0
    lefts, rights = [], []
    for share in shares:
        lefts.append((refs[k : k + count], refs[k + count : k + 2 * count]))
        k += 2 * count
        rights.append([(refs[k + 2 * i], refs[k + 2 * i + 1]) for i in range(share)])
        k += 2 * share
    got = refs[k] if adds else None
    outs = refs[k + adds :]

    def work(out):
        m = 0
        for (left_own, left_oth), group in zip(lefts, rights, strict=True):
            rows = left_own[0].shape[0]
            for own, oth in group:
                at = slice(m * FT, (m + 1) * FT)
                for i in range(count):
                    part = slice(i * rows, (i + 1) * rows)
                    total = dot(left_own[i][...], own[0]) + dot(left_oth[i][...], oth[0])
                    if adds:
                        total = total + got[part, at].astype(F32)
                    if spread == 1:
                        out[part, at] = total.astype(BF16)
                    else:
                        size = rows // spread
                        for b in range(spread):
                            to = slice((b * count + i) * size, (b * count + i + 1) * size)
                            out[to, at] = total[b * size : (b + 1) * size, :].astype(BF16)
                m += 1

    if len(parts) == 1:
        work(outs[0])
        return
    step = pl.program_id(0)
    start = 0
    for out, size in zip(outs, parts, strict=True):
        pl.when((step >= start) & (step < start + size))(functools.partial(work, out))
        start += size


def outer(sc, groups, rows, first, parts, name, got=None, deps=(), spread=1):
    n = groups[0][0].shape[1]
    count = sc.shape[0]
    number = sum(parts)
    shares = tuple(len(g[2]) for g in groups)
    ins, specs = [], []
    for own, oth, rights in groups:
        ins += [own] * count + [oth] * count
        for i in range(count):
            specs.append(pl.BlockSpec((rows, n), lambda j, s, i=i: (s[i], 0)))
        specs += specs[-count:]
        for r_own, r_oth, at in rights:
            ins += [r_own, r_oth]
            specs += [pl.BlockSpec((1, n, FT), lambda i, s, at=at: (at, 0, first + i))] * 2
    members = sum(shares)
    height = count * rows
    ospecs, start = [], 0
    for size in parts:
        ospecs.append(
            pl.BlockSpec(
                (height, members * FT),
                lambda i, s, start=start, size=size: (0, jnp.clip(i - start, 0, size - 1)),
            )
        )
        start += size
    if got is not None:
        ins.append(got)
        specs.append(ospecs[0])
    c = number * FT
    return launch(
        functools.partial(outer_kernel, shares, count, tuple(parts), int(got is not None), spread),
        (sc, *ins),
        prefetch=1,
        grid=(number,),
        in_specs=specs,
        out_specs=ospecs,
        out_shape=[jax.ShapeDtypeStruct((height, members * size * FT), BF16) for size in parts],
        mib=48,
        estimate=cost(8 * n * height * c * members, members * c * (4 * n + 2 * height)),
        name=name,
        deps=deps,
    )


def finish_kernel(count, *refs):
    parts = refs[:count]
    outs = refs[count:]
    at = 0
    for part in parts:
        for tile in range(part.shape[2] // (3 * FT)):
            for m in range(3):
                columns = slice((3 * tile + m) * FT, (3 * tile + m + 1) * FT)
                total = part[0, :, columns].astype(F32)
                for b in range(1, part.shape[0]):
                    total = total + part[b, :, columns].astype(F32)
                outs[m][:, at : at + FT] = total
            at += FT


def finish(parts):
    parts = [x.reshape(count, x.shape[0] // count, x.shape[1]) for x, count in parts]
    rows = parts[0].shape[1]
    width = sum(x.shape[2] for x in parts) // 3
    whole = lambda shape: pl.BlockSpec(shape, lambda i: (0,) * len(shape))
    return launch(
        functools.partial(finish_kernel, len(parts)),
        tuple(parts),
        grid=(1,),
        in_specs=[whole(x.shape) for x in parts],
        out_specs=[whole((rows, width))] * 3,
        out_shape=[jax.ShapeDtypeStruct((rows, width), F32)] * 3,
        mib=48,
        estimate=cost(0, 8 * parts[0].shape[0] * rows * width),
        name="finish",
    )


def finish_rows_kernel(shares, *outs):
    at = 0
    for out in outs[:-1]:
        columns = slice(at, at + out.shape[1])
        total = shares[0, :, columns].astype(F32)
        for b in range(1, shares.shape[0]):
            total = total + shares[b, :, columns].astype(F32)
        out[...] = total
        at += out.shape[1]
    total = shares[0, :, at:].astype(F32)
    for b in range(1, shares.shape[0]):
        total = total + shares[b, :, at:].astype(F32)
    outs[-1][...] = total.T


def finish_rows(shares, widths):
    _, rows, columns = shares.shape
    left = columns - sum(widths)
    whole = lambda shape: pl.BlockSpec(shape, lambda i: (0,) * len(shape))
    shapes = [(rows, w) for w in widths] + [(left, rows)]
    return launch(
        finish_rows_kernel,
        (shares,),
        grid=(1,),
        in_specs=[whole(shares.shape)],
        out_specs=[whole(x) for x in shapes],
        out_shape=[jax.ShapeDtypeStruct(x, F32) for x in shapes],
        mib=32,
        estimate=cost(0, 4 * shares.size),
        name="finish_rows",
    )


def body(
    inputs,
    cotangent,
    lengths,
    attn_gain,
    w_query,
    w_key,
    w_value,
    w_out,
    mlp_gain,
    gate_weight,
    up_weight,
    down_weight,
):
    t, rows, half = inputs.shape
    n = t * rows
    heads = lax.axis_size("head")
    nblk = lax.axis_size("blk")
    ndp = lax.axis_size("dp")
    d = half * heads
    h = lax.axis_index("head").astype(jnp.int32)
    blk = lax.axis_index("blk").astype(jnp.int32)
    dp = lax.axis_index("dp").astype(jnp.int32)
    sc_h = h.reshape(1)
    sc_blk = blk.reshape(1)

    def flat(x):
        return jnp.transpose(x, (1, 0, 2)).reshape(n, x.shape[2])

    def unflat(x):
        return jnp.transpose(x.reshape(rows, t, x.shape[1]), (1, 0, 2))

    x_own = flat(inputs)
    g_own = flat(cotangent)
    gain_one = attn_gain.astype(F32).reshape(1, d)
    gain_two = mlp_gain.astype(F32).reshape(1, d)

    pos = blk * t + jnp.arange(t, dtype=jnp.int32)
    ends = jnp.cumsum(lengths, axis=1)
    passed = ends[:, None, :] <= pos[None, :, None]
    start = jnp.max(jnp.where(passed, ends[:, None, :], 0), axis=2)
    valid = (jnp.sum(passed.astype(jnp.int32), axis=2) < DOCS).astype(F32).reshape(n)
    start_rows = start.reshape(rows, 1, t)
    freq = jnp.power(THETA, -2.0 * jnp.arange(HD // 2, dtype=F32) / HD)
    angles = pos.astype(F32)[:, None] * freq[None, :]
    cos_h, sin_h = jnp.cos(angles), jnp.sin(angles)
    cos = jnp.tile(jnp.concatenate([cos_h, cos_h, cos_h, cos_h], axis=1), (rows, 1))
    sin = jnp.tile(jnp.concatenate([-sin_h, sin_h, -sin_h, sin_h], axis=1), (rows, 1))

    CHAIN.clear()
    WEIGHT[0] = EARLY

    def tie(x, *also):
        return lax.optimization_barrier((x, *also))[0]

    def by_head(x):
        return jnp.where(h == 0, x[:, :half], x[:, half:])

    def gate(x):
        x, CHAIN[0] = lax.optimization_barrier((x, CHAIN[0]))
        return x

    def mate(x):
        return swap(x, "dp", 1)

    x_oth = swap(x_own, "head", 1)
    share = w_out.shape[0] // ndp
    piece = lax.dynamic_slice_in_dim(w_out, dp * share, share, 0)
    x_oth, piece, g_own, cos, sin, start_rows = lax.optimization_barrier(
        (x_oth, piece, g_own, cos, sin, start_rows)
    )
    piece = swap(piece, "head", 1)
    full, a_one, queries, kv, ssx = project(
        sc_h, x_own, x_oth, gain_one, w_query, w_key, w_value, cos, sin
    )

    kvs, state = [kv], ()
    for s in range(nblk):
        if s + 1 < nblk:
            steps = [(i, i + 1) for i in range(s, nblk - 1)]
            kvs.append(lax.ppermute(kvs[s], "blk", steps))
        state = attend(s, s == nblk - 1, sc_blk, queries, kvs[s], start_rows, state, rows)
        if s + 1 < nblk - 1:
            kvs[s + 1] = gate(kvs[s + 1])
        if s == 0:
            a_one_t = flip(a_one, "flip_a")
            piece = gate(piece)
            w_out_oth = lax.all_gather(piece, "dp", axis=0, tiled=True)
            g_own, piece = lax.optimization_barrier((g_own, piece))
            g_oth = swap(g_own, "head", 1)
    acc, ml = state
    o_own = flip(acc)
    o_oth = swap(o_own, "head", 1)
    part_own = own_part(o_own, w_out)
    g_full = jnp.concatenate(
        [jnp.where(h == 0, g_own, g_oth), jnp.where(h == 0, g_oth, g_own)], axis=1
    )
    g_t = flip(g_full, "flip_g")
    o_mate, g_mate = mate(o_own), mate(g_t)
    h_one, a_two, a_two_t, inv_two, ssa = merge(
        part_own, o_oth, w_out_oth, full, gain_two
    )
    a_two_mate = mate(a_two_t)

    low_bit = dp & 1
    block_rows = d // ndp
    sc_send = (dp ^ 2).reshape(1)
    sc_keep = dp.reshape(1)
    sc_both = jnp.stack([2 * i + low_bit for i in range(ndp // 2)])
    y_groups = [[0, 2], [1, 3]]

    def both_halves(groups, parts, name, deps=()):
        return [
            lax.psum_scatter(
                x, "dp", scatter_dimension=0, axis_index_groups=y_groups, tiled=True
            )
            for x in outer(sc_both, groups, block_rows, 0, parts, name, deps=deps)
        ]

    def over_blk(x):
        return lax.all_to_all(x, "blk", split_axis=0, concat_axis=0, tiled=True)

    tiles = gate_weight.shape[1] // FT
    size_a = max(1, tiles // 5)
    size_b = (tiles - size_a + 1) // 3
    size_c = tiles - size_a - size_b

    def unit_part(first, count, deps=()):
        x = units(a_two, g_full, gate_weight, up_weight, down_weight, first, count, deps)
        x_mate = mate(x)
        return x, [
            (g_t, g_mate, [(x, x_mate, 0)]),
            (a_two_t, a_two_mate, [(x, x_mate, 1), (x, x_mate, 2)]),
        ]

    part_a, groups_a = unit_part(0, size_a)
    (sum0,) = both_halves(groups_a, (size_a,), "mlp0")
    part_b, groups_b = unit_part(size_a, size_b)
    part_c, groups_c = unit_part(size_a + size_b, size_c)
    (sum1,) = both_halves(groups_b, (size_b,), "mlp1")

    da, branch, all0 = exchange(
        [part_a, part_b, part_c], gate_weight, up_weight, down_weight, sum0, nblk, "exchange"
    )
    WEIGHT[0] = LATE
    sum2, sum3 = both_halves(groups_c, (size_c - size_c // 2, size_c // 2), "mlp2")
    all1 = over_blk(gate(sum1))
    dh_one, d_attn_t, d_out, gain_two_sum = stream(
        da, h_one, inv_two, gain_two, g_full, w_out
    )
    d_attn_mate, a_one_mate = mate(d_attn_t), mate(gate(a_one_t))
    out_groups = [(d_attn_t, d_attn_mate, [(o_own[None], o_mate[None], 0)])]
    out_parts = (o_own.shape[1] // FT,)
    to_other = gate(lax.dynamic_index_in_dim(branch, 1 - h, 0, keepdims=False))
    branch_oth = swap(to_other, "head", 1)

    state, parts = (), []
    for s in reversed(range(nblk)):
        out = attend_back(
            s, s == nblk - 1, s == 0, sc_blk, queries, d_out, o_own, ml, start_rows, cos, sin,
            kvs[s], state, rows, deps=(),
        )
        state = (out[0], out[2] if s == nblk - 1 else state[1])
        part = out[1]
        parts.append(
            lax.ppermute(part, "blk", [(i, i - s) for i in range(s, nblk)]) if s else part
        )
        if s == min(1, nblk - 1):
            (sum_out,) = both_halves(
                out_groups, out_parts, "out", deps=(all1, a_one_mate) + tuple(parts[: nblk - 1])
            )
            all2 = over_blk(gate(sum2))
    d_q = state[0]
    d_kv_own = gather_dkv(parts, cos, sin)
    d_qkv = jnp.concatenate([d_q, d_kv_own], axis=1)
    d_qkv_mate = mate(d_qkv)
    d_part, gain_one_sum, row_sum = entry(
        d_q, d_kv_own, w_query, w_key, w_value, full, ssx, gain_one
    )
    qkv_groups = [(a_one_t, a_one_mate, [(d_qkv[None], d_qkv_mate[None], 0)])]
    qkv_parts = (d_qkv.shape[1] // FT,)
    (first_qkv,) = outer(sc_send, qkv_groups, block_rows, 0, qkv_parts, "qkv_send")
    got_qkv = swap(first_qkv, "dp", 2)
    sum3 = lax.psum_scatter(gate(sum3), "blk", scatter_dimension=0, tiled=True)
    d_send = lax.dynamic_index_in_dim(d_part, 1 - h, 0, keepdims=False)
    d_send, row_sum, gain_one_sum, CHAIN[0] = lax.optimization_barrier(
        (d_send, row_sum, gain_one_sum, CHAIN[0])
    )
    h_late, branch_late = gate(h_one), gate(branch)
    h_half = jnp.concatenate(
        [
            jnp.where(h == 0, h_late[i], h_late[i + h_late.shape[0] // 2])
            for i in range(h_late.shape[0] // 2)
        ],
        axis=1,
    )
    mlp_half = lax.dynamic_index_in_dim(branch_late, h, 0, keepdims=False).astype(F32) + (
        branch_oth.astype(F32)
    )
    output = unflat((h_half + mlp_half).astype(BF16))
    d_other = swap(d_send, "head", 1)
    row_total = row_sum + swap(row_sum, "head", 1)
    (keep_qkv,) = outer(
        sc_keep, qkv_groups, block_rows, 0, qkv_parts, "qkv_keep", got_qkv, deps=(all2, branch_oth)
    )
    per_head = 1.0 / heads
    tail = jnp.stack(
        [
            jnp.sum(valid) * per_head,
            jnp.sum(valid * ssx[:, 0]) * per_head,
            jnp.sum(valid * ssa[:, 0]) * per_head,
            jnp.sum(valid[:, None] * mlp_half * mlp_half),
        ]
    )
    small = jnp.concatenate(
        [gain_one_sum[0], gain_two_sum[0] * per_head, tail, jnp.zeros((PAIR - 4,), F32)]
    ).reshape(-1, PAIR)
    for axis in ("head", "dp"):
        for i in range(lax.axis_size(axis).bit_length() - 1):
            small = small + swap(small, axis, 1 << i)
    small = small.reshape(-1)
    mine = [
        lax.dynamic_slice_in_dim(small, at + dp * block_rows, block_rows, 0)[:, None]
        for at in (0, d)
    ]
    sums4 = jnp.broadcast_to(small[None, 2 * d : 2 * d + 4], (block_rows, 4))
    exact = jnp.concatenate(mine + [sums4], axis=1)
    coarse = exact.astype(BF16)
    fine = (exact - coarse.astype(F32)).astype(BF16)
    extra = jnp.concatenate(
        [coarse, fine, jnp.zeros((block_rows, PAIR - 12), BF16)], axis=1
    )
    all_qkv = over_blk(jnp.concatenate([keep_qkv, sum_out, extra], axis=1))
    grad_down, grad_gate, grad_up = finish([(all0.reshape(-1, all0.shape[2]), nblk), (all1, nblk), (all2, nblk), (sum3, 1)])
    qw, kvw = w_query.shape[1], w_key.shape[1]
    sum_query, sum_key, sum_value, sum_out, small = finish_rows(
        all_qkv.reshape(nblk, -1, all_qkv.shape[1]), (qw, kvw, kvw, o_own.shape[1])
    )

    inv_one = lax.rsqrt(ssx[:, :1] * (1.0 / d) + EPS)
    d_one = lax.dynamic_index_in_dim(d_part, h, 0, keepdims=False).astype(F32) + d_other.astype(F32)
    norm_half = x_own.astype(F32) * inv_one
    grad_input = by_head(tie(dh_one, d_other)) + inv_one * (
        d_one * by_head(gain_one) - norm_half * (row_total[:, :1] * (1.0 / d))
    )

    small = small[:6] + small[6:12]
    grad_attn_gain, grad_mlp_gain = small[0], small[1]
    stats = jnp.sqrt(small[3:6, 0] / (small[2, 0] * d))

    return (
        output,
        unflat(grad_input),
        grad_attn_gain,
        sum_query,
        sum_key,
        sum_value,
        sum_out,
        grad_mlp_gain,
        grad_gate,
        grad_up,
        grad_down,
        stats,
    )


def solution(mesh):
    tokens = P("blk", "dp", "head")
    split = P(None, "head")
    in_specs = (tokens, tokens, P("dp", None), P()) + (split,) * 4 + (P(),) + (split,) * 3
    vec, mat = P(("dp", "blk")), P(("dp", "blk"), "head")
    out_specs = (tokens, tokens, vec, mat, mat, mat, mat, vec, mat, mat, mat, P())
    return jax.shard_map(body, mesh=mesh, in_specs=in_specs, out_specs=out_specs, check_vma=False)
```

```python
import functools

import jax
import jax.numpy as jnp
from jax import lax
from jax.experimental import pallas as pl
from jax.experimental.pallas import tpu as pltpu
from jax.sharding import PartitionSpec as P

HD = 64
PAIR = 2 * HD
DOCS = 8
EPS = 1e-05
THETA = 10000.0
NEG = -1e30
F32 = jnp.float32
BF16 = jnp.bfloat16
FT = 256


EARLY, LATE = 0.4, 0.4
WEIGHT = [EARLY]


def params(mib, collective=None):
    if collective is None:
        return pltpu.CompilerParams(vmem_limit_bytes=mib << 20)
    return pltpu.CompilerParams(
        vmem_limit_bytes=mib << 20, collective_id=collective, has_side_effects=True
    )


def cost(flops, byte_count, trans=0):
    return pl.CostEstimate(
        flops=int(flops * WEIGHT[0]),
        bytes_accessed=int(byte_count * WEIGHT[0]),
        transcendentals=int(trans * WEIGHT[0]),
    )


CHAIN = []


def in_hbm(x):
    return pltpu.with_memory_space_constraint(x, pltpu.HBM)


def launch(kernel, args, *, grid, in_specs, out_specs, out_shape, mib, estimate, name, scratch=(), prefetch=0, deps=(), pin_in=True, pin_out=True, collective=None):
    extra = list(CHAIN) + list(deps)
    n_in, n_out = len(args), len(out_shape)

    def wrapped(*refs):
        rest = refs[n_in + len(extra) :]
        kernel(*refs[:n_in], *rest[:n_out], *rest[n_out + 1 :])

    if pin_in:
        args = tuple(args[:prefetch]) + tuple(in_hbm(x) for x in args[prefetch:])
    if pin_out:
        out_shape = [pltpu.HBM(o.shape, o.dtype) for o in out_shape]
    extra = [in_hbm(x) for x in extra]
    *outs, token = pl.pallas_call(
        wrapped,
        grid_spec=pltpu.PrefetchScalarGridSpec(
            num_scalar_prefetch=prefetch,
            grid=grid,
            in_specs=list(in_specs) + [pl.BlockSpec(memory_space=pltpu.HBM)] * len(extra),
            out_specs=list(out_specs) + [pl.BlockSpec(memory_space=pltpu.HBM)],
            scratch_shapes=list(scratch),
        ),
        out_shape=list(out_shape) + [pltpu.HBM((8, 128), F32)],
        compiler_params=params(mib, collective),
        cost_estimate=estimate,
        name=name,
    )(*args, *extra)
    CHAIN[:] = [token]
    return outs


def dot(a, b):
    return jnp.dot(a, b, preferred_element_type=F32)


def dot_nt(a, b):
    return lax.dot_general(a, b, (((1,), (1,)), ((), ())), preferred_element_type=F32)


def dot_tn(a, b):
    return lax.dot_general(a, b, (((0,), (0,)), ((), ())), preferred_element_type=F32)


def swap(x, axis, bit):
    n = lax.axis_size(axis)
    return lax.ppermute(x, axis, [(i, i ^ bit) for i in range(n)])


def lanes(shape):
    return lax.broadcasted_iota(jnp.int32, shape, len(shape) - 1)


def turn(x, cos, sin):
    out = []
    for c in range(x.shape[1] // PAIR):
        v = x[:, c * PAIR : (c + 1) * PAIR]
        low = lanes(v.shape) % HD < HD // 2
        other = jnp.where(low, pltpu.roll(v, PAIR - HD // 2, 1), pltpu.roll(v, HD // 2, 1))
        out.append(v * cos + other * sin)
    return out[0] if len(out) == 1 else jnp.concatenate(out, axis=1)


def project_kernel(h_ref, own, oth, gain, wq, wk, wv, cos, sin, full, a1, q, kv, ssx):
    first = h_ref[0] == 0
    x_own = own[...].astype(F32)
    x_oth = oth[...].astype(F32)
    x = jnp.concatenate(
        [jnp.where(first, x_own, x_oth), jnp.where(first, x_oth, x_own)], axis=1
    )
    width = x.shape[1]
    total = jnp.sum(x * x, axis=1, keepdims=True)
    inv = lax.rsqrt(total * (1.0 / width) + EPS)
    act = (x * inv * gain[...]).astype(BF16)
    full[...] = x.astype(BF16)
    a1[...] = act
    ssx[...] = jnp.broadcast_to(total, ssx.shape)
    q[...] = turn(dot(act, wq[...]), cos[...], sin[...]).astype(BF16) * (HD**-0.5)
    kvw = wk.shape[1]
    kv[:, :kvw] = turn(dot(act, wk[...]), cos[...], sin[...]).astype(BF16)
    kv[:, kvw:] = dot(act, wv[...]).astype(BF16)


def project(h, own, oth, gain, wq, wk, wv, cos, sin):
    n, half = own.shape
    d = 2 * half
    tt = min(n, 256)
    qw, kvw = wq.shape[1], wk.shape[1]
    row = lambda w: pl.BlockSpec((tt, w), lambda i, *_: (i, 0))
    const = lambda a: pl.BlockSpec(a.shape, lambda i, *_: (0, 0), pipeline_mode=pl.Buffered(1))
    return launch(
        project_kernel,
        (h, own, oth, gain, wq, wk, wv, cos, sin),
        prefetch=1,
        grid=(n // tt,),
        in_specs=[row(half), row(half), const(gain), const(wq), const(wk), const(wv)]
        + [row(PAIR), row(PAIR)],
        out_specs=[row(d), row(d), row(qw), row(2 * kvw), row(PAIR)],
        out_shape=[
            jax.ShapeDtypeStruct((n, d), BF16),
            jax.ShapeDtypeStruct((n, d), BF16),
            jax.ShapeDtypeStruct((n, qw), BF16),
            jax.ShapeDtypeStruct((n, 2 * kvw), BF16),
            jax.ShapeDtypeStruct((n, PAIR), F32),
        ],
        mib=32,
        pin_in=False,
        estimate=cost(2 * n * d * (qw + 2 * kvw), 2 * d * (qw + 2 * kvw) + 12 * n * d),
        name="project",
    )


def place(kv, kvh, base):
    x = kv[:, base : base + PAIR].astype(F32)
    x = jnp.where(kvh == 0, x, pltpu.roll(x, HD, 1))
    low = jnp.where(lanes(x.shape) < HD, x, 0.0)
    return low.astype(BF16), pltpu.roll(low, HD, 1).astype(BF16)


def flip_head(kv, kvh, base):
    x = kv[:, base : base + PAIR].astype(F32).T
    return jnp.where(kvh == 0, x[:HD, :], x[HD:, :])


def attend_kernel(step, last, ppk, sc, q_ref, kv_ref, start_ref, *refs):
    refs = list(refs)
    if step:
        acc_in, ml_in = refs[:2]
        refs = refs[2:]
    acc_out, ml_out = refs
    t = q_ref.shape[0]
    kvh = pl.program_id(1)
    blk = sc[0]

    def finish(pair, par, acc, m, l):
        rows = slice(pair * PAIR + par * HD, pair * PAIR + (par + 1) * HD)
        if last:
            acc = acc / l
            m = m + jnp.log(l)
        acc_out[rows, :] = acc
        ml_out[pair, par : par + 1, :] = m
        ml_out[pair, 2 + par : 3 + par, :] = l

    heads = [(pair, par) for pair in range(ppk) for par in range(2)]

    def work():
        u = lax.broadcasted_iota(jnp.int32, (t, t), 0) + (blk - step) * t
        keep = u >= start_ref[0]
        if step == 0:
            keep = keep & (u <= lanes((t, t)) + blk * t)
        bias = jnp.where(keep, 0.0, NEG)
        kv = kv_ref[...]
        kk = place(kv, kvh, 0)
        ones = jnp.where(lax.broadcasted_iota(jnp.int32, (16, t), 0) == 0, 1.0, 0.0)
        vt = jnp.concatenate([flip_head(kv, kvh, PAIR), ones], axis=0).astype(BF16)
        scores = [
            dot_nt(kk[par], q_ref[:, pair * PAIR : (pair + 1) * PAIR]) + bias
            for pair, par in heads
        ]
        for (pair, par), s in zip(heads, scores, strict=True):
            m = jnp.max(s, axis=0, keepdims=True)
            if step:
                old = ml_in[pair, par : par + 1, :]
                m = jnp.maximum(m, old)
            pv = dot(vt, jnp.exp(s - m).astype(BF16))
            acc, l = pv[:HD], pv[HD : HD + 1]
            if step:
                factor = jnp.exp(old - m)
                rows = slice(pair * PAIR + par * HD, pair * PAIR + (par + 1) * HD)
                acc = acc + acc_in[rows, :] * factor
                l = l + ml_in[pair, 2 + par : 3 + par, :] * factor
            finish(pair, par, acc, m, l)

    if step == 0:
        work()
    else:
        pl.when(blk >= step)(work)

        @pl.when(blk < step)
        def _():
            for pair, par in heads:
                rows = slice(pair * PAIR + par * HD, pair * PAIR + (par + 1) * HD)
                m = ml_in[pair, par : par + 1, :]
                finish(pair, par, acc_in[rows, :], m, ml_in[pair, 2 + par : 3 + par, :])


def attend(step, last, sc, q, kv, start, state, rows, deps=()):
    n, qw = q.shape
    t = n // rows
    pairs = qw // PAIR
    kv_heads = kv.shape[1] // 2 // HD
    ppk = pairs // kv_heads
    accspec = pl.BlockSpec((ppk * PAIR, t), lambda r, k, *_: (k, r))
    mlspec = pl.BlockSpec((ppk, 8, t), lambda r, k, *_: (k, 0, r))
    work = n * t * qw
    return launch(
        functools.partial(attend_kernel, step, last, ppk),
        (sc, in_hbm(q), in_hbm(kv), in_hbm(start), *state),
        prefetch=1,
        grid=(rows, kv_heads),
        in_specs=[
            pl.BlockSpec((t, ppk * PAIR), lambda r, k, *_: (r, k)),
            pl.BlockSpec((t, kv.shape[1]), lambda r, k, *_: (r, 0)),
            pl.BlockSpec((1, 1, t), lambda r, k, *_: (r, 0, 0)),
        ]
        + ([accspec, mlspec] if state else []),
        out_specs=[accspec, mlspec],
        out_shape=[
            jax.ShapeDtypeStruct((qw, n), F32),
            jax.ShapeDtypeStruct((pairs, 8, n), F32),
        ],
        mib=28,
        estimate=cost(24 * work, 20 * n * qw, n * t * qw // HD),
        name=f"attend{step}",
        deps=deps,
        pin_in=False,
        pin_out=False,
    )


def flip_kernel(x, out):
    out[...] = x[...].T.astype(BF16)


def flip(x, name="flip"):
    w, n = x.shape
    by_rows = w > n
    step = 512 if max(w, n) % 512 == 0 else max(w, n)
    across = pl.BlockSpec((step, n) if by_rows else (w, step), lambda i: (i, 0) if by_rows else (0, i))
    down = pl.BlockSpec((n, step) if by_rows else (step, w), lambda i: (0, i) if by_rows else (i, 0))
    return launch(
        flip_kernel,
        (x,),
        grid=(max(w, n) // step,),
        in_specs=[across],
        out_specs=[down],
        out_shape=[jax.ShapeDtypeStruct((n, w), BF16)],
        mib=32,
        estimate=cost(8 * n * w, 6 * n * w),
        name=name,
        pin_in=False,
    )[0]


def attend_back_kernel(step, first, last, ppk, sc, q_ref, do_ref, ml_ref, start_ref, kv_ref, *refs):
    refs = list(refs)
    o_ref = refs.pop(0) if first else None
    dq_in, delta_in = (None, None) if first else (refs.pop(0), refs.pop(0))
    cos, sin = (refs.pop(0), refs.pop(0)) if last else (None, None)
    dq_out, dkv_out = refs.pop(0), refs.pop(0)
    delta_out = refs.pop(0) if first else None
    dk_acc, dv_acc, dq_acc = refs
    t = q_ref.shape[0]
    kvh = pl.program_id(1)
    blk = sc[0]
    heads = [(pair, par) for pair in range(ppk) for par in range(2)]

    if first:
        for pair in range(ppk):
            both = slice(pair * PAIR, (pair + 1) * PAIR)
            prod = (do_ref[:, both].astype(F32) * o_ref[:, both].astype(F32)).T
            for par in range(2):
                delta_out[pair, par : par + 1, :] = jnp.sum(
                    prod[par * HD : (par + 1) * HD, :], axis=0, keepdims=True
                )
        dq_acc[...] = jnp.zeros_like(dq_acc)
    else:
        dq_acc[...] = dq_in[...]
    delta = delta_out if first else delta_in

    @pl.when(kvh == 0)
    def _():
        dkv_out[...] = jnp.zeros_like(dkv_out)

    def work():
        u = lax.broadcasted_iota(jnp.int32, (t, t), 0) + (blk - step) * t
        keep = u >= start_ref[0]
        if step == 0:
            keep = keep & (u <= lanes((t, t)) + blk * t)
        bias = jnp.where(keep, 0.0, NEG)
        kv = kv_ref[...]
        kk = place(kv, kvh, 0)
        vv = place(kv, kvh, PAIR)
        kt = flip_head(kv, kvh, 0).astype(BF16)
        dk_acc[...] = jnp.zeros_like(dk_acc)
        dv_acc[...] = jnp.zeros_like(dv_acc)
        for pair, par in heads:
            q = q_ref[:, pair * PAIR : (pair + 1) * PAIR]
            do = do_ref[:, pair * PAIR : (pair + 1) * PAIR]
            st = dot_nt(kk[par], q) + bias
            dp = dot_nt(vv[par], do)
            pt = jnp.exp(st - ml_ref[pair, par : par + 1, :])
            ds = (pt * (dp - delta[pair, par : par + 1, :])).astype(BF16)
            dv_acc[par] += dot(pt.astype(BF16), do)
            dk_acc[par] += dot(ds, q)
            rows = slice(pair * PAIR + par * HD, pair * PAIR + (par + 1) * HD)
            dq_acc[rows, :] += dot(kt, ds)
        low = lanes((t, PAIR)) < HD
        for acc, base in ((dk_acc, 0), (dv_acc, PAIR)):
            both = acc[0] + pltpu.roll(acc[1], HD, 1)
            here = jnp.where(kvh == 0, both, pltpu.roll(both, HD, 1))
            mine = low == (kvh == 0)
            old = dkv_out[:, base : base + PAIR].astype(F32)
            dkv_out[:, base : base + PAIR] = jnp.where(mine, here, old).astype(BF16)

    if step == 0:
        work()
    else:
        pl.when(blk >= step)(work)

    if last:
        for pair in range(ppk):
            rows = slice(pair * PAIR, (pair + 1) * PAIR)
            dq = (dq_acc[rows, :] * (HD**-0.5)).T
            dq_out[:, rows] = turn(dq, cos[...], -sin[...]).astype(BF16)
    else:
        dq_out[...] = dq_acc[...]


def attend_back(step, first, last, sc, q, do, o, ml, start, cos, sin, kv, state, rows, deps=()):
    n, qw = q.shape
    t = n // rows
    pairs = qw // PAIR
    kvw = kv.shape[1]
    kv_heads = kvw // 2 // HD
    ppk = pairs // kv_heads
    width = ppk * PAIR
    pairspec = pl.BlockSpec((t, width), lambda r, k, *_: (r, k))
    accspec = pl.BlockSpec((width, t), lambda r, k, *_: (k, r))
    mlspec = pl.BlockSpec((ppk, 8, t), lambda r, k, *_: (k, 0, r))
    rowspec = lambda w: pl.BlockSpec((t, w), lambda r, k, *_: (r, 0))
    work = n * t * qw
    return launch(
        functools.partial(attend_back_kernel, step, first, last, ppk),
        (sc, q, do, ml, start, kv)
        + ((o,) if first else tuple(state))
        + ((cos, sin) if last else ()),
        prefetch=1,
        grid=(rows, kv_heads),
        in_specs=[pairspec, pairspec, mlspec]
        + [pl.BlockSpec((1, 1, t), lambda r, k, *_: (r, 0, 0))]
        + [rowspec(kvw)]
        + ([pairspec] if first else [accspec, mlspec])
        + ([rowspec(PAIR)] * 2 if last else []),
        out_specs=[pairspec if last else accspec, rowspec(kvw)] + ([mlspec] if first else []),
        scratch=[
            pltpu.VMEM((2, t, PAIR), F32),
            pltpu.VMEM((2, t, PAIR), F32),
            pltpu.VMEM((width, t), F32),
        ],
        out_shape=[
            jax.ShapeDtypeStruct((n, qw), BF16) if last else jax.ShapeDtypeStruct((qw, n), F32),
            jax.ShapeDtypeStruct((n, kvw), BF16),
        ]
        + ([jax.ShapeDtypeStruct((pairs, 8, n), F32)] if first else []),
        mib=40,
        estimate=cost(54 * work, 20 * n * qw, work // HD),
        name=f"attend_back{step}",
        deps=deps,
    )


def gather_dkv_kernel(count, *refs):
    parts = refs[:count]
    cos, sin, out = refs[count:]
    total = parts[0][...].astype(F32)
    for x in parts[1:]:
        total = total + x[...].astype(F32)
    half = total.shape[1] // 2
    out[:, :half] = turn(total[:, :half], cos[...], -sin[...]).astype(BF16)
    out[:, half:] = total[:, half:].astype(BF16)


def gather_dkv(parts, cos, sin, deps=()):
    whole = lambda x: pl.BlockSpec(x.shape, lambda i: (0, 0))
    return launch(
        functools.partial(gather_dkv_kernel, len(parts)),
        (*parts, cos, sin),
        grid=(1,),
        in_specs=[whole(x) for x in (*parts, cos, sin)],
        out_specs=[whole(parts[0])],
        out_shape=[jax.ShapeDtypeStruct(parts[0].shape, BF16)],
        mib=32,
        estimate=cost(10 * parts[0].size, 4 * len(parts) * parts[0].size),
        name="gather_dkv",
        deps=deps,
    )[0]


def own_part_kernel(o_own, w_own, out):
    out[0] = dot_nt(o_own[...], w_own[...])


def own_part(o_own, w_own):
    n, e = o_own.shape
    d = w_own.shape[0]
    dt = 512
    return launch(
        own_part_kernel,
        (o_own, w_own),
        grid=(d // dt,),
        in_specs=[
            pl.BlockSpec((n, e), lambda i: (0, 0), pipeline_mode=pl.Buffered(1)),
            pl.BlockSpec((dt, e), lambda i: (i, 0)),
        ],
        out_specs=[pl.BlockSpec((1, n, dt), lambda i: (i, 0, 0))],
        out_shape=[jax.ShapeDtypeStruct((d // dt, n, dt), F32)],
        mib=40,
        estimate=cost(n * d * e, 2 * d * e),
        name="own_part",
    )[0]


def merge_kernel(part, o_oth, w_oth, full, gain, h1, a2, a2_t, r2, ssa, held, sums):
    i = pl.program_id(0)
    attn = part[0] + dot_nt(o_oth[...], w_oth[...])
    x = full[...].astype(F32) + attn
    h1[0] = x
    held[i] = x

    @pl.when(i == 0)
    def _():
        sums[...] = jnp.zeros_like(sums)
        ssa[...] = jnp.zeros_like(ssa)

    sums[...] += jnp.sum(x * x, axis=1, keepdims=True)
    ssa[...] += jnp.sum(attn * attn, axis=1, keepdims=True)

    @pl.when(i == pl.num_programs(0) - 1)
    def _():
        count, _, dt = held.shape
        inv = lax.rsqrt(sums[...] * (1.0 / (count * dt)) + EPS)
        r2[...] = inv
        for j in range(count):
            at = slice(j * dt, (j + 1) * dt)
            act = (held[j] * inv[:, :1] * gain[:, at]).astype(BF16)
            a2[:, at] = act
            a2_t[at, :] = act.T


def merge(part, o_oth, w_oth, full, gain, deps=()):
    n, d = full.shape
    dt = 512
    e = o_oth.shape[1]
    const = lambda a: pl.BlockSpec(a.shape, lambda i: (0, 0), pipeline_mode=pl.Buffered(1))
    return launch(
        merge_kernel,
        (part, o_oth, w_oth, full, gain),
        grid=(d // dt,),
        in_specs=[
            pl.BlockSpec((1, n, dt), lambda i: (i, 0, 0)),
            const(o_oth),
            pl.BlockSpec((dt, e), lambda i: (i, 0)),
            pl.BlockSpec((n, dt), lambda i: (0, i)),
            const(gain),
        ],
        out_specs=[
            pl.BlockSpec((1, n, dt), lambda i: (i, 0, 0)),
            pl.BlockSpec((n, d), lambda i: (0, 0)),
            pl.BlockSpec((d, n), lambda i: (0, 0)),
            pl.BlockSpec((n, PAIR), lambda i: (0, 0)),
            pl.BlockSpec((n, PAIR), lambda i: (0, 0)),
        ],
        out_shape=[
            jax.ShapeDtypeStruct((d // dt, n, dt), F32),
            jax.ShapeDtypeStruct((n, d), BF16),
            jax.ShapeDtypeStruct((d, n), BF16),
            jax.ShapeDtypeStruct((n, PAIR), F32),
            jax.ShapeDtypeStruct((n, PAIR), F32),
        ],
        scratch=[pltpu.VMEM((d // dt, n, dt), F32), pltpu.VMEM((n, PAIR), F32)],
        mib=48,
        estimate=cost(3 * n * d * d, 2 * d * d + 12 * n * d),
        name="merge",
        deps=deps,
    )


def units_kernel(a2, g, wg, wu, wd, out):
    gate = dot(a2[...], wg[...])
    up = dot(a2[...], wu[...])
    dh = dot(g[...], wd[...])
    sig = jax.nn.sigmoid(gate)
    act = gate * sig
    out[0] = (act * up).astype(BF16)
    out[1] = (dh * up * sig * (1.0 + gate * (1.0 - sig))).astype(BF16)
    out[2] = (dh * act).astype(BF16)


def units(a2, g, wg, wu, wd, first, count, deps=()):
    n, d = a2.shape
    const = pl.BlockSpec((n, d), lambda i: (0, 0), pipeline_mode=pl.Buffered(1))
    wspec = pl.BlockSpec((d, FT), lambda i: (0, first + i))
    return launch(
        units_kernel,
        (a2, g, wg, wu, wd),
        grid=(count,),
        in_specs=[const, const, wspec, wspec, wspec],
        out_specs=[pl.BlockSpec((3, n, FT), lambda i: (0, 0, i))],
        out_shape=[jax.ShapeDtypeStruct((3, n, count * FT), BF16)],
        mib=58,
        estimate=cost(10 * n * d * FT * count, 6 * d * FT * count, n * FT * count),
        name=f"units{first}",
        deps=deps,
    )[0]


def exchange_kernel(count, tiles, nblk, *refs):
    acts = refs[: 3 * count]
    wg, wu, wd, early, total, branch, shares = refs[3 * count : 3 * count + 7]
    mine, theirs, send_sem, recv_sem, z_send, z_recv, own_sem = refs[3 * count + 7 :]
    i = pl.program_id(0)
    other = 1 - lax.axis_index("head")
    blk = lax.axis_index("blk")
    rows = early.shape[0] // nblk

    def copy(j):
        return pltpu.make_async_remote_copy(
            src_ref=mine.at[j],
            dst_ref=theirs.at[j],
            send_sem=send_sem.at[j],
            recv_sem=recv_sem.at[j],
            device_id={"head": other},
            device_id_type=pl.DeviceIdType.MESH,
        )

    def block(b):
        return early.at[pl.ds(pl.multiple_of(b * rows, rows), rows), :]

    def share(k):
        to = lax.rem(blk + k, nblk)
        return pltpu.make_async_remote_copy(
            src_ref=block(to),
            dst_ref=shares.at[blk],
            send_sem=z_send.at[k],
            recv_sem=z_recv.at[k],
            device_id={"blk": to},
            device_id_type=pl.DeviceIdType.MESH,
        )

    def keep():
        return pltpu.make_async_copy(block(blk), shares.at[blk], own_sem)

    def product(m, weight):
        out, at = None, 0
        for act in acts[m * count : (m + 1) * count]:
            term = dot_nt(act[0], weight[:, at : at + act.shape[2]])
            out = term if out is None else out + term
            at += act.shape[2]
        return out

    @pl.when(i == 0)
    def _():
        barrier = pltpu.get_barrier_semaphore()
        pl.semaphore_signal(
            barrier, inc=1, device_id={"head": other}, device_id_type=pl.DeviceIdType.MESH
        )
        for k in range(1, nblk):
            pl.semaphore_signal(
                barrier,
                inc=1,
                device_id={"blk": lax.rem(blk + k, nblk)},
                device_id_type=pl.DeviceIdType.MESH,
            )
        pl.semaphore_wait(barrier, nblk)
        for k in range(1, nblk):
            share(k).start()
        keep().start()

    @pl.when(i < tiles)
    def _():
        mine[i] = (product(1, wg) + product(2, wu)).astype(BF16)
        copy(i).start()

    @pl.when(i >= tiles)
    def _():
        branch[0] = product(0, wd).astype(BF16)

    @pl.when(i == 2 * tiles - 1)
    def _():
        width = mine.shape[2]
        for j in range(tiles):
            copy(j).wait()
            total[:, j * width : (j + 1) * width] = mine[j].astype(F32) + theirs[j].astype(F32)
        for k in range(1, nblk):
            share(k).wait()
        keep().wait()


def exchange(stacks, wg, wu, wd, early, nblk, name):
    n = stacks[0].shape[1]
    d, ff = wg.shape
    dt = 256
    tiles = d // dt
    per = tiles // 2
    acts = [x for _ in range(3) for x in stacks]
    specs = [
        pl.BlockSpec((1,) + x.shape[1:], lambda i, m=m: (m, 0, 0), pipeline_mode=pl.Buffered(1))
        for m in range(3)
        for x in stacks
    ]
    first = pl.BlockSpec((dt, ff), lambda i: (jnp.minimum(i, tiles - 1), 0))
    second = pl.BlockSpec((dt, ff), lambda i: (jnp.maximum(i - tiles, 0), 0))
    place_hbm = pl.BlockSpec(memory_space=pltpu.HBM)

    def branch_at(i):
        j = jnp.maximum(i - tiles, 0)
        return (j // per, 0, j % per)

    return launch(
        functools.partial(exchange_kernel, len(stacks), tiles, nblk),
        (*acts, wg, wu, wd, early),
        grid=(2 * tiles,),
        in_specs=specs + [first, first, second, place_hbm],
        out_specs=[
            pl.BlockSpec((n, d), lambda i: (0, 0)),
            pl.BlockSpec((1, n, dt), branch_at),
            place_hbm,
        ],
        out_shape=[
            jax.ShapeDtypeStruct((n, d), F32),
            jax.ShapeDtypeStruct((2, n, d // 2), BF16),
            jax.ShapeDtypeStruct((nblk, early.shape[0] // nblk, early.shape[1]), BF16),
        ],
        scratch=[
            pltpu.VMEM((tiles, n, dt), BF16),
            pltpu.VMEM((tiles, n, dt), BF16),
            pltpu.SemaphoreType.DMA((tiles,)),
            pltpu.SemaphoreType.DMA((tiles,)),
            pltpu.SemaphoreType.DMA((nblk,)),
            pltpu.SemaphoreType.DMA((nblk,)),
            pltpu.SemaphoreType.DMA,
        ],
        mib=58,
        estimate=cost(6 * n * d * ff, 6 * d * ff),
        name=name,
        collective=1,
    )


def stream_kernel(da_sum, h1, r2, gain, g, w_out, dh1, dattn_t, dout, gsum):
    da = da_sum[...]
    inv = r2[:, :1]
    norm = jnp.concatenate([h1[j] for j in range(h1.shape[0])], axis=1) * inv
    grad = da * norm

    @pl.when(pl.program_id(0) == 0)
    def _():
        gsum[...] = jnp.zeros_like(gsum)

    gsum[...] += jnp.sum(grad, axis=0, keepdims=True)
    e2 = da * gain[...]
    mean = jnp.sum(e2 * norm, axis=1, keepdims=True) * (1.0 / da.shape[1])
    dh = g[...].astype(F32) + inv * (e2 - norm * mean)
    dh1[...] = dh
    low = dh.astype(BF16)
    dattn_t[...] = low.T
    dout[...] = dot(low, w_out[...]).astype(BF16)


def stream(da, h1, r2, gain, g, w_out, deps=()):
    parts, n, dt = h1.shape
    d = parts * dt
    tt = min(n, 128)
    ew = w_out.shape[1]
    row = lambda w: pl.BlockSpec((tt, w), lambda i: (i, 0))
    const = lambda a: pl.BlockSpec(a.shape, lambda i: (0, 0), pipeline_mode=pl.Buffered(1))
    return launch(
        stream_kernel,
        (da, h1, r2, gain, g, w_out),
        grid=(n // tt,),
        in_specs=[
            row(d),
            pl.BlockSpec((parts, tt, dt), lambda i: (0, i, 0)),
            row(PAIR),
            const(gain),
            row(d),
            const(w_out),
        ],
        out_specs=[
            row(d),
            pl.BlockSpec((d, tt), lambda i: (0, i)),
            row(ew),
            pl.BlockSpec((1, d), lambda i: (0, 0)),
        ],
        out_shape=[
            jax.ShapeDtypeStruct((n, d), F32),
            jax.ShapeDtypeStruct((d, n), BF16),
            jax.ShapeDtypeStruct((n, ew), BF16),
            jax.ShapeDtypeStruct((1, d), F32),
        ],
        mib=56,
        estimate=cost(2 * n * d * ew, 2 * d * ew + 20 * n * d),
        name="stream",
        deps=deps,
    )


def entry_kernel(dq, dkv, wq, wk, wv, full, ssx, gain, part, gsum, rsum):
    kvw = wk.shape[1]
    da = dot_nt(dq[...], wq[...])
    da = da + dot_nt(dkv[:, :kvw], wk[...]) + dot_nt(dkv[:, kvw:], wv[...])
    width = pl.num_programs(0) * da.shape[1]
    inv = lax.rsqrt(ssx[:, :1] * (1.0 / width) + EPS)
    grad = da * (full[...].astype(F32) * inv)
    gsum[...] = jnp.sum(grad, axis=0, keepdims=True)

    @pl.when(pl.program_id(0) == 0)
    def _():
        rsum[...] = jnp.zeros_like(rsum)

    rsum[...] += jnp.sum(grad * gain[...], axis=1, keepdims=True)
    part[0] = da.astype(BF16)


def entry(dq, dkv, wq, wk, wv, full, ssx, gain):
    n, d = full.shape
    dt = 256
    per = d // 2 // dt
    const = lambda a: pl.BlockSpec(a.shape, lambda i: (0, 0), pipeline_mode=pl.Buffered(1))
    wspec = lambda w: pl.BlockSpec((dt, w.shape[1]), lambda i: (i, 0))
    return launch(
        entry_kernel,
        (dq, dkv, wq, wk, wv, full, ssx, gain),
        grid=(d // dt,),
        in_specs=[const(dq), const(dkv), wspec(wq), wspec(wk), wspec(wv)]
        + [
            pl.BlockSpec((n, dt), lambda i: (0, i)),
            const(ssx),
            pl.BlockSpec((1, dt), lambda i: (0, i)),
        ],
        out_specs=[
            pl.BlockSpec((1, n, dt), lambda i: (i // per, 0, i % per)),
            pl.BlockSpec((1, dt), lambda i: (0, i)),
            pl.BlockSpec((n, PAIR), lambda i: (0, 0)),
        ],
        out_shape=[
            jax.ShapeDtypeStruct((2, n, d // 2), BF16),
            jax.ShapeDtypeStruct((1, d), F32),
            jax.ShapeDtypeStruct((n, PAIR), F32),
        ],
        mib=56,
        estimate=cost(2 * n * d * (wq.shape[1] + 2 * wk.shape[1]), 20 * n * d),
        name="entry",
    )


def outer_kernel(shares, count, parts, adds, spread, sc, *refs):
    k = 0
    lefts, rights = [], []
    for share in shares:
        lefts.append((refs[k : k + count], refs[k + count : k + 2 * count]))
        k += 2 * count
        rights.append([(refs[k + 2 * i], refs[k + 2 * i + 1]) for i in range(share)])
        k += 2 * share
    got = refs[k] if adds else None
    outs = refs[k + adds :]

    def work(out):
        m = 0
        for (left_own, left_oth), group in zip(lefts, rights, strict=True):
            rows = left_own[0].shape[0]
            for own, oth in group:
                at = slice(m * FT, (m + 1) * FT)
                for i in range(count):
                    part = slice(i * rows, (i + 1) * rows)
                    total = dot(left_own[i][...], own[0]) + dot(left_oth[i][...], oth[0])
                    if adds:
                        total = total + got[part, at].astype(F32)
                    if spread == 1:
                        out[part, at] = total.astype(BF16)
                    else:
                        size = rows // spread
                        for b in range(spread):
                            to = slice((b * count + i) * size, (b * count + i + 1) * size)
                            out[to, at] = total[b * size : (b + 1) * size, :].astype(BF16)
                m += 1

    if len(parts) == 1:
        work(outs[0])
        return
    step = pl.program_id(0)
    start = 0
    for out, size in zip(outs, parts, strict=True):
        pl.when((step >= start) & (step < start + size))(functools.partial(work, out))
        start += size


def outer(sc, groups, rows, first, parts, name, got=None, deps=(), spread=1):
    n = groups[0][0].shape[1]
    count = sc.shape[0]
    number = sum(parts)
    shares = tuple(len(g[2]) for g in groups)
    ins, specs = [], []
    for own, oth, rights in groups:
        ins += [own] * count + [oth] * count
        for i in range(count):
            specs.append(pl.BlockSpec((rows, n), lambda j, s, i=i: (s[i], 0)))
        specs += specs[-count:]
        for r_own, r_oth, at in rights:
            ins += [r_own, r_oth]
            specs += [pl.BlockSpec((1, n, FT), lambda i, s, at=at: (at, 0, first + i))] * 2
    members = sum(shares)
    height = count * rows
    ospecs, start = [], 0
    for size in parts:
        ospecs.append(
            pl.BlockSpec(
                (height, members * FT),
                lambda i, s, start=start, size=size: (0, jnp.clip(i - start, 0, size - 1)),
            )
        )
        start += size
    if got is not None:
        ins.append(got)
        specs.append(ospecs[0])
    c = number * FT
    return launch(
        functools.partial(outer_kernel, shares, count, tuple(parts), int(got is not None), spread),
        (sc, *ins),
        prefetch=1,
        grid=(number,),
        in_specs=specs,
        out_specs=ospecs,
        out_shape=[jax.ShapeDtypeStruct((height, members * size * FT), BF16) for size in parts],
        mib=48,
        estimate=cost(8 * n * height * c * members, members * c * (4 * n + 2 * height)),
        name=name,
        deps=deps,
    )


def finish_kernel(count, *refs):
    parts = refs[:count]
    outs = refs[count:]
    at = 0
    for part in parts:
        for tile in range(part.shape[2] // (3 * FT)):
            for m in range(3):
                columns = slice((3 * tile + m) * FT, (3 * tile + m + 1) * FT)
                total = part[0, :, columns].astype(F32)
                for b in range(1, part.shape[0]):
                    total = total + part[b, :, columns].astype(F32)
                outs[m][:, at : at + FT] = total
            at += FT


def finish(parts):
    parts = [x.reshape(count, x.shape[0] // count, x.shape[1]) for x, count in parts]
    rows = parts[0].shape[1]
    width = sum(x.shape[2] for x in parts) // 3
    whole = lambda shape: pl.BlockSpec(shape, lambda i: (0,) * len(shape))
    return launch(
        functools.partial(finish_kernel, len(parts)),
        tuple(parts),
        grid=(1,),
        in_specs=[whole(x.shape) for x in parts],
        out_specs=[whole((rows, width))] * 3,
        out_shape=[jax.ShapeDtypeStruct((rows, width), F32)] * 3,
        mib=48,
        estimate=cost(0, 8 * parts[0].shape[0] * rows * width),
        name="finish",
    )


def finish_rows_kernel(shares, *outs):
    at = 0
    for out in outs[:-1]:
        columns = slice(at, at + out.shape[1])
        total = shares[0, :, columns].astype(F32)
        for b in range(1, shares.shape[0]):
            total = total + shares[b, :, columns].astype(F32)
        out[...] = total
        at += out.shape[1]
    total = shares[0, :, at:].astype(F32)
    for b in range(1, shares.shape[0]):
        total = total + shares[b, :, at:].astype(F32)
    outs[-1][...] = total.T


def finish_rows(shares, widths):
    _, rows, columns = shares.shape
    left = columns - sum(widths)
    whole = lambda shape: pl.BlockSpec(shape, lambda i: (0,) * len(shape))
    shapes = [(rows, w) for w in widths] + [(left, rows)]
    return launch(
        finish_rows_kernel,
        (shares,),
        grid=(1,),
        in_specs=[whole(shares.shape)],
        out_specs=[whole(x) for x in shapes],
        out_shape=[jax.ShapeDtypeStruct(x, F32) for x in shapes],
        mib=32,
        estimate=cost(0, 4 * shares.size),
        name="finish_rows",
    )


def body(
    inputs,
    cotangent,
    lengths,
    attn_gain,
    w_query,
    w_key,
    w_value,
    w_out,
    mlp_gain,
    gate_weight,
    up_weight,
    down_weight,
):
    t, rows, half = inputs.shape
    n = t * rows
    heads = lax.axis_size("head")
    nblk = lax.axis_size("blk")
    ndp = lax.axis_size("dp")
    d = half * heads
    h = lax.axis_index("head").astype(jnp.int32)
    blk = lax.axis_index("blk").astype(jnp.int32)
    dp = lax.axis_index("dp").astype(jnp.int32)
    sc_h = h.reshape(1)
    sc_blk = blk.reshape(1)

    def flat(x):
        return jnp.transpose(x, (1, 0, 2)).reshape(n, x.shape[2])

    def unflat(x):
        return jnp.transpose(x.reshape(rows, t, x.shape[1]), (1, 0, 2))

    x_own = flat(inputs)
    g_own = flat(cotangent)
    gain_one = attn_gain.astype(F32).reshape(1, d)
    gain_two = mlp_gain.astype(F32).reshape(1, d)

    pos = blk * t + jnp.arange(t, dtype=jnp.int32)
    ends = jnp.cumsum(lengths, axis=1)
    passed = ends[:, None, :] <= pos[None, :, None]
    start = jnp.max(jnp.where(passed, ends[:, None, :], 0), axis=2)
    valid = (jnp.sum(passed.astype(jnp.int32), axis=2) < DOCS).astype(F32).reshape(n)
    start_rows = start.reshape(rows, 1, t)
    freq = jnp.power(THETA, -2.0 * jnp.arange(HD // 2, dtype=F32) / HD)
    angles = pos.astype(F32)[:, None] * freq[None, :]
    cos_h, sin_h = jnp.cos(angles), jnp.sin(angles)
    cos = jnp.tile(jnp.concatenate([cos_h, cos_h, cos_h, cos_h], axis=1), (rows, 1))
    sin = jnp.tile(jnp.concatenate([-sin_h, sin_h, -sin_h, sin_h], axis=1), (rows, 1))

    CHAIN.clear()
    WEIGHT[0] = EARLY

    def tie(x, *also):
        return lax.optimization_barrier((x, *also))[0]

    def by_head(x):
        return jnp.where(h == 0, x[:, :half], x[:, half:])

    def gate(x):
        x, CHAIN[0] = lax.optimization_barrier((x, CHAIN[0]))
        return x

    def mate(x):
        return swap(x, "dp", 1)

    x_oth = swap(x_own, "head", 1)
    share = w_out.shape[0] // ndp
    piece = lax.dynamic_slice_in_dim(w_out, dp * share, share, 0)
    x_oth, piece, g_own, cos, sin, start_rows = lax.optimization_barrier(
        (x_oth, piece, g_own, cos, sin, start_rows)
    )
    piece = swap(piece, "head", 1)
    full, a_one, queries, kv, ssx = project(
        sc_h, x_own, x_oth, gain_one, w_query, w_key, w_value, cos, sin
    )

    kvs, state = [kv], ()
    for s in range(nblk):
        if s + 1 < nblk:
            steps = [(i, i + 1) for i in range(s, nblk - 1)]
            kvs.append(lax.ppermute(kvs[s], "blk", steps))
        state = attend(s, s == nblk - 1, sc_blk, queries, kvs[s], start_rows, state, rows)
        if s + 1 < nblk - 1:
            kvs[s + 1] = gate(kvs[s + 1])
        if s == 0:
            a_one_t = flip(a_one, "flip_a")
            piece = gate(piece)
            w_out_oth = lax.all_gather(piece, "dp", axis=0, tiled=True)
            g_own, piece = lax.optimization_barrier((g_own, piece))
            g_oth = swap(g_own, "head", 1)
    acc, ml = state
    o_own = flip(acc)
    o_oth = swap(o_own, "head", 1)
    part_own = own_part(o_own, w_out)
    g_full = jnp.concatenate(
        [jnp.where(h == 0, g_own, g_oth), jnp.where(h == 0, g_oth, g_own)], axis=1
    )
    g_t = flip(g_full, "flip_g")
    o_mate, g_mate = mate(o_own), mate(g_t)
    h_one, a_two, a_two_t, inv_two, ssa = merge(
        part_own, o_oth, w_out_oth, full, gain_two
    )
    a_two_mate = mate(a_two_t)

    low_bit = dp & 1
    block_rows = d // ndp
    sc_send = (dp ^ 2).reshape(1)
    sc_keep = dp.reshape(1)
    sc_both = jnp.stack([2 * i + low_bit for i in range(ndp // 2)])
    y_groups = [[0, 2], [1, 3]]

    def both_halves(groups, parts, name, deps=()):
        return [
            lax.psum_scatter(
                x, "dp", scatter_dimension=0, axis_index_groups=y_groups, tiled=True
            )
            for x in outer(sc_both, groups, block_rows, 0, parts, name, deps=deps)
        ]

    def over_blk(x):
        return lax.all_to_all(x, "blk", split_axis=0, concat_axis=0, tiled=True)

    tiles = gate_weight.shape[1] // FT
    size_a = max(1, tiles // 5)
    size_b = (tiles - size_a + 1) // 3
    size_c = tiles - size_a - size_b

    def unit_part(first, count, deps=()):
        x = units(a_two, g_full, gate_weight, up_weight, down_weight, first, count, deps)
        x_mate = mate(x)
        return x, [
            (g_t, g_mate, [(x, x_mate, 0)]),
            (a_two_t, a_two_mate, [(x, x_mate, 1), (x, x_mate, 2)]),
        ]

    part_a, groups_a = unit_part(0, size_a)
    (sum0,) = both_halves(groups_a, (size_a,), "mlp0")
    part_b, groups_b = unit_part(size_a, size_b)
    part_c, groups_c = unit_part(size_a + size_b, size_c)
    (sum1,) = both_halves(groups_b, (size_b,), "mlp1")

    da, branch, all0 = exchange(
        [part_a, part_b, part_c], gate_weight, up_weight, down_weight, sum0, nblk, "exchange"
    )
    WEIGHT[0] = LATE
    sum2, sum3 = both_halves(groups_c, (size_c - size_c // 2, size_c // 2), "mlp2")
    all1 = over_blk(gate(sum1))
    dh_one, d_attn_t, d_out, gain_two_sum = stream(
        da, h_one, inv_two, gain_two, g_full, w_out
    )
    d_attn_mate, a_one_mate = mate(d_attn_t), mate(gate(a_one_t))
    out_groups = [(d_attn_t, d_attn_mate, [(o_own[None], o_mate[None], 0)])]
    out_parts = (o_own.shape[1] // FT,)
    to_other = gate(lax.dynamic_index_in_dim(branch, 1 - h, 0, keepdims=False))
    branch_oth = swap(to_other, "head", 1)

    state, parts = (), []
    for s in reversed(range(nblk)):
        out = attend_back(
            s, s == nblk - 1, s == 0, sc_blk, queries, d_out, o_own, ml, start_rows, cos, sin,
            kvs[s], state, rows, deps=(),
        )
        state = (out[0], out[2] if s == nblk - 1 else state[1])
        part = out[1]
        parts.append(
            lax.ppermute(part, "blk", [(i, i - s) for i in range(s, nblk)]) if s else part
        )
        if s == min(1, nblk - 1):
            (both_out,) = outer(
                sc_both, out_groups, block_rows, 0, out_parts, "out",
                deps=(all1, a_one_mate) + tuple(parts[: nblk - 1]),
            )
            all2 = over_blk(gate(sum2))
    d_q = state[0]
    d_kv_own = gather_dkv(parts, cos, sin)
    d_qkv = jnp.concatenate([d_q, d_kv_own], axis=1)
    d_qkv_mate = mate(d_qkv)
    d_part, gain_one_sum, row_sum = entry(
        d_q, d_kv_own, w_query, w_key, w_value, full, ssx, gain_one
    )
    qkv_groups = [(a_one_t, a_one_mate, [(d_qkv[None], d_qkv_mate[None], 0)])]
    qkv_parts = (d_qkv.shape[1] // FT,)
    sum3 = lax.psum_scatter(gate(sum3), "blk", scatter_dimension=0, tiled=True)
    (first_qkv,) = outer(sc_send, qkv_groups, block_rows, 0, qkv_parts, "qkv_send", deps=(all2,))
    got_qkv = swap(first_qkv, "dp", 2)
    sum_out = lax.psum_scatter(
        gate(both_out), "dp", scatter_dimension=0, axis_index_groups=y_groups, tiled=True
    )
    sum_out = lax.psum_scatter(sum_out, "blk", scatter_dimension=0, tiled=True)
    d_send = lax.dynamic_index_in_dim(d_part, 1 - h, 0, keepdims=False)
    d_send, row_sum, gain_one_sum, CHAIN[0] = lax.optimization_barrier(
        (d_send, row_sum, gain_one_sum, CHAIN[0])
    )
    h_late, branch_late = gate(h_one), gate(branch)
    h_half = jnp.concatenate(
        [
            jnp.where(h == 0, h_late[i], h_late[i + h_late.shape[0] // 2])
            for i in range(h_late.shape[0] // 2)
        ],
        axis=1,
    )
    mlp_half = lax.dynamic_index_in_dim(branch_late, h, 0, keepdims=False).astype(F32) + (
        branch_oth.astype(F32)
    )
    output = unflat((h_half + mlp_half).astype(BF16))
    d_other = swap(d_send, "head", 1)
    row_total = row_sum + swap(row_sum, "head", 1)
    (keep_qkv,) = outer(
        sc_keep, qkv_groups, block_rows, 0, qkv_parts, "qkv_keep", got_qkv, deps=(branch_oth,)
    )
    per_head = 1.0 / heads
    tail = jnp.stack(
        [
            jnp.sum(valid) * per_head,
            jnp.sum(valid * ssx[:, 0]) * per_head,
            jnp.sum(valid * ssa[:, 0]) * per_head,
            jnp.sum(valid[:, None] * mlp_half * mlp_half),
        ]
    )
    small = jnp.concatenate(
        [gain_one_sum[0], gain_two_sum[0] * per_head, tail, jnp.zeros((PAIR - 4,), F32)]
    ).reshape(-1, PAIR)
    for axis in ("head", "dp"):
        for i in range(lax.axis_size(axis).bit_length() - 1):
            small = small + swap(small, axis, 1 << i)
    small = small.reshape(-1)
    mine = [
        lax.dynamic_slice_in_dim(small, at + dp * block_rows, block_rows, 0)[:, None]
        for at in (0, d)
    ]
    sums4 = jnp.broadcast_to(small[None, 2 * d : 2 * d + 4], (block_rows, 4))
    exact = jnp.concatenate(mine + [sums4], axis=1)
    coarse = exact.astype(BF16)
    fine = (exact - coarse.astype(F32)).astype(BF16)
    extra = jnp.concatenate(
        [coarse, fine, jnp.zeros((block_rows, PAIR - 12), BF16)], axis=1
    )
    all_qkv = over_blk(jnp.concatenate([keep_qkv, extra], axis=1))
    grad_down, grad_gate, grad_up = finish([(all0.reshape(-1, all0.shape[2]), nblk), (all1, nblk), (all2, nblk), (sum3, 1)])
    qw, kvw = w_query.shape[1], w_key.shape[1]
    sum_query, sum_key, sum_value, small = finish_rows(
        all_qkv.reshape(nblk, -1, all_qkv.shape[1]), (qw, kvw, kvw)
    )

    inv_one = lax.rsqrt(ssx[:, :1] * (1.0 / d) + EPS)
    d_one = lax.dynamic_index_in_dim(d_part, h, 0, keepdims=False).astype(F32) + d_other.astype(F32)
    norm_half = x_own.astype(F32) * inv_one
    grad_input = by_head(tie(dh_one, d_other)) + inv_one * (
        d_one * by_head(gain_one) - norm_half * (row_total[:, :1] * (1.0 / d))
    )

    small = small[:6] + small[6:12]
    grad_attn_gain, grad_mlp_gain = small[0], small[1]
    stats = jnp.sqrt(small[3:6, 0] / (small[2, 0] * d))

    return (
        output,
        unflat(grad_input),
        grad_attn_gain,
        sum_query,
        sum_key,
        sum_value,
        sum_out.astype(F32),
        grad_mlp_gain,
        grad_gate,
        grad_up,
        grad_down,
        stats,
    )


def solution(mesh):
    tokens = P("blk", "dp", "head")
    split = P(None, "head")
    in_specs = (tokens, tokens, P("dp", None), P()) + (split,) * 4 + (P(),) + (split,) * 3
    vec, mat = P(("dp", "blk")), P(("dp", "blk"), "head")
    out_specs = (tokens, tokens, vec, mat, mat, mat, mat, vec, mat, mat, mat, P())
    return jax.shard_map(body, mesh=mesh, in_specs=in_specs, out_specs=out_specs, check_vma=False)
```
